256 devices in a mesh: outer: 16 (over x, y_hi, core), inner: 16 (over y_lo, z).
Axes of the slice: x: 4, y: 4 (y_hi: 2, y_lo: 2; y = y_hi * 2 + y_lo), z: 8, core: 2. Of those that a mesh axis runs over, the one named last changes fastest.
Arguments:
- q_nope: bfloat16 [4096, 8192], P('inner', 'outer'), may hold values from -6 to 6
- q_rope: bfloat16 [4096, 4096], P('inner', 'outer'), may hold values from -8 to 8
- absorb_key: bfloat16 [64, 128, 512], P('outer'), may hold values from -0.5 to 0.5
- kv_latent: bfloat16 [4096, 576], P('inner'), may hold values from -8 to 8
- value_up: bfloat16 [64, 512, 128], P('outer'), may hold values from -0.75 to 0.75
- out_proj: bfloat16 [8192, 7168], P(None, 'outer'), may hold values from -0.0625 to 0.0625
Outputs:
- mixed: bfloat16 [4096, 7168], P('inner', 'outer')
The draws below stay inside these ranges and needn't reach their ends.
All inputs are finite; a program needn't handle non-finite values.
Results may differ from the reference program's by a relative error of at most 0.012.
Values may be sent and summed in bfloat16 or wider, within the bound.
A program may use at most 64 MiB of HBM per device.

```python
import math
import jax
import jax.numpy as jnp
from jax import lax

D = 7168
HEADS = 64
NOPE = 128
ROPE = 64
LAT = 512
VDIM = 128
SEQ = 4096


def draw_kv_latent(key, part):
    own_key = jax.random.fold_in(key, 11)
    base = jnp.clip(jax.random.normal(own_key, (SEQ, LAT + ROPE), jnp.float32), -6.0, 6.0)
    return base.astype(jnp.bfloat16)


def draw_q_rope(key, part):
    own_key = jax.random.fold_in(key, 12)
    base = jnp.clip(jax.random.normal(own_key, (SEQ, HEADS * ROPE), jnp.float32), -6.0, 6.0)
    return base.astype(jnp.bfloat16)


def steps_of(rng, dims, split, low, high):
    def one(position, parts):
        heights = jax.random.uniform(jax.random.fold_in(jax.random.fold_in(rng, 6), position), (parts,), jnp.float32, low / len(split), high / len(split))
        return jnp.repeat(jnp.exp(heights), dims[position] // parts).reshape((-1,) + (1,) * (len(dims) - position - 1))

    factor_of = one(*split[0])
    for cut in split[1:]:
        factor_of = factor_of * one(*cut)
    return factor_of


def centred(key, extent, width, reach, split=(), kind=jnp.bfloat16):
    result = jax.random.normal(key, extent, jnp.float32) * width
    if len(split) > 0:
        result = steps_of(key, extent, split, -0.22, 0.18) * result
    return jnp.clip(result, min=-reach, max=reach).astype(kind)


def setup_inputs(seed: int = 0) -> dict:
    key_list = jax.random.split(jax.random.key(seed), 7)
    q_nope = centred(key_list[0], (SEQ, HEADS * NOPE), 1.0, 6.0, ((0, 16), (1, 16)))
    q_rope = draw_q_rope(jax.random.fold_in(key_list[6], 71), 0)
    absorb_key = centred(key_list[2], (HEADS, NOPE, LAT), NOPE ** -0.5, 0.5, ((0, 16),))
    kv_latent = draw_kv_latent(jax.random.fold_in(key_list[6], 71), 0)
    value_up = centred(key_list[4], (HEADS, LAT, VDIM), (LAT // 8) ** -0.5, 0.75, ((0, 16),))
    out_proj = centred(key_list[5], (HEADS * VDIM, D), (HEADS * VDIM) ** -0.5, 0.0625, ((1, 16),))
    return dict(q_nope=q_nope, q_rope=q_rope, absorb_key=absorb_key, kv_latent=kv_latent, value_up=value_up, out_proj=out_proj)


def head_output(query_part, rotary_part, key_up, value_map, kv_latent, score_scale):
    seq_len = query_part.shape[0]
    lat_width = key_up.shape[1]
    absorbed = jnp.dot(query_part, key_up, preferred_element_type=jnp.float32).astype(jnp.bfloat16)
    scores = jnp.dot(absorbed, kv_latent[:, :lat_width].T, preferred_element_type=jnp.float32)
    scores = scores + jnp.dot(rotary_part, kv_latent[:, lat_width:].T, preferred_element_type=jnp.float32)
    scores = scores * score_scale
    row_index = lax.broadcasted_iota(jnp.int32, (seq_len, seq_len), 0)
    col_index = lax.broadcasted_iota(jnp.int32, (seq_len, seq_len), 1)
    visible = col_index <= row_index
    peak = lax.optimization_barrier(jnp.max(jnp.where(visible, scores, jnp.float32(-1e+30)), axis=1))
    weights = jnp.where(visible, jnp.exp(scores - peak[:, None]), jnp.float32(0.0))
    total = lax.optimization_barrier(jnp.sum(weights, axis=1))
    latent_out = jnp.dot(weights.astype(jnp.bfloat16), kv_latent[:, :lat_width], preferred_element_type=jnp.float32)
    latent_out = (latent_out / total[:, None]).astype(jnp.bfloat16)
    return jnp.dot(latent_out, value_map, preferred_element_type=jnp.float32).astype(jnp.bfloat16)

def reference(q_nope, q_rope, absorb_key, kv_latent, value_up, out_proj):
    seq_len = q_nope.shape[0]
    head_count = absorb_key.shape[0]
    score_scale = 1.0 / math.sqrt(NOPE + ROPE)
    query_heads = q_nope.reshape(seq_len, head_count, NOPE).transpose(1, 0, 2)
    rotary_heads = q_rope.reshape(seq_len, head_count, ROPE).transpose(1, 0, 2)

    def per_head(inputs):
        return head_output(inputs[0], inputs[1], inputs[2], inputs[3], kv_latent, score_scale)
    values = lax.map(per_head, (query_heads, rotary_heads, absorb_key, value_up))
    values = values.transpose(1, 0, 2).reshape(seq_len, head_count * VDIM)
    return jnp.dot(values, out_proj, preferred_element_type=jnp.float32).astype(jnp.bfloat16)
```

```python
import math

import jax
import jax.numpy as jnp
from jax import lax
from jax.experimental import pallas as pl
from jax.experimental.pallas import tpu as pltpu
from jax.sharding import PartitionSpec as P

NOPE = 128
ROPE = 64
VDIM = 128
LAT = 512
WIDE = LAT + ROPE
MESH = pl.DeviceIdType.MESH
NT = (((1,), (1,)), ((), ()))
SCALE = math.log2(math.e) / math.sqrt(NOPE + ROPE)
NX, NZ = 4, 8


def div(a, b):
    return a // b if isinstance(a, int) else lax.div(a, b)


def rem(a, b):
    return a % b if isinstance(a, int) else lax.rem(a, b)


def kernel(
    qn_hbm, qr_hbm, ak_hbm, kv_hbm, vu_hbm, wo_hbm, out_ref,
    qn, qr, ak, vu, wo, kvbuf, vbuf, query, peak, total, acc, mix,
    local_sem, kv_recv, send_z, send_y, sib_a, sib_b, v_recv, send_x, send_c, sib_v,
):
    heads, rows = query.shape[0], query.shape[1]
    o, i = lax.axis_index("outer"), lax.axis_index("inner")
    core, yh, x = rem(o, 2), rem(div(o, 2), 2), div(o, 4)
    yl, z = div(i, NZ), rem(i, NZ)

    def outer_of(x_, yh_, core_):
        return (x_ * 2 + yh_) * 2 + core_

    sibling = (outer_of(x, yh, 1 - core), i)
    z_up = (o, yl * NZ + rem(z + 1, NZ))
    z_down = (o, yl * NZ + rem(z + NZ - 1, NZ))
    y_up = (outer_of(x, rem(yh + yl, 2), core), (1 - yl) * NZ + z)
    y_down = (outer_of(x, rem(yh + 1 - yl, 2), core), (1 - yl) * NZ + z)
    y_far = (outer_of(x, 1 - yh, core), i)
    x_up = (outer_of(rem(x + 1, NX), yh, core), i)
    x_down = (outer_of(rem(x + NX - 1, NX), yh, core), i)

    locals_ = [
        pltpu.make_async_copy(kv_hbm.at[part], kvbuf.at[i, part], local_sem.at[part])
        for part in range(4)
    ]
    for n, (src, dst) in enumerate(
        [(qn_hbm, qn), (ak_hbm, ak), (qr_hbm, qr), (vu_hbm, vu), (wo_hbm, wo)]
    ):
        locals_.append(pltpu.make_async_copy(src, dst, local_sem.at[4 + n]))
    for copy in locals_:
        copy.start()

    barrier = pltpu.get_barrier_semaphore()
    partners = (sibling, z_up, z_down, y_up, y_down, y_far, x_up, x_down)
    for partner in partners:
        pl.semaphore_signal(barrier, inc=1, device_id=partner, device_id_type=MESH)
    pl.semaphore_wait(barrier, len(partners))

    def kv_copy(j, k, send_sem, target):
        piece = kvbuf.at[j, 2 * core + k]
        return pltpu.make_async_remote_copy(
            src_ref=piece, dst_ref=piece, send_sem=send_sem,
            recv_sem=kv_recv.at[j, 2 * core + k], device_id=target, device_id_type=MESH,
        )

    def kv_arrived(j, part):
        piece = kvbuf.at[j, part]
        pltpu.make_async_remote_copy(
            src_ref=piece, dst_ref=piece, send_sem=send_z.at[0, 0],
            recv_sem=kv_recv.at[j, part], device_id=sibling, device_id_type=MESH,
        ).wait_recv()

    def z_of(r):
        step = div(r + 1, 2) * (1 - 2 * rem(r, 2))
        return rem(z + step + NZ, NZ)

    y_target = (y_up, y_down)

    for part in range(4):
        locals_[part].wait()
    for k in range(2):
        kv_copy(i, k, send_z.at[0, k], z_up).start()
        kv_copy(i, k, send_z.at[7, k], z_down).start()
    for k in range(2):
        @pl.when(yl == 0)
        def _():
            kv_copy(i, k, send_y.at[0, k], y_target[k]).start()

    def z_forwards(r, k):
        return (r <= 4) | (r == 5 + k)

    def z_target(r):
        return (o, yl * NZ + rem(z + 2 * rem(r, 2) - 1 + NZ, NZ))

    def relay_a(r):
        j = yl * NZ + z_of(r)
        for k in range(2):
            kv_arrived(j, 2 * core + k)

            @pl.when(z_forwards(r, k))
            def _():
                kv_copy(j, k, send_z.at[r, k], z_target(r)).start()

            @pl.when(yl == 0)
            def _():
                kv_copy(j, k, send_y.at[r, k], y_target[k]).start()

            kv_copy(j, k, sib_a.at[r, k], sibling).start()

    def relay_b(r):
        j = z_of(r)
        for k in range(2):
            kv_arrived(j, 2 * core + k)
            kv_copy(j, k, sib_b.at[r, k], sibling).start()

    locals_[4].wait()
    locals_[5].wait()
    locals_[6].wait()
    for h in range(heads):
        query[h, :, :LAT] = jnp.dot(
            qn[:, h * NOPE : (h + 1) * NOPE], ak[h], preferred_element_type=jnp.float32
        ).astype(jnp.bfloat16)
        query[h, :, LAT:] = qr[:, h * ROPE : (h + 1) * ROPE]

    def attend(j, first):
        keys = kvbuf[j].reshape(rows, WIDE)
        latent = keys[:, :LAT]

        def scores(h):
            s = lax.dot_general(query[h], keys, NT, preferred_element_type=jnp.float32) * SCALE
            if first:
                row = lax.broadcasted_iota(jnp.int32, s.shape, 0)
                col = lax.broadcasted_iota(jnp.int32, s.shape, 1)
                s = jnp.where(col <= row, s, jnp.float32(-1e30))
            return s

        def fold(h, s):
            top = jnp.max(s, axis=1, keepdims=True)
            if first:
                new = jnp.broadcast_to(top, (rows, 128))
            else:
                old = peak[h]
                new = jnp.maximum(old, top)
            w = jnp.exp2(s - jnp.concatenate([new] * (rows // 128), axis=1))
            part = w[:, :128]
            for n in range(1, rows // 128):
                part = part + w[:, n * 128 : (n + 1) * 128]
            update = jnp.dot(w.astype(jnp.bfloat16), latent, preferred_element_type=jnp.float32)
            peak[h] = new
            if first:
                total[h] = part
                acc[h] = update
            else:
                shrink = jnp.exp2(old - new)
                total[h] = total[h] * shrink + part
                acc[h] = acc[h] * jnp.concatenate([shrink] * (LAT // 128), axis=1) + update

        s = scores(0)
        for h in range(heads):
            ahead = scores(h + 1) if h + 1 < heads else None
            fold(h, s)
            s = ahead

    attend(i, True)

    @pl.when(yl == 1)
    def _():
        relay_b(0)

    def round_(r, carry):
        @pl.when(r < 7)
        def _():
            relay_a(r + 1)

        @pl.when((r < 7) & (yl == 1))
        def _():
            relay_b(r + 1)

        def side(ab, carry):
            j = (1 - ab) * (yl * NZ) + z_of(r)
            held = ((ab == 0) & (r > 0)) | ((ab == 1) & (yl == 1))

            @pl.when(held)
            def _():
                for k in range(2):
                    kv_arrived(j, 2 * (1 - core) + k)

            @pl.when(held & (j < i))
            def _():
                attend(j, False)

            return carry

        return lax.fori_loop(0, 2, side, carry)

    lax.fori_loop(0, 8, round_, 0)

    def block(e):
        n, dy = rem(e, 4), div(e, 4)
        dx = n + div(n, 2) * (1 - 2 * rem(n, 2))
        return rem(x + dx, NX), rem(yh + dy, 2)

    def v_copy(e, k, send_sem, target):
        xx, yy = block(e)
        slot = outer_of(xx, yy, core)
        piece = vbuf.at[slot, k]
        return pltpu.make_async_remote_copy(
            src_ref=piece, dst_ref=piece, send_sem=send_sem,
            recv_sem=v_recv.at[slot, k], device_id=target, device_id_type=MESH,
        )

    def v_arrived(slot, k):
        piece = vbuf.at[slot, k]
        pltpu.make_async_remote_copy(
            src_ref=piece, dst_ref=piece, send_sem=send_c.at[0],
            recv_sem=v_recv.at[slot, k], device_id=sibling, device_id_type=MESH,
        ).wait_recv()

    def own_slot(e):
        xx, yy = block(e)
        return outer_of(xx, yy, core)

    def sib_slot(e):
        xx, yy = block(e)
        return outer_of(xx, yy, 1 - core)

    locals_[7].wait()

    def send(e, k, way):
        sem = {
            "far": lambda: send_c.at[k], "up": lambda: send_x.at[e, k, 0],
            "down": lambda: send_x.at[e, k, 1], "sib": lambda: sib_v.at[e, k],
        }[way]()
        target = {"far": y_far, "up": x_up, "down": x_down, "sib": sibling}[way]
        return v_copy(e, k, sem, target)

    for h in range(heads):
        whole = jnp.sum(total[h], axis=1, keepdims=True)
        latent_out = (acc[h] * (1.0 / whole)).astype(jnp.bfloat16)
        vbuf[o, h // 2, :, (h % 2) * VDIM : (h % 2 + 1) * VDIM] = jnp.dot(
            latent_out, vu[h], preferred_element_type=jnp.float32
        ).astype(jnp.bfloat16)
        if h % 2 == 1:
            k = h // 2
            send(0, k, "far").start()
            send(0, k, "up").start()
            send(0, k, "down").start()
            send(0, k, "sib").start()

    locals_[8].wait()
    mix[...] = jnp.zeros_like(mix)

    def project(slot):
        for k in range(2):
            depth = heads * VDIM // 2
            start = pl.multiple_of((slot * 2 + k) * depth, depth)
            mix[...] += jnp.dot(
                vbuf[slot, k], wo[pl.ds(start, depth), :], preferred_element_type=jnp.float32
            )

    def relay_v(e):
        def came(e, k):
            v_arrived(own_slot(e), k)
            send(e, k, "sib").start()

        if e == 1:
            came(1, 0)
            came(1, 1)
            send(1, 1, "down").start()
        if e == 2:
            came(2, 0)
            send(2, 0, "up").start()
            came(2, 1)
        if e == 3:
            for k in range(2):
                v_arrived(own_slot(4), k)
                send(4, k, "up").start()
                send(4, k, "down").start()
                send(4, k, "sib").start()
            came(3, 0)
            came(3, 1)
        if e == 5:
            came(5, 0)
            came(5, 1)
            send(5, 1, "down").start()
        if e == 6:
            came(6, 0)
            send(6, 0, "up").start()
            came(6, 1)
        if e == 7:
            came(7, 0)
            came(7, 1)

    def event(e, carry):
        for n in (1, 2, 3, 5, 6, 7):
            @pl.when(e == n)
            def _():
                relay_v(n)

        @pl.when(e > 0)
        def _():
            project(own_slot(e - 1))
            for k in range(2):
                v_arrived(sib_slot(e - 1), k)
            project(sib_slot(e - 1))

        return carry

    lax.fori_loop(0, 9, event, 0)
    out_ref[...] = mix[...].astype(jnp.bfloat16)

    for e in range(8):
        for k in range(2):
            ways = ["sib"]
            if e == 0:
                ways += ["far"]
            if e in (0, 4):
                ways += ["up", "down"]
            if (e, k) in ((2, 0), (6, 0)):
                ways += ["up"]
            if (e, k) in ((1, 1), (5, 1)):
                ways += ["down"]
            for way in ways:
                send(e, k, way).wait_send()
    for k in range(2):
        kv_copy(i, k, send_z.at[0, k], z_up).wait_send()
        kv_copy(i, k, send_z.at[7, k], z_down).wait_send()

    def drain(r, carry):
        for k in range(2):
            @pl.when((r > 0) & z_forwards(r, k))
            def _():
                kv_copy(yl * NZ + z_of(r), k, send_z.at[r, k], z_target(r)).wait_send()

            @pl.when(yl == 0)
            def _():
                kv_copy(yl * NZ + z_of(r), k, send_y.at[r, k], y_target[k]).wait_send()

            @pl.when(r > 0)
            def _():
                kv_copy(yl * NZ + z_of(r), k, sib_a.at[r, k], sibling).wait_send()

            @pl.when(yl == 1)
            def _():
                kv_copy(z_of(r), k, sib_b.at[r, k], sibling).wait_send()

        return carry

    lax.fori_loop(0, 8, drain, 0)


def on_device(q_nope, q_rope, absorb_key, kv_latent, value_up, out_proj):
    rows = q_nope.shape[0]
    heads = absorb_key.shape[0]
    columns = out_proj.shape[1]
    kv_parts = kv_latent.reshape(4, rows // 4, WIDE)
    dma = pltpu.SemaphoreType.DMA
    return pl.pallas_call(
        kernel,
        out_shape=jax.ShapeDtypeStruct((rows, columns), jnp.bfloat16),
        in_specs=[pl.BlockSpec(memory_space=pl.ANY)] * 6,
        out_specs=pl.BlockSpec(memory_space=pltpu.VMEM),
        scratch_shapes=[
            pltpu.VMEM(q_nope.shape, jnp.bfloat16),
            pltpu.VMEM(q_rope.shape, jnp.bfloat16),
            pltpu.VMEM(absorb_key.shape, jnp.bfloat16),
            pltpu.VMEM(value_up.shape, jnp.bfloat16),
            pltpu.VMEM(out_proj.shape, jnp.bfloat16),
            pltpu.VMEM((16, 4, rows // 4, WIDE), jnp.bfloat16),
            pltpu.VMEM((16, 2, rows, heads * VDIM // 2), jnp.bfloat16),
            pltpu.VMEM((heads, rows, WIDE), jnp.bfloat16),
            pltpu.VMEM((heads, rows, 128), jnp.float32),
            pltpu.VMEM((heads, rows, 128), jnp.float32),
            pltpu.VMEM((heads, rows, LAT), jnp.float32),
            pltpu.VMEM((rows, columns), jnp.float32),
            dma((9,)),
            dma((16, 4)),
            dma((8, 2)),
            dma((8, 2)),
            dma((8, 2)),
            dma((8, 2)),
            dma((16, 2)),
            dma((8, 2, 2)),
            dma((2,)),
            dma((8, 2)),
        ],
        compiler_params=pltpu.CompilerParams(
            collective_id=0, has_side_effects=True, vmem_limit_bytes=56 * 1024 * 1024
        ),
        cost_estimate=pl.CostEstimate(
            flops=12 * 10**9, bytes_accessed=10 * 10**6, transcendentals=4 * 10**6
        ),
    )(q_nope, q_rope, absorb_key, kv_parts, value_up, out_proj)


def solution(mesh):
    placed = (
        P("inner", "outer"),
        P("inner", "outer"),
        P("outer", None, None),
        P("inner", None),
        P("outer", None, None),
        P(None, "outer"),
    )
    return jax.shard_map(
        on_device, mesh=mesh, in_specs=placed, out_specs=P("inner", "outer"), check_vma=False
    )
```

```python
import math

import jax
import jax.numpy as jnp
from jax import lax
from jax.experimental import pallas as pl
from jax.experimental.pallas import tpu as pltpu
from jax.sharding import PartitionSpec as P

NOPE = 128
ROPE = 64
VDIM = 128
LAT = 512
WIDE = LAT + ROPE
MESH = pl.DeviceIdType.MESH
NT = (((1,), (1,)), ((), ()))
SCALE = math.log2(math.e) / math.sqrt(NOPE + ROPE)
NX, NZ = 4, 8


def div(a, b):
    return a // b if isinstance(a, int) else lax.div(a, b)


def rem(a, b):
    return a % b if isinstance(a, int) else lax.rem(a, b)


def kernel(
    qn_hbm, qr_hbm, ak_hbm, kv_hbm, vu_hbm, wo_hbm, out_ref,
    qn, qr, ak, vu, wo, kvbuf, vbuf, query, peak, total, acc, mix,
    local_sem, kv_recv, send_z, send_y, sib_a, sib_b, v_recv, send_x, send_c, sib_v,
):
    heads, rows = query.shape[0], query.shape[1]
    o, i = lax.axis_index("outer"), lax.axis_index("inner")
    core, yh, x = rem(o, 2), rem(div(o, 2), 2), div(o, 4)
    yl, z = div(i, NZ), rem(i, NZ)

    def outer_of(x_, yh_, core_):
        return (x_ * 2 + yh_) * 2 + core_

    sibling = (outer_of(x, yh, 1 - core), i)
    z_up = (o, yl * NZ + rem(z + 1, NZ))
    z_down = (o, yl * NZ + rem(z + NZ - 1, NZ))
    y_up = (outer_of(x, rem(yh + yl, 2), core), (1 - yl) * NZ + z)
    y_down = (outer_of(x, rem(yh + 1 - yl, 2), core), (1 - yl) * NZ + z)
    y_far = (outer_of(x, 1 - yh, core), i)
    x_up = (outer_of(rem(x + 1, NX), yh, core), i)
    x_down = (outer_of(rem(x + NX - 1, NX), yh, core), i)

    locals_ = [
        pltpu.make_async_copy(kv_hbm.at[part], kvbuf.at[i, part], local_sem.at[part])
        for part in range(4)
    ]
    for n, (src, dst) in enumerate(
        [(qn_hbm, qn), (ak_hbm, ak), (qr_hbm, qr), (vu_hbm, vu), (wo_hbm, wo)]
    ):
        locals_.append(pltpu.make_async_copy(src, dst, local_sem.at[4 + n]))
    for copy in locals_:
        copy.start()

    barrier = pltpu.get_barrier_semaphore()
    partners = (sibling, z_up, z_down, y_up, y_down, y_far, x_up, x_down)
    for partner in partners:
        pl.semaphore_signal(barrier, inc=1, device_id=partner, device_id_type=MESH)
    pl.semaphore_wait(barrier, len(partners))

    def kv_copy(j, k, send_sem, target):
        piece = kvbuf.at[j, 2 * core + k]
        return pltpu.make_async_remote_copy(
            src_ref=piece, dst_ref=piece, send_sem=send_sem,
            recv_sem=kv_recv.at[j, 2 * core + k], device_id=target, device_id_type=MESH,
        )

    def kv_arrived(j, part):
        piece = kvbuf.at[j, part]
        pltpu.make_async_remote_copy(
            src_ref=piece, dst_ref=piece, send_sem=send_z.at[0, 0],
            recv_sem=kv_recv.at[j, part], device_id=sibling, device_id_type=MESH,
        ).wait_recv()

    def z_of(r):
        step = div(r + 1, 2) * (1 - 2 * rem(r, 2))
        return rem(z + step + NZ, NZ)

    y_target = (y_up, y_down)

    for part in range(4):
        locals_[part].wait()
    for k in range(2):
        kv_copy(i, k, send_z.at[0, k], z_up).start()
        kv_copy(i, k, send_z.at[7, k], z_down).start()
    for k in range(2):
        @pl.when(yl == 0)
        def _():
            kv_copy(i, k, send_y.at[0, k], y_target[k]).start()

    def z_forwards(r, k):
        return (r <= 4) | (r == 5 + k)

    def z_target(r):
        return (o, yl * NZ + rem(z + 2 * rem(r, 2) - 1 + NZ, NZ))

    def relay_a(r):
        j = yl * NZ + z_of(r)
        for k in range(2):
            kv_arrived(j, 2 * core + k)

            @pl.when(z_forwards(r, k))
            def _():
                kv_copy(j, k, send_z.at[r, k], z_target(r)).start()

            @pl.when(yl == 0)
            def _():
                kv_copy(j, k, send_y.at[r, k], y_target[k]).start()

            kv_copy(j, k, sib_a.at[r, k], sibling).start()

    def relay_b(r):
        j = z_of(r)
        for k in range(2):
            kv_arrived(j, 2 * core + k)
            kv_copy(j, k, sib_b.at[r, k], sibling).start()

    locals_[4].wait()
    locals_[5].wait()
    locals_[6].wait()
    for h in range(heads):
        query[h, :, :LAT] = jnp.dot(
            qn[:, h * NOPE : (h + 1) * NOPE], ak[h], preferred_element_type=jnp.float32
        ).astype(jnp.bfloat16)
        query[h, :, LAT:] = qr[:, h * ROPE : (h + 1) * ROPE]

    def attend(j, first):
        keys = kvbuf[j].reshape(WIDE, rows)
        latent = keys[:LAT]

        def scores(h):
            s = jnp.dot(query[h], keys, preferred_element_type=jnp.float32) * SCALE
            if first:
                row = lax.broadcasted_iota(jnp.int32, s.shape, 0)
                col = lax.broadcasted_iota(jnp.int32, s.shape, 1)
                s = jnp.where(col <= row, s, jnp.float32(-1e30))
            return s

        def fold(h, s):
            top = jnp.max(s, axis=1, keepdims=True)
            if first:
                new = jnp.broadcast_to(top, (rows, 128))
            else:
                old = peak[h]
                new = jnp.maximum(old, top)
            w = jnp.exp2(s - jnp.concatenate([new] * (rows // 128), axis=1))
            part = w[:, :128]
            for n in range(1, rows // 128):
                part = part + w[:, n * 128 : (n + 1) * 128]
            update = lax.dot_general(
                w.astype(jnp.bfloat16), latent, NT, preferred_element_type=jnp.float32
            )
            peak[h] = new
            if first:
                total[h] = part
                acc[h] = update
            else:
                shrink = jnp.exp2(old - new)
                total[h] = total[h] * shrink + part
                acc[h] = acc[h] * jnp.concatenate([shrink] * (LAT // 128), axis=1) + update

        s = scores(0)
        for h in range(heads):
            ahead = scores(h + 1) if h + 1 < heads else None
            fold(h, s)
            s = ahead

    attend(i, True)

    @pl.when(yl == 1)
    def _():
        relay_b(0)

    def round_(r, carry):
        @pl.when(r < 7)
        def _():
            relay_a(r + 1)

        def side(ab, carry):
            @pl.when((ab == 1) & (r < 7) & (yl == 1))
            def _():
                relay_b(r + 1)

            j = (1 - ab) * (yl * NZ) + z_of(r)
            held = ((ab == 0) & (r > 0)) | ((ab == 1) & (yl == 1))

            @pl.when(held)
            def _():
                for k in range(2):
                    kv_arrived(j, 2 * (1 - core) + k)

            @pl.when(held & (j < i))
            def _():
                attend(j, False)

            return carry

        return lax.fori_loop(0, 2, side, carry)

    lax.fori_loop(0, 8, round_, 0)

    def block(e):
        n, dy = rem(e, 4), div(e, 4)
        dx = n + div(n, 2) * (1 - 2 * rem(n, 2))
        return rem(x + dx, NX), rem(yh + dy, 2)

    def v_copy(e, k, send_sem, target):
        xx, yy = block(e)
        slot = outer_of(xx, yy, core)
        piece = vbuf.at[slot, k]
        return pltpu.make_async_remote_copy(
            src_ref=piece, dst_ref=piece, send_sem=send_sem,
            recv_sem=v_recv.at[slot, k], device_id=target, device_id_type=MESH,
        )

    def v_arrived(slot, k):
        piece = vbuf.at[slot, k]
        pltpu.make_async_remote_copy(
            src_ref=piece, dst_ref=piece, send_sem=send_c.at[0],
            recv_sem=v_recv.at[slot, k], device_id=sibling, device_id_type=MESH,
        ).wait_recv()

    def own_slot(e):
        xx, yy = block(e)
        return outer_of(xx, yy, core)

    def sib_slot(e):
        xx, yy = block(e)
        return outer_of(xx, yy, 1 - core)

    locals_[7].wait()

    def send(e, k, way):
        sem = {
            "far": lambda: send_c.at[k], "up": lambda: send_x.at[e, k, 0],
            "down": lambda: send_x.at[e, k, 1], "sib": lambda: sib_v.at[e, k],
        }[way]()
        target = {"far": y_far, "up": x_up, "down": x_down, "sib": sibling}[way]
        return v_copy(e, k, sem, target)

    for h in range(heads):
        whole = jnp.sum(total[h], axis=1, keepdims=True)
        latent_out = (acc[h] * (1.0 / whole)).astype(jnp.bfloat16)
        vbuf[o, h // 2, :, (h % 2) * VDIM : (h % 2 + 1) * VDIM] = jnp.dot(
            latent_out, vu[h], preferred_element_type=jnp.float32
        ).astype(jnp.bfloat16)
        if h % 2 == 1:
            k = h // 2
            send(0, k, "far").start()
            send(0, k, "up").start()
            send(0, k, "down").start()
            send(0, k, "sib").start()

    locals_[8].wait()
    mix[...] = jnp.zeros_like(mix)

    def project(slot):
        depth = heads * VDIM // 2
        term = mix[...]
        for k in range(2):
            start = pl.multiple_of((slot * 2 + k) * depth, depth)
            term = term + lax.dot_general(
                wo[:, pl.ds(start, depth)], vbuf[slot, k], NT, preferred_element_type=jnp.float32
            )
        mix[...] = term

    def relay_v(e):
        def came(e, k):
            v_arrived(own_slot(e), k)
            send(e, k, "sib").start()

        if e == 1:
            came(1, 0)
            came(1, 1)
            send(1, 1, "down").start()
        if e == 2:
            came(2, 0)
            send(2, 0, "up").start()
            came(2, 1)
        if e == 3:
            for k in range(2):
                v_arrived(own_slot(4), k)
                send(4, k, "up").start()
                send(4, k, "down").start()
                send(4, k, "sib").start()
            came(3, 0)
            came(3, 1)
        if e == 5:
            came(5, 0)
            came(5, 1)
            send(5, 1, "down").start()
        if e == 6:
            came(6, 0)
            send(6, 0, "up").start()
            came(6, 1)
        if e == 7:
            came(7, 0)
            came(7, 1)

    def event(e, carry):
        for n in (1, 2, 3, 5, 6, 7):
            @pl.when(e == n)
            def _():
                relay_v(n)

        @pl.when(e > 0)
        def _():
            project(own_slot(e - 1))
            for k in range(2):
                v_arrived(sib_slot(e - 1), k)
            project(sib_slot(e - 1))

        return carry

    lax.fori_loop(0, 9, event, 0)
    out_ref[...] = mix[...].astype(jnp.bfloat16)

    for e in range(8):
        for k in range(2):
            ways = ["sib"]
            if e == 0:
                ways += ["far"]
            if e in (0, 4):
                ways += ["up", "down"]
            if (e, k) in ((2, 0), (6, 0)):
                ways += ["up"]
            if (e, k) in ((1, 1), (5, 1)):
                ways += ["down"]
            for way in ways:
                send(e, k, way).wait_send()
    for k in range(2):
        kv_copy(i, k, send_z.at[0, k], z_up).wait_send()
        kv_copy(i, k, send_z.at[7, k], z_down).wait_send()

    def drain(r, carry):
        for k in range(2):
            @pl.when((r > 0) & z_forwards(r, k))
            def _():
                kv_copy(yl * NZ + z_of(r), k, send_z.at[r, k], z_target(r)).wait_send()

            @pl.when(yl == 0)
            def _():
                kv_copy(yl * NZ + z_of(r), k, send_y.at[r, k], y_target[k]).wait_send()

            @pl.when(r > 0)
            def _():
                kv_copy(yl * NZ + z_of(r), k, sib_a.at[r, k], sibling).wait_send()

            @pl.when(yl == 1)
            def _():
                kv_copy(z_of(r), k, sib_b.at[r, k], sibling).wait_send()

        return carry

    lax.fori_loop(0, 8, drain, 0)


def on_device(q_nope, q_rope, absorb_key, kv_latent, value_up, out_proj):
    rows = q_nope.shape[0]
    heads = absorb_key.shape[0]
    columns = out_proj.shape[1]
    kv_parts = kv_latent.T.reshape(4, WIDE // 4, rows)
    out_proj = out_proj.T
    dma = pltpu.SemaphoreType.DMA
    mixed = pl.pallas_call(
        kernel,
        out_shape=jax.ShapeDtypeStruct((columns, rows), jnp.bfloat16),
        in_specs=[pl.BlockSpec(memory_space=pl.ANY)] * 6,
        out_specs=pl.BlockSpec(memory_space=pltpu.VMEM),
        scratch_shapes=[
            pltpu.VMEM(q_nope.shape, jnp.bfloat16),
            pltpu.VMEM(q_rope.shape, jnp.bfloat16),
            pltpu.VMEM(absorb_key.shape, jnp.bfloat16),
            pltpu.VMEM(value_up.shape, jnp.bfloat16),
            pltpu.VMEM(out_proj.shape, jnp.bfloat16),
            pltpu.VMEM((16, 4, WIDE // 4, rows), jnp.bfloat16),
            pltpu.VMEM((16, 2, rows, heads * VDIM // 2), jnp.bfloat16),
            pltpu.VMEM((heads, rows, WIDE), jnp.bfloat16),
            pltpu.VMEM((heads, rows, 128), jnp.float32),
            pltpu.VMEM((heads, rows, 128), jnp.float32),
            pltpu.VMEM((heads, rows, LAT), jnp.float32),
            pltpu.VMEM((columns, rows), jnp.float32),
            dma((9,)),
            dma((16, 4)),
            dma((8, 2)),
            dma((8, 2)),
            dma((8, 2)),
            dma((8, 2)),
            dma((16, 2)),
            dma((8, 2, 2)),
            dma((2,)),
            dma((8, 2)),
        ],
        compiler_params=pltpu.CompilerParams(
            collective_id=0, has_side_effects=True, vmem_limit_bytes=56 * 1024 * 1024
        ),
        cost_estimate=pl.CostEstimate(
            flops=12 * 10**9, bytes_accessed=10 * 10**6, transcendentals=4 * 10**6
        ),
    )(q_nope, q_rope, absorb_key, kv_parts, value_up, out_proj)
    return mixed.T


def solution(mesh):
    placed = (
        P("inner", "outer"),
        P("inner", "outer"),
        P("outer", None, None),
        P("inner", None),
        P("outer", None, None),
        P(None, "outer"),
    )
    return jax.shard_map(
        on_device, mesh=mesh, in_specs=placed, out_specs=P("inner", "outer"), check_vma=False
    )
```

```python
import math

import jax
import jax.numpy as jnp
from jax import lax
from jax.experimental import pallas as pl
from jax.experimental.pallas import tpu as pltpu
from jax.sharding import PartitionSpec as P

NOPE = 128
ROPE = 64
VDIM = 128
LAT = 512
WIDE = LAT + ROPE
MESH = pl.DeviceIdType.MESH
NT = (((1,), (1,)), ((), ()))
SCALE = math.log2(math.e) / math.sqrt(NOPE + ROPE)
NX, NZ = 4, 8


def div(a, b):
    return a // b if isinstance(a, int) else lax.div(a, b)


def rem(a, b):
    return a % b if isinstance(a, int) else lax.rem(a, b)


def kernel(
    qn_hbm, qr_hbm, ak_hbm, kv_hbm, vu_hbm, wo_hbm, out_ref,
    qn, qr, ak, vu, wo, kvbuf, vbuf, query, peak, total, acc, mix,
    local_sem, kv_recv, send_z, send_y, sib_a, sib_b, v_recv, send_x, send_c, sib_v,
):
    heads, rows = query.shape[0], query.shape[1]
    o, i = lax.axis_index("outer"), lax.axis_index("inner")
    core, yh, x = rem(o, 2), rem(div(o, 2), 2), div(o, 4)
    yl, z = div(i, NZ), rem(i, NZ)

    def outer_of(x_, yh_, core_):
        return (x_ * 2 + yh_) * 2 + core_

    sibling = (outer_of(x, yh, 1 - core), i)
    z_up = (o, yl * NZ + rem(z + 1, NZ))
    z_down = (o, yl * NZ + rem(z + NZ - 1, NZ))
    y_up = (outer_of(x, rem(yh + yl, 2), core), (1 - yl) * NZ + z)
    y_down = (outer_of(x, rem(yh + 1 - yl, 2), core), (1 - yl) * NZ + z)
    y_far = (outer_of(x, 1 - yh, core), i)
    x_up = (outer_of(rem(x + 1, NX), yh, core), i)
    x_down = (outer_of(rem(x + NX - 1, NX), yh, core), i)

    locals_ = [
        pltpu.make_async_copy(kv_hbm.at[part], kvbuf.at[i, part], local_sem.at[part])
        for part in range(4)
    ]
    for n, (src, dst) in enumerate(
        [(qn_hbm, qn), (ak_hbm, ak), (qr_hbm, qr), (vu_hbm, vu), (wo_hbm, wo)]
    ):
        locals_.append(pltpu.make_async_copy(src, dst, local_sem.at[4 + n]))
    for copy in locals_:
        copy.start()

    barrier = pltpu.get_barrier_semaphore()
    partners = (sibling, z_up, z_down, y_up, y_down, y_far, x_up, x_down)
    for partner in partners:
        pl.semaphore_signal(barrier, inc=1, device_id=partner, device_id_type=MESH)
    pl.semaphore_wait(barrier, len(partners))

    def kv_copy(j, k, send_sem, target):
        piece = kvbuf.at[j, 2 * core + k]
        return pltpu.make_async_remote_copy(
            src_ref=piece, dst_ref=piece, send_sem=send_sem,
            recv_sem=kv_recv.at[j, 2 * core + k], device_id=target, device_id_type=MESH,
        )

    def kv_arrived(j, part):
        piece = kvbuf.at[j, part]
        pltpu.make_async_remote_copy(
            src_ref=piece, dst_ref=piece, send_sem=send_z.at[0, 0],
            recv_sem=kv_recv.at[j, part], device_id=sibling, device_id_type=MESH,
        ).wait_recv()

    def z_of(r):
        step = div(r + 1, 2) * (1 - 2 * rem(r, 2))
        return rem(z + step + NZ, NZ)

    y_target = (y_up, y_down)

    for part in range(4):
        locals_[part].wait()
    for k in range(2):
        kv_copy(i, k, send_z.at[0, k], z_up).start()
        kv_copy(i, k, send_z.at[7, k], z_down).start()
    for k in range(2):
        @pl.when(yl == 0)
        def _():
            kv_copy(i, k, send_y.at[0, k], y_target[k]).start()

    def z_forwards(r, k):
        return (r <= 4) | (r == 5 + k)

    def z_target(r):
        return (o, yl * NZ + rem(z + 2 * rem(r, 2) - 1 + NZ, NZ))

    def relay_a(r):
        j = yl * NZ + z_of(r)
        for k in range(2):
            kv_arrived(j, 2 * core + k)

            @pl.when(z_forwards(r, k))
            def _():
                kv_copy(j, k, send_z.at[r, k], z_target(r)).start()

            @pl.when(yl == 0)
            def _():
                kv_copy(j, k, send_y.at[r, k], y_target[k]).start()

            kv_copy(j, k, sib_a.at[r, k], sibling).start()

    def relay_b(r):
        j = z_of(r)
        for k in range(2):
            kv_arrived(j, 2 * core + k)
            kv_copy(j, k, sib_b.at[r, k], sibling).start()

    locals_[4].wait()
    locals_[5].wait()
    locals_[6].wait()
    for h in range(heads):
        query[h, :, :LAT] = jnp.dot(
            qn[:, h * NOPE : (h + 1) * NOPE], ak[h], preferred_element_type=jnp.float32
        ).astype(jnp.bfloat16)
        query[h, :, LAT:] = qr[:, h * ROPE : (h + 1) * ROPE]

    def attend(j, first):
        keys = kvbuf[j].reshape(WIDE, rows)
        latent = keys[:LAT]

        def scores(h):
            s = jnp.dot(query[h], keys, preferred_element_type=jnp.float32) * SCALE
            if first:
                row = lax.broadcasted_iota(jnp.int32, s.shape, 0)
                col = lax.broadcasted_iota(jnp.int32, s.shape, 1)
                s = jnp.where(col <= row, s, jnp.float32(-1e30))
            return s

        def fold(h, s):
            top = jnp.max(s, axis=1, keepdims=True)
            if first:
                new = jnp.broadcast_to(top, (rows, 128))
            else:
                old = peak[h]
                new = jnp.maximum(old, top)
            w = jnp.exp2(s - jnp.concatenate([new] * (rows // 128), axis=1))
            part = w[:, :128]
            for n in range(1, rows // 128):
                part = part + w[:, n * 128 : (n + 1) * 128]
            update = lax.dot_general(
                w.astype(jnp.bfloat16), latent, NT, preferred_element_type=jnp.float32
            )
            peak[h] = new
            if first:
                total[h] = part
                acc[h] = update
            else:
                shrink = jnp.exp2(old - new)
                total[h] = total[h] * shrink + part
                acc[h] = acc[h] * jnp.concatenate([shrink] * (LAT // 128), axis=1) + update

        s = scores(0)
        for h in range(heads):
            ahead = scores(h + 1) if h + 1 < heads else None
            fold(h, s)
            s = ahead

    attend(i, True)

    @pl.when(yl == 1)
    def _():
        relay_b(0)

    def round_(r, carry):
        @pl.when(r < 7)
        def _():
            relay_a(r + 1)

        def side(ab, carry):
            @pl.when((ab == 1) & (r < 7) & (yl == 1))
            def _():
                relay_b(r + 1)

            j = (1 - ab) * (yl * NZ) + z_of(r)
            held = ((ab == 0) & (r > 0)) | ((ab == 1) & (yl == 1))

            @pl.when(held)
            def _():
                for k in range(2):
                    kv_arrived(j, 2 * (1 - core) + k)

            @pl.when(held & (j < i))
            def _():
                attend(j, False)

            return carry

        return lax.fori_loop(0, 2, side, carry)

    lax.fori_loop(0, 8, round_, 0)

    def block(e):
        n, dy = rem(e, 4), div(e, 4)
        dx = n + div(n, 2) * (1 - 2 * rem(n, 2))
        return rem(x + dx, NX), rem(yh + dy, 2)

    def v_copy(e, k, send_sem, target):
        xx, yy = block(e)
        slot = outer_of(xx, yy, core)
        piece = vbuf.at[slot, k]
        return pltpu.make_async_remote_copy(
            src_ref=piece, dst_ref=piece, send_sem=send_sem,
            recv_sem=v_recv.at[slot, k], device_id=target, device_id_type=MESH,
        )

    def v_arrived(slot, k):
        piece = vbuf.at[slot, k]
        pltpu.make_async_remote_copy(
            src_ref=piece, dst_ref=piece, send_sem=send_c.at[0, 0],
            recv_sem=v_recv.at[slot, k], device_id=sibling, device_id_type=MESH,
        ).wait_recv()

    def own_slot(e):
        xx, yy = block(e)
        return outer_of(xx, yy, core)

    def sib_slot(e):
        xx, yy = block(e)
        return outer_of(xx, yy, 1 - core)

    locals_[7].wait()

    def send(e, k, way):
        sem = {
            "far": lambda: send_c.at[e, k], "up": lambda: send_x.at[e, k, 0],
            "down": lambda: send_x.at[e, k, 1], "sib": lambda: sib_v.at[e, k],
        }[way]()
        target = {"far": y_far, "up": x_up, "down": x_down, "sib": sibling}[way]
        return v_copy(e, k, sem, target)

    for h in range(heads):
        whole = jnp.sum(total[h], axis=1, keepdims=True)
        latent_out = (acc[h] * (1.0 / whole)).astype(jnp.bfloat16)
        vbuf[o, h // 2, :, (h % 2) * VDIM : (h % 2 + 1) * VDIM] = jnp.dot(
            latent_out, vu[h], preferred_element_type=jnp.float32
        ).astype(jnp.bfloat16)
        if h % 2 == 1:
            k = h // 2
            send(0, k, "far").start()
            send(0, k, "up").start()
            send(0, k, "down").start()
            send(0, k, "sib").start()

    locals_[8].wait()
    mix[...] = jnp.zeros_like(mix)

    def project(slot):
        depth = heads * VDIM // 2
        term = mix[...]
        for k in range(2):
            start = pl.multiple_of((slot * 2 + k) * depth, depth)
            term = term + lax.dot_general(
                wo[:, pl.ds(start, depth)], vbuf[slot, k], NT, preferred_element_type=jnp.float32
            )
        mix[...] = term

    def relay_v(e):
        def came(e, k, *ways):
            v_arrived(own_slot(e), k)
            for way in ways:
                send(e, k, way).start()
            send(e, k, "sib").start()

        if e == 1:
            came(1, 0, "far")
            came(1, 1, "down", "far")
        if e == 2:
            came(2, 0, "up")
            came(2, 1)
        if e == 3:
            came(4, 0, "up")
            came(4, 1, "up")
            came(3, 0)
            came(3, 1)
        if e == 5:
            came(5, 0, "down")
            came(5, 1, "down")
        if e >= 6:
            came(e, 0)
            came(e, 1)

    def event(e, carry):
        for n in (1, 2, 3, 5, 6, 7):
            @pl.when(e == n)
            def _():
                relay_v(n)

        @pl.when(e > 0)
        def _():
            project(own_slot(e - 1))
            for k in range(2):
                v_arrived(sib_slot(e - 1), k)
            project(sib_slot(e - 1))

        return carry

    lax.fori_loop(0, 9, event, 0)
    out_ref[...] = mix[...].astype(jnp.bfloat16)

    for e in range(8):
        for k in range(2):
            ways = ["sib"]
            if e <= 1:
                ways += ["far"]
            if e in (0, 4) or (e, k) == (2, 0):
                ways += ["up"]
            if e in (0, 5) or (e, k) == (1, 1):
                ways += ["down"]
            for way in ways:
                send(e, k, way).wait_send()
    for k in range(2):
        kv_copy(i, k, send_z.at[0, k], z_up).wait_send()
        kv_copy(i, k, send_z.at[7, k], z_down).wait_send()

    def drain(r, carry):
        for k in range(2):
            @pl.when((r > 0) & z_forwards(r, k))
            def _():
                kv_copy(yl * NZ + z_of(r), k, send_z.at[r, k], z_target(r)).wait_send()

            @pl.when(yl == 0)
            def _():
                kv_copy(yl * NZ + z_of(r), k, send_y.at[r, k], y_target[k]).wait_send()

            @pl.when(r > 0)
            def _():
                kv_copy(yl * NZ + z_of(r), k, sib_a.at[r, k], sibling).wait_send()

            @pl.when(yl == 1)
            def _():
                kv_copy(z_of(r), k, sib_b.at[r, k], sibling).wait_send()

        return carry

    lax.fori_loop(0, 8, drain, 0)


def on_device(q_nope, q_rope, absorb_key, kv_latent, value_up, out_proj):
    rows = q_nope.shape[0]
    heads = absorb_key.shape[0]
    columns = out_proj.shape[1]
    kv_parts = kv_latent.T.reshape(4, WIDE // 4, rows)
    out_proj = out_proj.T
    dma = pltpu.SemaphoreType.DMA
    mixed = pl.pallas_call(
        kernel,
        out_shape=jax.ShapeDtypeStruct((columns, rows), jnp.bfloat16),
        in_specs=[pl.BlockSpec(memory_space=pl.ANY)] * 6,
        out_specs=pl.BlockSpec(memory_space=pltpu.VMEM),
        scratch_shapes=[
            pltpu.VMEM(q_nope.shape, jnp.bfloat16),
            pltpu.VMEM(q_rope.shape, jnp.bfloat16),
            pltpu.VMEM(absorb_key.shape, jnp.bfloat16),
            pltpu.VMEM(value_up.shape, jnp.bfloat16),
            pltpu.VMEM(out_proj.shape, jnp.bfloat16),
            pltpu.VMEM((16, 4, WIDE // 4, rows), jnp.bfloat16),
            pltpu.VMEM((16, 2, rows, heads * VDIM // 2), jnp.bfloat16),
            pltpu.VMEM((heads, rows, WIDE), jnp.bfloat16),
            pltpu.VMEM((heads, rows, 128), jnp.float32),
            pltpu.VMEM((heads, rows, 128), jnp.float32),
            pltpu.VMEM((heads, rows, LAT), jnp.float32),
            pltpu.VMEM((columns, rows), jnp.float32),
            dma((9,)),
            dma((16, 4)),
            dma((8, 2)),
            dma((8, 2)),
            dma((8, 2)),
            dma((8, 2)),
            dma((16, 2)),
            dma((8, 2, 2)),
            dma((2, 2)),
            dma((8, 2)),
        ],
        compiler_params=pltpu.CompilerParams(
            collective_id=0, has_side_effects=True, vmem_limit_bytes=56 * 1024 * 1024
        ),
        cost_estimate=pl.CostEstimate(
            flops=12 * 10**9, bytes_accessed=10 * 10**6, transcendentals=4 * 10**6
        ),
    )(q_nope, q_rope, absorb_key, kv_parts, value_up, out_proj)
    return mixed.T


def solution(mesh):
    placed = (
        P("inner", "outer"),
        P("inner", "outer"),
        P("outer", None, None),
        P("inner", None),
        P("outer", None, None),
        P(None, "outer"),
    )
    return jax.shard_map(
        on_device, mesh=mesh, in_specs=placed, out_specs=P("inner", "outer"), check_vma=False
    )
```

```python
import math

import jax
import jax.numpy as jnp
from jax import lax
from jax.experimental import pallas as pl
from jax.experimental.pallas import tpu as pltpu
from jax.sharding import PartitionSpec as P

NOPE = 128
ROPE = 64
VDIM = 128
LAT = 512
WIDE = LAT + ROPE
MESH = pl.DeviceIdType.MESH
NT = (((1,), (1,)), ((), ()))
SCALE = math.log2(math.e) / math.sqrt(NOPE + ROPE)
NX, NZ = 4, 8


def div(a, b):
    return a // b if isinstance(a, int) else lax.div(a, b)


def rem(a, b):
    return a % b if isinstance(a, int) else lax.rem(a, b)


def kernel(
    qn_hbm, qr_hbm, ak_hbm, kv_hbm, vu_hbm, wo_hbm, out_ref,
    qn, qr, ak, vu, wo, kvbuf, vbuf, query, peak, total, acc, mix,
    local_sem, kv_recv, send_z, send_y, sib_a, sib_b, v_recv, send_x, send_c, sib_v,
):
    heads, rows = query.shape[0], query.shape[1]
    o, i = lax.axis_index("outer"), lax.axis_index("inner")
    core, yh, x = rem(o, 2), rem(div(o, 2), 2), div(o, 4)
    yl, z = div(i, NZ), rem(i, NZ)

    def outer_of(x_, yh_, core_):
        return (x_ * 2 + yh_) * 2 + core_

    sibling = (outer_of(x, yh, 1 - core), i)
    z_up = (o, yl * NZ + rem(z + 1, NZ))
    z_down = (o, yl * NZ + rem(z + NZ - 1, NZ))
    y_up = (outer_of(x, rem(yh + yl, 2), core), (1 - yl) * NZ + z)
    y_down = (outer_of(x, rem(yh + 1 - yl, 2), core), (1 - yl) * NZ + z)
    y_far = (outer_of(x, 1 - yh, core), i)
    x_up = (outer_of(rem(x + 1, NX), yh, core), i)
    x_down = (outer_of(rem(x + NX - 1, NX), yh, core), i)

    locals_ = [
        pltpu.make_async_copy(kv_hbm.at[part], kvbuf.at[i, part], local_sem.at[part])
        for part in range(4)
    ]
    for n, (src, dst) in enumerate(
        [(qn_hbm, qn), (ak_hbm, ak), (qr_hbm, qr), (vu_hbm, vu), (wo_hbm, wo)]
    ):
        locals_.append(pltpu.make_async_copy(src, dst, local_sem.at[4 + n]))
    for copy in locals_:
        copy.start()

    barrier = pltpu.get_barrier_semaphore()
    partners = (sibling, z_up, z_down, y_up, y_down, y_far, x_up, x_down)
    for partner in partners:
        pl.semaphore_signal(barrier, inc=1, device_id=partner, device_id_type=MESH)
    pl.semaphore_wait(barrier, len(partners))

    def kv_copy(j, k, send_sem, target):
        piece = kvbuf.at[j, 2 * core + k]
        return pltpu.make_async_remote_copy(
            src_ref=piece, dst_ref=piece, send_sem=send_sem,
            recv_sem=kv_recv.at[j, 2 * core + k], device_id=target, device_id_type=MESH,
        )

    def kv_arrived(j, part):
        piece = kvbuf.at[j, part]
        pltpu.make_async_remote_copy(
            src_ref=piece, dst_ref=piece, send_sem=send_z.at[0, 0, 0],
            recv_sem=kv_recv.at[j, part], device_id=sibling, device_id_type=MESH,
        ).wait_recv()

    def ring(d, side):
        return rem(z + (d if side else NZ - d), NZ)

    def z_forwards(d, side, k):
        return (d <= 2) | ((d == 3) & (k == side))

    def held_a(d, side, k):
        return (d <= 3) | ((d == 4) & (k == side))

    def held_b(d, side, k):
        return ((d == 0) & (side == 0)) | ((d >= 1) & (d <= 3)) | ((d == 4) & (k == side))

    def z_send(d, side, k):
        return kv_copy(yl * NZ + ring(d, side), k, send_z.at[side, d, k], (z_up, z_down)[side])

    def y_send(d, side, k):
        target = (outer_of(x, rem(yh + k, 2), core), NZ + z)
        return kv_copy(ring(d, side), k, send_y.at[side, d, k], target)

    def sib_a_send(d, side, k):
        return kv_copy(yl * NZ + ring(d, side), k, sib_a.at[side, d, k], sibling)

    def sib_b_send(d, side, k):
        return kv_copy(ring(d, side), k, sib_b.at[side, d, k], sibling)

    def relay_a(d, k):
        for side in range(2):
            j = yl * NZ + ring(d, side)

            @pl.when(held_a(d, side, k))
            def _():
                kv_arrived(j, 2 * core + k)

                @pl.when(z_forwards(d, side, k))
                def _():
                    z_send(d, side, k).start()

                @pl.when(yl == 0)
                def _():
                    y_send(d, side, k).start()

                @pl.when(j < i)
                def _():
                    sib_a_send(d, side, k).start()

    def relay_b(d, k):
        for side in range(2):
            @pl.when(held_b(d, side, k))
            def _():
                kv_arrived(ring(d, side), 2 * core + k)
                sib_b_send(d, side, k).start()

    for part in range(4):
        locals_[part].wait()

    def own(k):
        for side in range(2):
            z_send(0, side, k).start()

        @pl.when(yl == 0)
        def _():
            y_send(0, 0, k).start()

    own(0)

    locals_[4].wait()
    locals_[5].wait()
    locals_[6].wait()
    for h in range(heads):
        query[h, :, :LAT] = jnp.dot(
            qn[:, h * NOPE : (h + 1) * NOPE], ak[h], preferred_element_type=jnp.float32
        ).astype(jnp.bfloat16)
        query[h, :, LAT:] = qr[:, h * ROPE : (h + 1) * ROPE]

    def attend(j, first, some):
        keys = kvbuf[j].reshape(WIDE, rows)
        latent = keys[:LAT]

        def scores(h):
            s = jnp.dot(query[h], keys, preferred_element_type=jnp.float32) * SCALE
            if first:
                row = lax.broadcasted_iota(jnp.int32, s.shape, 0)
                col = lax.broadcasted_iota(jnp.int32, s.shape, 1)
                s = jnp.where(col <= row, s, jnp.float32(-1e30))
            return s

        def fold(h, s):
            top = jnp.max(s, axis=1, keepdims=True)
            if first:
                new = jnp.broadcast_to(top, (rows, 128))
            else:
                old = peak[h]
                new = jnp.maximum(old, top)
            w = jnp.exp2(s - jnp.concatenate([new] * (rows // 128), axis=1))
            part = w[:, :128]
            for n in range(1, rows // 128):
                part = part + w[:, n * 128 : (n + 1) * 128]
            update = lax.dot_general(
                w.astype(jnp.bfloat16), latent, NT, preferred_element_type=jnp.float32
            )
            peak[h] = new
            if first:
                total[h] = part
                acc[h] = update
            else:
                shrink = jnp.exp2(old - new)
                total[h] = total[h] * shrink + part
                acc[h] = acc[h] * jnp.concatenate([shrink] * (LAT // 128), axis=1) + update

        s = scores(some[0])
        for h in some:
            ahead = scores(h + 1) if h < some[-1] else None
            fold(h, s)
            s = ahead

    own(1)
    attend(i, True, range(heads))

    def swapped(j):
        for k in range(2):
            kv_arrived(j, 2 * (1 - core) + k)

    def half_step(n, carry):
        d, k = div(n, 2) + 1, rem(n, 2)

        @pl.when(d <= 4)
        def _():
            relay_a(d, k)

        def group(ab, carry):
            @pl.when((ab == 1) & (yl == 1))
            def _():
                relay_b(d - 1, k)

            dd = d - 1 - ab
            j = (1 - ab) * (yl * NZ) + rem(z + dd * (2 * k - 1) + NZ, NZ)
            in_a = (ab == 0) & (((dd >= 1) & (dd <= 3)) | ((dd == 4) & (k == 0) & (yl == 1)))
            in_b = (ab == 1) & (yl == 1) & (((dd >= 1) & (dd <= 3)) | ((dd == 0) & (k == 0)))

            @pl.when((in_a | in_b) & (j < i))
            def _():
                swapped(j)
                attend(j, False, range(heads))

            return carry

        return lax.fori_loop(0, 2, group, carry)

    lax.fori_loop(0, 10, half_step, 0)
    last = rem(z + 4, NZ)

    def block(e):
        n, dy = rem(e, 4), div(e, 4)
        dx = n + div(n, 2) * (1 - 2 * rem(n, 2))
        return rem(x + dx, NX), rem(yh + dy, 2)

    def v_copy(e, k, send_sem, target):
        xx, yy = block(e)
        slot = outer_of(xx, yy, core)
        piece = vbuf.at[slot, k]
        return pltpu.make_async_remote_copy(
            src_ref=piece, dst_ref=piece, send_sem=send_sem,
            recv_sem=v_recv.at[slot, k], device_id=target, device_id_type=MESH,
        )

    def v_arrived(slot, k):
        piece = vbuf.at[slot, k]
        pltpu.make_async_remote_copy(
            src_ref=piece, dst_ref=piece, send_sem=send_c.at[0, 0],
            recv_sem=v_recv.at[slot, k], device_id=sibling, device_id_type=MESH,
        ).wait_recv()

    def own_slot(e):
        xx, yy = block(e)
        return outer_of(xx, yy, core)

    def sib_slot(e):
        xx, yy = block(e)
        return outer_of(xx, yy, 1 - core)

    locals_[7].wait()

    def send(e, k, way):
        sem = {
            "far": lambda: send_c.at[e, k], "up": lambda: send_x.at[e, k, 0],
            "down": lambda: send_x.at[e, k, 1], "sib": lambda: sib_v.at[e, k],
        }[way]()
        target = {"far": y_far, "up": x_up, "down": x_down, "sib": sibling}[way]
        return v_copy(e, k, sem, target)

    for k in range(2):
        pair = (2 * k, 2 * k + 1)

        @pl.when(last < i)
        def _():
            if k == 0:
                swapped(last)
            attend(last, False, pair)

        for h in pair:
            whole = jnp.sum(total[h], axis=1, keepdims=True)
            latent_out = (acc[h] * (1.0 / whole)).astype(jnp.bfloat16)
            vbuf[o, k, :, (h % 2) * VDIM : (h % 2 + 1) * VDIM] = jnp.dot(
                latent_out, vu[h], preferred_element_type=jnp.float32
            ).astype(jnp.bfloat16)
        for way in ("up", "down", "far", "sib"):
            send(0, k, way).start()

    locals_[8].wait()
    mix[...] = jnp.zeros_like(mix)

    def project(e):
        depth = heads * VDIM // 2
        term = mix[...]
        for slot in (own_slot(e), sib_slot(e)):
            for k in range(2):
                start = pl.multiple_of((slot * 2 + k) * depth, depth)
                term = term + lax.dot_general(
                    wo[:, pl.ds(start, depth)], vbuf[slot, k], NT,
                    preferred_element_type=jnp.float32,
                )
        mix[...] = term

    came = (
        ((1, 0, "far"), (2, 0, "up"), (4, 0, "up")),
        ((1, 1, "down", "far"), (2, 1), (4, 1, "up")),
        ((3, 0), (5, 0, "down"), (3, 1)),
        ((6, 0), (5, 1, "down")),
        ((6, 1),),
        ((7, 0),),
        ((7, 1),),
    )

    def event(t, carry):
        for n, items in enumerate(came):
            @pl.when(t == n)
            def _():
                for e, k, *ways in items:
                    v_arrived(own_slot(e), k)
                    for way in (*ways, "sib"):
                        send(e, k, way).start()

        for k in range(2):
            v_arrived(sib_slot(t), k)
        project(t)
        return carry

    lax.fori_loop(0, 8, event, 0)
    out_ref[...] = mix[...].astype(jnp.bfloat16)

    for k in range(2):
        for way in ("up", "down", "far", "sib"):
            send(0, k, way).wait_send()
    for items in came:
        for e, k, *ways in items:
            for way in (*ways, "sib"):
                send(e, k, way).wait_send()

    def drain(n, carry):
        d, k = div(n, 2), rem(n, 2)
        for side in range(2):
            @pl.when(z_forwards(d, side, k))
            def _():
                z_send(d, side, k).wait_send()

            @pl.when((yl == 0) & held_b(d, side, k))
            def _():
                y_send(d, side, k).wait_send()

            @pl.when((d >= 1) & held_a(d, side, k) & (yl * NZ + ring(d, side) < i))
            def _():
                sib_a_send(d, side, k).wait_send()

            @pl.when((yl == 1) & held_b(d, side, k))
            def _():
                sib_b_send(d, side, k).wait_send()

        return carry

    lax.fori_loop(0, 10, drain, 0)


def on_device(q_nope, q_rope, absorb_key, kv_latent, value_up, out_proj):
    rows = q_nope.shape[0]
    heads = absorb_key.shape[0]
    columns = out_proj.shape[1]
    kv_parts = kv_latent.T.reshape(4, WIDE // 4, rows)
    out_proj = out_proj.T
    dma = pltpu.SemaphoreType.DMA
    mixed = pl.pallas_call(
        kernel,
        out_shape=jax.ShapeDtypeStruct((columns, rows), jnp.bfloat16),
        in_specs=[pl.BlockSpec(memory_space=pl.ANY)] * 6,
        out_specs=pl.BlockSpec(memory_space=pltpu.VMEM),
        scratch_shapes=[
            pltpu.VMEM(q_nope.shape, jnp.bfloat16),
            pltpu.VMEM(q_rope.shape, jnp.bfloat16),
            pltpu.VMEM(absorb_key.shape, jnp.bfloat16),
            pltpu.VMEM(value_up.shape, jnp.bfloat16),
            pltpu.VMEM(out_proj.shape, jnp.bfloat16),
            pltpu.VMEM((16, 4, WIDE // 4, rows), jnp.bfloat16),
            pltpu.VMEM((16, 2, rows, heads * VDIM // 2), jnp.bfloat16),
            pltpu.VMEM((heads, rows, WIDE), jnp.bfloat16),
            pltpu.VMEM((heads, rows, 128), jnp.float32),
            pltpu.VMEM((heads, rows, 128), jnp.float32),
            pltpu.VMEM((heads, rows, LAT), jnp.float32),
            pltpu.VMEM((columns, rows), jnp.float32),
            dma((9,)),
            dma((16, 4)),
            dma((2, 4, 2)),
            dma((2, 5, 2)),
            dma((2, 5, 2)),
            dma((2, 5, 2)),
            dma((16, 2)),
            dma((8, 2, 2)),
            dma((2, 2)),
            dma((8, 2)),
        ],
        compiler_params=pltpu.CompilerParams(
            collective_id=0, has_side_effects=True, vmem_limit_bytes=56 * 1024 * 1024
        ),
        cost_estimate=pl.CostEstimate(
            flops=12 * 10**9, bytes_accessed=10 * 10**6, transcendentals=4 * 10**6
        ),
    )(q_nope, q_rope, absorb_key, kv_parts, value_up, out_proj)
    return mixed.T


def solution(mesh):
    placed = (
        P("inner", "outer"),
        P("inner", "outer"),
        P("outer", None, None),
        P("inner", None),
        P("outer", None, None),
        P(None, "outer"),
    )
    return jax.shard_map(
        on_device, mesh=mesh, in_specs=placed, out_specs=P("inner", "outer"), check_vma=False
    )
```

```python
import math

import jax
import jax.numpy as jnp
from jax import lax
from jax.experimental import pallas as pl
from jax.experimental.pallas import tpu as pltpu
from jax.sharding import PartitionSpec as P

NOPE = 128
ROPE = 64
VDIM = 128
LAT = 512
WIDE = LAT + ROPE
MESH = pl.DeviceIdType.MESH
NT = (((1,), (1,)), ((), ()))
SCALE = math.log2(math.e) / math.sqrt(NOPE + ROPE)
NX, NZ = 4, 8


def div(a, b):
    return a // b if isinstance(a, int) else lax.div(a, b)


def rem(a, b):
    return a % b if isinstance(a, int) else lax.rem(a, b)


def kernel(
    qn_hbm, qr_hbm, ak_hbm, kv_hbm, vu_hbm, wo_hbm, out_ref,
    qn, qr, ak, vu, wo, kvbuf, vbuf, query, peak, total, acc, mix,
    local_sem, kv_recv, send_z, send_y, sib_a, sib_b, far_z, far_y, far_x, far_sib,
    v_recv, send_x, send_c, sib_v,
):
    heads, rows = query.shape[0], query.shape[1]
    o, i = lax.axis_index("outer"), lax.axis_index("inner")
    core, yh, x = rem(o, 2), rem(div(o, 2), 2), div(o, 4)
    yl, z = div(i, NZ), rem(i, NZ)

    def outer_of(x_, yh_, core_):
        return (x_ * 2 + yh_) * 2 + core_

    sibling = (outer_of(x, yh, 1 - core), i)
    z_up = (o, yl * NZ + rem(z + 1, NZ))
    z_down = (o, yl * NZ + rem(z + NZ - 1, NZ))
    y_up = (outer_of(x, rem(yh + yl, 2), core), (1 - yl) * NZ + z)
    y_down = (outer_of(x, rem(yh + 1 - yl, 2), core), (1 - yl) * NZ + z)
    y_far = (outer_of(x, 1 - yh, core), i)
    x_up = (outer_of(rem(x + 1, NX), yh, core), i)
    x_down = (outer_of(rem(x + NX - 1, NX), yh, core), i)

    x_far = (outer_of(rem(x + 2, NX), yh, core), i)
    far_target = tuple((o, yl * NZ + rem(z + n, NZ)) for n in (3, NZ - 3, 4))

    locals_ = [
        pltpu.make_async_copy(kv_hbm.at[part], kvbuf.at[i, part], local_sem.at[part])
        for part in range(4)
    ]
    for n, (src, dst) in enumerate(
        [(qn_hbm, qn), (ak_hbm, ak), (qr_hbm, qr), (vu_hbm, vu), (wo_hbm, wo)]
    ):
        locals_.append(pltpu.make_async_copy(src, dst, local_sem.at[4 + n]))
    for copy in locals_:
        copy.start()

    barrier = pltpu.get_barrier_semaphore()
    partners = (sibling, z_up, z_down, *far_target, y_up, y_down, y_far, x_up, x_down, x_far)
    for partner in partners:
        pl.semaphore_signal(barrier, inc=1, device_id=partner, device_id_type=MESH)
    pl.semaphore_wait(barrier, len(partners))

    def part_copy(j, part, send_sem, target):
        piece = kvbuf.at[j, part]
        return pltpu.make_async_remote_copy(
            src_ref=piece, dst_ref=piece, send_sem=send_sem,
            recv_sem=kv_recv.at[j, part], device_id=target, device_id_type=MESH,
        )

    def kv_copy(j, k, send_sem, target):
        return part_copy(j, 2 * core + k, send_sem, target)

    def kv_arrived(j, part):
        piece = kvbuf.at[j, part]
        pltpu.make_async_remote_copy(
            src_ref=piece, dst_ref=piece, send_sem=send_z.at[0, 0, 0],
            recv_sem=kv_recv.at[j, part], device_id=sibling, device_id_type=MESH,
        ).wait_recv()

    def ring(d, side):
        return rem(z + (d if side else NZ - d), NZ)

    def held_b(d, side):
        return (d <= 2) & ((d >= 1) | (side == 0))

    def z_send(d, side, k):
        return kv_copy(yl * NZ + ring(d, side), k, send_z.at[side, d, k], (z_up, z_down)[side])

    def y_send(d, side, k):
        target = (outer_of(x, rem(yh + k, 2), core), NZ + z)
        return kv_copy(ring(d, side), k, send_y.at[side, d, k], target)

    def sib_a_send(d, side, k):
        return kv_copy(yl * NZ + ring(d, side), k, sib_a.at[side, d, k], sibling)

    def sib_b_send(d, side, k):
        return kv_copy(ring(d, side), k, sib_b.at[side, d, k], sibling)

    def relay_a(d, k):
        for side in range(2):
            j = yl * NZ + ring(d, side)
            kv_arrived(j, 2 * core + k)

            @pl.when(d == 1)
            def _():
                z_send(d, side, k).start()

            @pl.when(yl == 0)
            def _():
                y_send(d, side, k).start()

            @pl.when(j < i)
            def _():
                sib_a_send(d, side, k).start()

    def relay_b(d, k):
        for side in range(2):
            @pl.when(held_b(d, side))
            def _():
                kv_arrived(ring(d, side), 2 * core + k)
                sib_b_send(d, side, k).start()

    far_hops = ((3, 0), (3, 1), (4, 0))
    far_core = (1, 0, rem(z, 2))

    def far_shard(f, group):
        return group * NZ + ring(*far_hops[f])

    def far_z_send(f):
        return part_copy(i, x, far_z.at[f], far_target[f])

    def far_y_send(f):
        way = (0, 1, rem(x, 2))[f]
        target = (outer_of(x, rem(yh + way, 2), core), NZ + z)
        return part_copy(far_shard(f, 0), x, far_y.at[f], target)

    def far_x_sends(f, group, ab):
        return [
            part_copy(far_shard(f, group), x, far_x.at[ab, f, n], target)
            for n, target in enumerate((x_up, x_down, x_far))
        ]

    def far_sib_send(f, group, ab, n):
        return part_copy(far_shard(f, group), rem(x + n, NX), far_sib.at[ab, f, n], sibling)

    def far_first(group, ab):
        for f in range(3):
            j = far_shard(f, group)

            @pl.when(core == far_core[f])
            def _():
                kv_arrived(j, x)
                if ab == 0:
                    @pl.when(yl == 0)
                    def _():
                        far_y_send(f).start()

                @pl.when(j < i)
                def _():
                    for copy in far_x_sends(f, group, ab):
                        copy.start()
                    far_sib_send(f, group, ab, 0).start()

    def far_rest(group, ab):
        for f in range(3):
            j = far_shard(f, group)

            @pl.when((core == far_core[f]) & (j < i))
            def _():
                for n in range(1, NX):
                    kv_arrived(j, rem(x + n, NX))
                    far_sib_send(f, group, ab, n).start()

    for part in range(4):
        locals_[part].wait()

    def own(k):
        for side in range(2):
            z_send(0, side, k).start()

        @pl.when(yl == 0)
        def _():
            y_send(0, 0, k).start()

    own(0)
    for f in range(3):
        @pl.when(core == far_core[f])
        def _():
            far_z_send(f).start()

    locals_[4].wait()
    locals_[5].wait()
    locals_[6].wait()
    for h in range(heads):
        query[h, :, :LAT] = jnp.dot(
            qn[:, h * NOPE : (h + 1) * NOPE], ak[h], preferred_element_type=jnp.float32
        ).astype(jnp.bfloat16)
        query[h, :, LAT:] = qr[:, h * ROPE : (h + 1) * ROPE]

    def attend(j, first, some):
        keys = kvbuf[j].reshape(WIDE, rows)
        latent = keys[:LAT]

        def scores(h):
            s = jnp.dot(query[h], keys, preferred_element_type=jnp.float32) * SCALE
            if first:
                row = lax.broadcasted_iota(jnp.int32, s.shape, 0)
                col = lax.broadcasted_iota(jnp.int32, s.shape, 1)
                s = jnp.where(col <= row, s, jnp.float32(-1e30))
            return s

        def fold(h, s):
            top = jnp.max(s, axis=1, keepdims=True)
            if first:
                new = jnp.broadcast_to(top, (rows, 128))
            else:
                old = peak[h]
                new = jnp.maximum(old, top)
            w = jnp.exp2(s - jnp.concatenate([new] * (rows // 128), axis=1))
            part = w[:, :128]
            for n in range(1, rows // 128):
                part = part + w[:, n * 128 : (n + 1) * 128]
            update = lax.dot_general(
                w.astype(jnp.bfloat16), latent, NT, preferred_element_type=jnp.float32
            )
            peak[h] = new
            if first:
                total[h] = part
                acc[h] = update
            else:
                shrink = jnp.exp2(old - new)
                total[h] = total[h] * shrink + part
                acc[h] = acc[h] * jnp.concatenate([shrink] * (LAT // 128), axis=1) + update

        s = scores(some[0])
        for h in some:
            ahead = scores(h + 1) if h < some[-1] else None
            fold(h, s)
            s = ahead

    own(1)
    attend(i, True, range(heads))

    def swapped(j, far, owner):
        @pl.when(jnp.logical_not(far))
        def _():
            for k in range(2):
                kv_arrived(j, 2 * (1 - core) + k)

        @pl.when(far & (core != owner))
        def _():
            for part in range(4):
                kv_arrived(j, part)

    def half_step(n, carry):
        d, k = div(n, 2) + 1, rem(n, 2)

        @pl.when(d <= 2)
        def _():
            relay_a(d, k)

        @pl.when(n == 1)
        def _():
            far_first(yl, 0)

        @pl.when(n == 4)
        def _():
            far_rest(yl, 0)

        def group(ab, carry):
            @pl.when((ab == 1) & (yl == 1))
            def _():
                relay_b(d - 1, k)

                @pl.when(n == 4)
                def _():
                    far_first(0, 1)

                @pl.when(n == 6)
                def _():
                    far_rest(0, 1)

            dd = d - 1 - ab
            j = (1 - ab) * (yl * NZ) + rem(z + dd * (2 * k - 1) + NZ, NZ)
            in_a = (ab == 0) & (((dd >= 1) & (dd <= 3)) | ((dd == 4) & (k == 0) & (yl == 1)))
            in_b = (ab == 1) & (yl == 1) & (((dd >= 1) & (dd <= 3)) | ((dd == 0) & (k == 0)))

            @pl.when((in_a | in_b) & (j < i))
            def _():
                swapped(j, dd >= 3, jnp.where(dd == 3, 1 - k, far_core[2]))
                attend(j, False, range(heads))

            return carry

        return lax.fori_loop(0, 2, group, carry)

    lax.fori_loop(0, 10, half_step, 0)
    last = rem(z + 4, NZ)

    def block(e):
        n, dy = rem(e, 4), div(e, 4)
        dx = n + div(n, 2) * (1 - 2 * rem(n, 2))
        return rem(x + dx, NX), rem(yh + dy, 2)

    def v_copy(e, k, send_sem, target):
        xx, yy = block(e)
        slot = outer_of(xx, yy, core)
        piece = vbuf.at[slot, k]
        return pltpu.make_async_remote_copy(
            src_ref=piece, dst_ref=piece, send_sem=send_sem,
            recv_sem=v_recv.at[slot, k], device_id=target, device_id_type=MESH,
        )

    def v_arrived(slot, k):
        piece = vbuf.at[slot, k]
        pltpu.make_async_remote_copy(
            src_ref=piece, dst_ref=piece, send_sem=send_c.at[0, 0],
            recv_sem=v_recv.at[slot, k], device_id=sibling, device_id_type=MESH,
        ).wait_recv()

    def own_slot(e):
        xx, yy = block(e)
        return outer_of(xx, yy, core)

    def sib_slot(e):
        xx, yy = block(e)
        return outer_of(xx, yy, 1 - core)

    locals_[7].wait()

    def send(e, k, way):
        sem = {
            "far": lambda: send_c.at[e, k], "up": lambda: send_x.at[e, k, 0],
            "down": lambda: send_x.at[e, k, 1], "sib": lambda: sib_v.at[e, k],
        }[way]()
        target = {"far": y_far, "up": x_up, "down": x_down, "sib": sibling}[way]
        return v_copy(e, k, sem, target)

    for k in range(2):
        pair = (2 * k, 2 * k + 1)

        @pl.when(last < i)
        def _():
            if k == 0:
                swapped(last, last >= 0, far_core[2])
            attend(last, False, pair)

        for h in pair:
            whole = jnp.sum(total[h], axis=1, keepdims=True)
            latent_out = (acc[h] * (1.0 / whole)).astype(jnp.bfloat16)
            vbuf[o, k, :, (h % 2) * VDIM : (h % 2 + 1) * VDIM] = jnp.dot(
                latent_out, vu[h], preferred_element_type=jnp.float32
            ).astype(jnp.bfloat16)
        for way in ("up", "down", "far", "sib"):
            send(0, k, way).start()

    locals_[8].wait()
    mix[...] = jnp.zeros_like(mix)

    def project(e):
        depth = heads * VDIM // 2
        term = mix[...]
        for slot in (own_slot(e), sib_slot(e)):
            for k in range(2):
                start = pl.multiple_of((slot * 2 + k) * depth, depth)
                term = term + lax.dot_general(
                    wo[:, pl.ds(start, depth)], vbuf[slot, k], NT,
                    preferred_element_type=jnp.float32,
                )
        mix[...] = term

    came = (
        ((1, 0, "far"), (2, 0, "up"), (4, 0, "up")),
        ((1, 1, "down", "far"), (2, 1), (4, 1, "up")),
        ((3, 0), (5, 0, "down"), (3, 1)),
        ((6, 0), (5, 1, "down")),
        ((6, 1),),
        ((7, 0),),
        ((7, 1),),
    )

    def event(t, carry):
        for n, items in enumerate(came):
            @pl.when(t == n)
            def _():
                for e, k, *ways in items:
                    v_arrived(own_slot(e), k)
                    for way in (*ways, "sib"):
                        send(e, k, way).start()

        for k in range(2):
            v_arrived(sib_slot(t), k)
        project(t)
        return carry

    lax.fori_loop(0, 8, event, 0)
    out_ref[...] = mix[...].astype(jnp.bfloat16)

    for k in range(2):
        for way in ("up", "down", "far", "sib"):
            send(0, k, way).wait_send()
    for items in came:
        for e, k, *ways in items:
            for way in (*ways, "sib"):
                send(e, k, way).wait_send()

    def drain(n, carry):
        d, k = div(n, 2), rem(n, 2)
        for side in range(2):
            @pl.when(d <= 1)
            def _():
                z_send(d, side, k).wait_send()

            @pl.when((yl == 0) & held_b(d, side))
            def _():
                y_send(d, side, k).wait_send()

            @pl.when((d >= 1) & (yl * NZ + ring(d, side) < i))
            def _():
                sib_a_send(d, side, k).wait_send()

            @pl.when((yl == 1) & held_b(d, side))
            def _():
                sib_b_send(d, side, k).wait_send()

        return carry

    lax.fori_loop(0, 6, drain, 0)

    for f in range(3):
        @pl.when(core == far_core[f])
        def _():
            far_z_send(f).wait_send()

            @pl.when(yl == 0)
            def _():
                far_y_send(f).wait_send()

            @pl.when(far_shard(f, yl) < i)
            def _():
                for copy in far_x_sends(f, yl, 0):
                    copy.wait_send()
                for n in range(NX):
                    far_sib_send(f, yl, 0, n).wait_send()

            @pl.when(yl == 1)
            def _():
                for copy in far_x_sends(f, 0, 1):
                    copy.wait_send()
                for n in range(NX):
                    far_sib_send(f, 0, 1, n).wait_send()


def on_device(q_nope, q_rope, absorb_key, kv_latent, value_up, out_proj):
    rows = q_nope.shape[0]
    heads = absorb_key.shape[0]
    columns = out_proj.shape[1]
    kv_parts = kv_latent.T.reshape(4, WIDE // 4, rows)
    out_proj = out_proj.T
    dma = pltpu.SemaphoreType.DMA
    mixed = pl.pallas_call(
        kernel,
        out_shape=jax.ShapeDtypeStruct((columns, rows), jnp.bfloat16),
        in_specs=[pl.BlockSpec(memory_space=pl.ANY)] * 6,
        out_specs=pl.BlockSpec(memory_space=pltpu.VMEM),
        scratch_shapes=[
            pltpu.VMEM(q_nope.shape, jnp.bfloat16),
            pltpu.VMEM(q_rope.shape, jnp.bfloat16),
            pltpu.VMEM(absorb_key.shape, jnp.bfloat16),
            pltpu.VMEM(value_up.shape, jnp.bfloat16),
            pltpu.VMEM(out_proj.shape, jnp.bfloat16),
            pltpu.VMEM((16, 4, WIDE // 4, rows), jnp.bfloat16),
            pltpu.VMEM((16, 2, rows, heads * VDIM // 2), jnp.bfloat16),
            pltpu.VMEM((heads, rows, WIDE), jnp.bfloat16),
            pltpu.VMEM((heads, rows, 128), jnp.float32),
            pltpu.VMEM((heads, rows, 128), jnp.float32),
            pltpu.VMEM((heads, rows, LAT), jnp.float32),
            pltpu.VMEM((columns, rows), jnp.float32),
            dma((9,)),
            dma((16, 4)),
            dma((2, 2, 2)),
            dma((2, 3, 2)),
            dma((2, 3, 2)),
            dma((2, 3, 2)),
            dma((3,)),
            dma((3,)),
            dma((2, 3, 3)),
            dma((2, 3, 4)),
            dma((16, 2)),
            dma((8, 2, 2)),
            dma((2, 2)),
            dma((8, 2)),
        ],
        compiler_params=pltpu.CompilerParams(
            collective_id=0, has_side_effects=True, vmem_limit_bytes=56 * 1024 * 1024
        ),
        cost_estimate=pl.CostEstimate(
            flops=12 * 10**9, bytes_accessed=10 * 10**6, transcendentals=4 * 10**6
        ),
    )(q_nope, q_rope, absorb_key, kv_parts, value_up, out_proj)
    return mixed.T


def solution(mesh):
    placed = (
        P("inner", "outer"),
        P("inner", "outer"),
        P("outer", None, None),
        P("inner", None),
        P("outer", None, None),
        P(None, "outer"),
    )
    return jax.shard_map(
        on_device, mesh=mesh, in_specs=placed, out_specs=P("inner", "outer"), check_vma=False
    )
```

```python
import math

import jax
import jax.numpy as jnp
from jax import lax
from jax.experimental import pallas as pl
from jax.experimental.pallas import tpu as pltpu
from jax.sharding import PartitionSpec as P

NOPE = 128
ROPE = 64
VDIM = 128
LAT = 512
WIDE = LAT + ROPE
MESH = pl.DeviceIdType.MESH
NT = (((1,), (1,)), ((), ()))
SCALE = math.log2(math.e) / math.sqrt(NOPE + ROPE)
NX, NZ = 4, 8


def div(a, b):
    return a // b if isinstance(a, int) else lax.div(a, b)


def rem(a, b):
    return a % b if isinstance(a, int) else lax.rem(a, b)


def kernel(
    qn_hbm, qr_hbm, ak_hbm, kv_hbm, vu_hbm, wo_hbm, out_ref,
    qn, qr, ak, vu, wo, kvbuf, vbuf, query, peak, total, acc, mix,
    local_sem, kv_recv, send_z, send_y, sib_a, sib_b, v_recv, send_x, send_c, sib_v,
):
    heads, rows = query.shape[0], query.shape[1]
    o, i = lax.axis_index("outer"), lax.axis_index("inner")
    core, yh, x = rem(o, 2), rem(div(o, 2), 2), div(o, 4)
    yl, z = div(i, NZ), rem(i, NZ)

    def outer_of(x_, yh_, core_):
        return (x_ * 2 + yh_) * 2 + core_

    sibling = (outer_of(x, yh, 1 - core), i)
    z_up = (o, yl * NZ + rem(z + 1, NZ))
    z_down = (o, yl * NZ + rem(z + NZ - 1, NZ))
    y_up = (outer_of(x, rem(yh + yl, 2), core), (1 - yl) * NZ + z)
    y_down = (outer_of(x, rem(yh + 1 - yl, 2), core), (1 - yl) * NZ + z)
    y_far = (outer_of(x, 1 - yh, core), i)
    x_up = (outer_of(rem(x + 1, NX), yh, core), i)
    x_down = (outer_of(rem(x + NX - 1, NX), yh, core), i)

    locals_ = [
        pltpu.make_async_copy(kv_hbm.at[part], kvbuf.at[i, part], local_sem.at[part])
        for part in range(4)
    ]
    for n, (src, dst) in enumerate(
        [(qn_hbm, qn), (ak_hbm, ak), (qr_hbm, qr), (vu_hbm, vu), (wo_hbm, wo)]
    ):
        locals_.append(pltpu.make_async_copy(src, dst, local_sem.at[4 + n]))
    for copy in locals_:
        copy.start()

    barrier = pltpu.get_barrier_semaphore()
    partners = (sibling, z_up, z_down, y_up, y_down, y_far, x_up, x_down)
    for partner in partners:
        pl.semaphore_signal(barrier, inc=1, device_id=partner, device_id_type=MESH)
    pl.semaphore_wait(barrier, len(partners))

    def kv_copy(j, k, send_sem, target):
        piece = kvbuf.at[j, 2 * core + k]
        return pltpu.make_async_remote_copy(
            src_ref=piece, dst_ref=piece, send_sem=send_sem,
            recv_sem=kv_recv.at[j, 2 * core + k], device_id=target, device_id_type=MESH,
        )

    def kv_arrived(j, part):
        piece = kvbuf.at[j, part]
        pltpu.make_async_remote_copy(
            src_ref=piece, dst_ref=piece, send_sem=send_z.at[0, 0, 0],
            recv_sem=kv_recv.at[j, part], device_id=sibling, device_id_type=MESH,
        ).wait_recv()

    def ring(d, side):
        return rem(z + (d if side else NZ - d), NZ)

    def z_forwards(d, side, k):
        return (d <= 2) | ((d == 3) & (k == side))

    def held_a(d, side, k):
        return (d <= 3) | ((d == 4) & (k == side))

    def held_b(d, side, k):
        return ((d == 0) & (side == 0)) | ((d >= 1) & (d <= 3)) | ((d == 4) & (k == side))

    def z_send(d, side, k):
        return kv_copy(yl * NZ + ring(d, side), k, send_z.at[side, d, k], (z_up, z_down)[side])

    def y_send(d, side, k):
        target = (outer_of(x, rem(yh + k, 2), core), NZ + z)
        return kv_copy(ring(d, side), k, send_y.at[side, d, k], target)

    def sib_a_send(d, side, k):
        return kv_copy(yl * NZ + ring(d, side), k, sib_a.at[side, d, k], sibling)

    def sib_b_send(d, side, k):
        return kv_copy(ring(d, side), k, sib_b.at[side, d, k], sibling)

    def relay_a(d, k):
        for side in range(2):
            j = yl * NZ + ring(d, side)

            @pl.when(held_a(d, side, k))
            def _():
                kv_arrived(j, 2 * core + k)

                @pl.when(z_forwards(d, side, k))
                def _():
                    z_send(d, side, k).start()

                @pl.when(yl == 0)
                def _():
                    y_send(d, side, k).start()

                @pl.when(j < i)
                def _():
                    sib_a_send(d, side, k).start()

    def relay_b(d, k):
        for side in range(2):
            @pl.when(held_b(d, side, k))
            def _():
                kv_arrived(ring(d, side), 2 * core + k)
                sib_b_send(d, side, k).start()

    for part in range(4):
        locals_[part].wait()

    def own(k):
        for side in range(2):
            z_send(0, side, k).start()

        @pl.when(yl == 0)
        def _():
            y_send(0, 0, k).start()

    own(0)

    locals_[4].wait()
    locals_[5].wait()
    locals_[6].wait()
    for h in range(heads):
        query[h, :, :LAT] = jnp.dot(
            qn[:, h * NOPE : (h + 1) * NOPE], ak[h], preferred_element_type=jnp.float32
        ).astype(jnp.bfloat16)
        query[h, :, LAT:] = qr[:, h * ROPE : (h + 1) * ROPE]

    def attend(j, first, some):
        keys = kvbuf[j].reshape(WIDE, rows)
        latent = keys[:LAT]

        def scores(h):
            s = jnp.dot(query[h], keys, preferred_element_type=jnp.float32) * SCALE
            if first:
                row = lax.broadcasted_iota(jnp.int32, s.shape, 0)
                col = lax.broadcasted_iota(jnp.int32, s.shape, 1)
                s = jnp.where(col <= row, s, jnp.float32(-1e30))
            return s

        def fold(h, s):
            top = jnp.max(s, axis=1, keepdims=True)
            if first:
                new = jnp.broadcast_to(top, (rows, 128))
            else:
                old = peak[h]
                new = jnp.maximum(old, top)
            w = jnp.exp2(s - jnp.concatenate([new] * (rows // 128), axis=1))
            part = w[:, :128]
            for n in range(1, rows // 128):
                part = part + w[:, n * 128 : (n + 1) * 128]
            update = lax.dot_general(
                w.astype(jnp.bfloat16), latent, NT, preferred_element_type=jnp.float32
            )
            peak[h] = new
            if first:
                total[h] = part
                acc[h] = update
            else:
                shrink = jnp.exp2(old - new)
                total[h] = total[h] * shrink + part
                acc[h] = acc[h] * jnp.concatenate([shrink] * (LAT // 128), axis=1) + update

        s = scores(some[0])
        for h in some:
            ahead = scores(h + 1) if h < some[-1] else None
            fold(h, s)
            s = ahead

    own(1)
    attend(i, True, range(heads))

    def swapped(j):
        for k in range(2):
            kv_arrived(j, 2 * (1 - core) + k)

    def half_step(n, carry):
        d, k = div(n, 2) + 1, rem(n, 2)

        @pl.when(d <= 4)
        def _():
            relay_a(d, k)

        def group(ab, carry):
            @pl.when((ab == 1) & (yl == 1))
            def _():
                relay_b(d - 1, k)

            dd = d - 1 - ab
            j = (1 - ab) * (yl * NZ) + rem(z + dd * (2 * k - 1) + NZ, NZ)
            in_a = (ab == 0) & (((dd >= 1) & (dd <= 3)) | ((dd == 4) & (k == 0) & (yl == 1)))
            in_b = (ab == 1) & (yl == 1) & (((dd >= 1) & (dd <= 3)) | ((dd == 0) & (k == 0)))

            @pl.when((in_a | in_b) & (j < i))
            def _():
                swapped(j)
                attend(j, False, range(heads))

            return carry

        return lax.fori_loop(0, 2, group, carry)

    lax.fori_loop(0, 10, half_step, 0)
    last = rem(z + 4, NZ)

    def block(e):
        n, dy = rem(e, 4), div(e, 4)
        dx = n + div(n, 2) * (1 - 2 * rem(n, 2))
        return rem(x + dx, NX), rem(yh + dy, 2)

    def v_copy(e, k, send_sem, target):
        xx, yy = block(e)
        slot = outer_of(xx, yy, core)
        piece = vbuf.at[slot, k]
        return pltpu.make_async_remote_copy(
            src_ref=piece, dst_ref=piece, send_sem=send_sem,
            recv_sem=v_recv.at[slot, k], device_id=target, device_id_type=MESH,
        )

    def v_arrived(slot, k):
        piece = vbuf.at[slot, k]
        pltpu.make_async_remote_copy(
            src_ref=piece, dst_ref=piece, send_sem=send_c.at[0, 0],
            recv_sem=v_recv.at[slot, k], device_id=sibling, device_id_type=MESH,
        ).wait_recv()

    def own_slot(e):
        xx, yy = block(e)
        return outer_of(xx, yy, core)

    def sib_slot(e):
        xx, yy = block(e)
        return outer_of(xx, yy, 1 - core)

    locals_[7].wait()

    def send(e, k, way):
        sem = {
            "far": lambda: send_c.at[e, k], "up": lambda: send_x.at[e, k, 0],
            "down": lambda: send_x.at[e, k, 1], "sib": lambda: sib_v.at[e, k],
        }[way]()
        target = {"far": y_far, "up": x_up, "down": x_down, "sib": sibling}[way]
        return v_copy(e, k, sem, target)

    for k in range(2):
        pair = (2 * k, 2 * k + 1)

        @pl.when(last < i)
        def _():
            if k == 0:
                swapped(last)
            attend(last, False, pair)

        for h in pair:
            whole = jnp.sum(total[h], axis=1, keepdims=True)
            latent_out = (acc[h] * (1.0 / whole)).astype(jnp.bfloat16)
            vbuf[o, k, :, (h % 2) * VDIM : (h % 2 + 1) * VDIM] = jnp.dot(
                latent_out, vu[h], preferred_element_type=jnp.float32
            ).astype(jnp.bfloat16)
        for way in ("up", "down", "far", "sib"):
            send(0, k, way).start()

    locals_[8].wait()
    mix[...] = jnp.zeros_like(mix)

    def project(e):
        depth = heads * VDIM // 2
        term = mix[...]
        for slot in (own_slot(e), sib_slot(e)):
            for k in range(2):
                start = pl.multiple_of((slot * 2 + k) * depth, depth)
                term = term + lax.dot_general(
                    wo[:, pl.ds(start, depth)], vbuf[slot, k], NT,
                    preferred_element_type=jnp.float32,
                )
        mix[...] = term

    came = (
        ((1, 0), (2, 0, "up")),
        ((1, 1, "down"), (2, 1)),
        ((4, 0, "up", "down"), (3, 0), (3, 1)),
        ((4, 1, "up", "down"),),
        ((5, 0), (6, 0, "up")),
        ((5, 1, "down"), (6, 1)),
        ((7, 0),),
        ((7, 1),),
    )

    def event(t, carry):
        for n, items in enumerate(came):
            @pl.when(t == n)
            def _():
                for e, k, *ways in items:
                    v_arrived(own_slot(e), k)
                    for way in (*ways, "sib"):
                        send(e, k, way).start()

        for k in range(2):
            v_arrived(sib_slot(t), k)
        project(t)
        return carry

    lax.fori_loop(0, 8, event, 0)
    out_ref[...] = mix[...].astype(jnp.bfloat16)

    for k in range(2):
        for way in ("up", "down", "far", "sib"):
            send(0, k, way).wait_send()
    for items in came:
        for e, k, *ways in items:
            for way in (*ways, "sib"):
                send(e, k, way).wait_send()

    def drain(n, carry):
        d, k = div(n, 2), rem(n, 2)
        for side in range(2):
            @pl.when(z_forwards(d, side, k))
            def _():
                z_send(d, side, k).wait_send()

            @pl.when((yl == 0) & held_b(d, side, k))
            def _():
                y_send(d, side, k).wait_send()

            @pl.when((d >= 1) & held_a(d, side, k) & (yl * NZ + ring(d, side) < i))
            def _():
                sib_a_send(d, side, k).wait_send()

            @pl.when((yl == 1) & held_b(d, side, k))
            def _():
                sib_b_send(d, side, k).wait_send()

        return carry

    lax.fori_loop(0, 10, drain, 0)


def on_device(q_nope, q_rope, absorb_key, kv_latent, value_up, out_proj):
    rows = q_nope.shape[0]
    heads = absorb_key.shape[0]
    columns = out_proj.shape[1]
    kv_parts = kv_latent.T.reshape(4, WIDE // 4, rows)
    out_proj = out_proj.T
    dma = pltpu.SemaphoreType.DMA
    mixed = pl.pallas_call(
        kernel,
        out_shape=jax.ShapeDtypeStruct((columns, rows), jnp.bfloat16),
        in_specs=[pl.BlockSpec(memory_space=pl.ANY)] * 6,
        out_specs=pl.BlockSpec(memory_space=pltpu.VMEM),
        scratch_shapes=[
            pltpu.VMEM(q_nope.shape, jnp.bfloat16),
            pltpu.VMEM(q_rope.shape, jnp.bfloat16),
            pltpu.VMEM(absorb_key.shape, jnp.bfloat16),
            pltpu.VMEM(value_up.shape, jnp.bfloat16),
            pltpu.VMEM(out_proj.shape, jnp.bfloat16),
            pltpu.VMEM((16, 4, WIDE // 4, rows), jnp.bfloat16),
            pltpu.VMEM((16, 2, rows, heads * VDIM // 2), jnp.bfloat16),
            pltpu.VMEM((heads, rows, WIDE), jnp.bfloat16),
            pltpu.VMEM((heads, rows, 128), jnp.float32),
            pltpu.VMEM((heads, rows, 128), jnp.float32),
            pltpu.VMEM((heads, rows, LAT), jnp.float32),
            pltpu.VMEM((columns, rows), jnp.float32),
            dma((9,)),
            dma((16, 4)),
            dma((2, 4, 2)),
            dma((2, 5, 2)),
            dma((2, 5, 2)),
            dma((2, 5, 2)),
            dma((16, 2)),
            dma((8, 2, 2)),
            dma((2, 2)),
            dma((8, 2)),
        ],
        compiler_params=pltpu.CompilerParams(
            collective_id=0, has_side_effects=True, vmem_limit_bytes=56 * 1024 * 1024
        ),
        cost_estimate=pl.CostEstimate(
            flops=12 * 10**9, bytes_accessed=10 * 10**6, transcendentals=4 * 10**6
        ),
    )(q_nope, q_rope, absorb_key, kv_parts, value_up, out_proj)
    return mixed.T


def solution(mesh):
    placed = (
        P("inner", "outer"),
        P("inner", "outer"),
        P("outer", None, None),
        P("inner", None),
        P("outer", None, None),
        P(None, "outer"),
    )
    return jax.shard_map(
        on_device, mesh=mesh, in_specs=placed, out_specs=P("inner", "outer"), check_vma=False
    )
```

```python
import math

import jax
import jax.numpy as jnp
from jax import lax
from jax.experimental import pallas as pl
from jax.experimental.pallas import tpu as pltpu
from jax.sharding import PartitionSpec as P

NOPE = 128
ROPE = 64
VDIM = 128
LAT = 512
WIDE = LAT + ROPE
MESH = pl.DeviceIdType.MESH
NT = (((1,), (1,)), ((), ()))
SCALE = math.log2(math.e) / math.sqrt(NOPE + ROPE)
NX, NZ = 4, 8


def div(a, b):
    return a // b if isinstance(a, int) else lax.div(a, b)


def rem(a, b):
    return a % b if isinstance(a, int) else lax.rem(a, b)


def kernel(
    qn_hbm, qr_hbm, ak_hbm, kv_hbm, vu_hbm, wo_hbm, out_ref,
    qn, qr, ak, vu, wo, kvbuf, vbuf, query, peak, total, acc, mix,
    local_sem, kv_recv, send_z, send_y, sib_a, sib_b, v_recv, send_x, send_c, sib_v,
):
    heads, rows = ak.shape[0], qn.shape[0]
    o, i = lax.axis_index("outer"), lax.axis_index("inner")
    core, yh, x = rem(o, 2), rem(div(o, 2), 2), div(o, 4)
    yl, z = div(i, NZ), rem(i, NZ)

    def outer_of(x_, yh_, core_):
        return (x_ * 2 + yh_) * 2 + core_

    sibling = (outer_of(x, yh, 1 - core), i)
    z_up = (o, yl * NZ + rem(z + 1, NZ))
    z_down = (o, yl * NZ + rem(z + NZ - 1, NZ))
    y_up = (outer_of(x, rem(yh + yl, 2), core), (1 - yl) * NZ + z)
    y_down = (outer_of(x, rem(yh + 1 - yl, 2), core), (1 - yl) * NZ + z)
    y_far = (outer_of(x, 1 - yh, core), i)
    x_up = (outer_of(rem(x + 1, NX), yh, core), i)
    x_down = (outer_of(rem(x + NX - 1, NX), yh, core), i)

    locals_ = [
        pltpu.make_async_copy(kv_hbm.at[part], kvbuf.at[i, part], local_sem.at[part])
        for part in range(4)
    ]
    for n, (src, dst) in enumerate(
        [(qn_hbm, qn), (ak_hbm, ak), (qr_hbm, qr), (vu_hbm, vu), (wo_hbm, wo)]
    ):
        locals_.append(pltpu.make_async_copy(src, dst, local_sem.at[4 + n]))
    for copy in locals_:
        copy.start()

    barrier = pltpu.get_barrier_semaphore()
    partners = (sibling, z_up, z_down, y_up, y_down, y_far, x_up, x_down)
    for partner in partners:
        pl.semaphore_signal(barrier, inc=1, device_id=partner, device_id_type=MESH)
    pl.semaphore_wait(barrier, len(partners))

    def kv_copy(j, k, send_sem, target):
        piece = kvbuf.at[j, 2 * core + k]
        return pltpu.make_async_remote_copy(
            src_ref=piece, dst_ref=piece, send_sem=send_sem,
            recv_sem=kv_recv.at[j, 2 * core + k], device_id=target, device_id_type=MESH,
        )

    def kv_arrived(j, part):
        piece = kvbuf.at[j, part]
        pltpu.make_async_remote_copy(
            src_ref=piece, dst_ref=piece, send_sem=send_z.at[0, 0, 0],
            recv_sem=kv_recv.at[j, part], device_id=sibling, device_id_type=MESH,
        ).wait_recv()

    def ring(d, side):
        return rem(z + (d if side else NZ - d), NZ)

    def z_forwards(d, side, k):
        return (d <= 2) | ((d == 3) & (k == side))

    def held_a(d, side, k):
        return (d <= 3) | ((d == 4) & (k == side))

    def held_b(d, side, k):
        return ((d == 0) & (side == 0)) | ((d >= 1) & (d <= 3)) | ((d == 4) & (k == side))

    def z_send(d, side, k):
        return kv_copy(yl * NZ + ring(d, side), k, send_z.at[side, d, k], (z_up, z_down)[side])

    def y_send(d, side, k):
        target = (outer_of(x, rem(yh + k, 2), core), NZ + z)
        return kv_copy(ring(d, side), k, send_y.at[side, d, k], target)

    def sib_a_send(d, side, k):
        return kv_copy(yl * NZ + ring(d, side), k, sib_a.at[side, d, k], sibling)

    def sib_b_send(d, side, k):
        return kv_copy(ring(d, side), k, sib_b.at[side, d, k], sibling)

    def relay_a(d, k):
        for side in range(2):
            j = yl * NZ + ring(d, side)

            @pl.when(held_a(d, side, k))
            def _():
                kv_arrived(j, 2 * core + k)

                @pl.when(z_forwards(d, side, k))
                def _():
                    z_send(d, side, k).start()

                @pl.when(yl == 0)
                def _():
                    y_send(d, side, k).start()

                @pl.when(j < i)
                def _():
                    sib_a_send(d, side, k).start()

    def relay_b(d, k):
        for side in range(2):
            @pl.when(held_b(d, side, k))
            def _():
                kv_arrived(ring(d, side), 2 * core + k)
                sib_b_send(d, side, k).start()

    for part in range(4):
        locals_[part].wait()

    def own(k):
        for side in range(2):
            z_send(0, side, k).start()

        @pl.when(yl == 0)
        def _():
            y_send(0, 0, k).start()

    own(0)

    locals_[4].wait()
    locals_[5].wait()
    locals_[6].wait()
    for h in range(heads):
        query[h * rows : (h + 1) * rows, :LAT] = jnp.dot(
            qn[:, h * NOPE : (h + 1) * NOPE], ak[h], preferred_element_type=jnp.float32
        ).astype(jnp.bfloat16)
        query[h * rows : (h + 1) * rows, LAT:] = qr[:, h * ROPE : (h + 1) * ROPE]

    def attend(j, first, pairs):
        keys = kvbuf[j].reshape(WIDE, rows)
        latent = keys[:LAT].T

        def scores(pair):
            own_rows = query[pair * 2 * rows : (pair + 1) * 2 * rows]
            s = jnp.dot(own_rows, keys, preferred_element_type=jnp.float32) * SCALE
            if first:
                row = rem(lax.broadcasted_iota(jnp.int32, s.shape, 0), rows)
                col = lax.broadcasted_iota(jnp.int32, s.shape, 1)
                s = jnp.where(col <= row, s, jnp.float32(-1e30))
            return s

        def fold(pair, s):
            at = slice(pair * 2 * rows, (pair + 1) * 2 * rows)
            top = jnp.max(s, axis=1, keepdims=True)
            if first:
                new = jnp.broadcast_to(top, (2 * rows, 128))
            else:
                old = peak[at]
                new = jnp.maximum(old, top)
            w = jnp.exp2(s - jnp.concatenate([new] * (rows // 128), axis=1))
            part = w[:, :128]
            for n in range(1, rows // 128):
                part = part + w[:, n * 128 : (n + 1) * 128]
            update = jnp.dot(w.astype(jnp.bfloat16), latent, preferred_element_type=jnp.float32)
            peak[at] = new
            if first:
                total[at] = part
                acc[at] = update
            else:
                shrink = jnp.exp2(old - new)
                total[at] = total[at] * shrink + part
                acc[at] = acc[at] * jnp.concatenate([shrink] * (LAT // 128), axis=1) + update

        s = [scores(pair) for pair in pairs]
        for pair, pair_scores in zip(pairs, s):
            fold(pair, pair_scores)

    own(1)
    attend(i, True, (0, 1))

    def swapped(j):
        for k in range(2):
            kv_arrived(j, 2 * (1 - core) + k)

    def half_step(n, carry):
        d, k = div(n, 2) + 1, rem(n, 2)

        @pl.when(d <= 4)
        def _():
            relay_a(d, k)

        def group(ab, carry):
            @pl.when((ab == 1) & (yl == 1))
            def _():
                relay_b(d - 1, k)

            dd = d - 1 - ab
            j = (1 - ab) * (yl * NZ) + rem(z + dd * (2 * k - 1) + NZ, NZ)
            in_a = (ab == 0) & (((dd >= 1) & (dd <= 3)) | ((dd == 4) & (k == 0) & (yl == 1)))
            in_b = (ab == 1) & (yl == 1) & (((dd >= 1) & (dd <= 3)) | ((dd == 0) & (k == 0)))

            @pl.when((in_a | in_b) & (j < i))
            def _():
                swapped(j)
                attend(j, False, (0, 1))

            return carry

        return lax.fori_loop(0, 2, group, carry)

    lax.fori_loop(0, 10, half_step, 0)
    last = rem(z + 4, NZ)

    def block(e):
        n, dy = rem(e, 4), div(e, 4)
        dx = n + div(n, 2) * (1 - 2 * rem(n, 2))
        return rem(x + dx, NX), rem(yh + dy, 2)

    def v_copy(e, k, send_sem, target):
        xx, yy = block(e)
        slot = outer_of(xx, yy, core)
        piece = vbuf.at[slot, k]
        return pltpu.make_async_remote_copy(
            src_ref=piece, dst_ref=piece, send_sem=send_sem,
            recv_sem=v_recv.at[slot, k], device_id=target, device_id_type=MESH,
        )

    def v_arrived(slot, k):
        piece = vbuf.at[slot, k]
        pltpu.make_async_remote_copy(
            src_ref=piece, dst_ref=piece, send_sem=send_c.at[0, 0],
            recv_sem=v_recv.at[slot, k], device_id=sibling, device_id_type=MESH,
        ).wait_recv()

    def own_slot(e):
        xx, yy = block(e)
        return outer_of(xx, yy, core)

    def sib_slot(e):
        xx, yy = block(e)
        return outer_of(xx, yy, 1 - core)

    locals_[7].wait()

    def send(e, k, way):
        sem = {
            "far": lambda: send_c.at[e, k], "up": lambda: send_x.at[e, k, 0],
            "down": lambda: send_x.at[e, k, 1], "sib": lambda: sib_v.at[e, k],
        }[way]()
        target = {"far": y_far, "up": x_up, "down": x_down, "sib": sibling}[way]
        return v_copy(e, k, sem, target)

    for k in range(2):
        pair = (2 * k, 2 * k + 1)

        @pl.when(last < i)
        def _():
            if k == 0:
                swapped(last)
            attend(last, False, (k,))

        for h in pair:
            at = slice(h * rows, (h + 1) * rows)
            whole = jnp.sum(total[at], axis=1, keepdims=True)
            latent_out = (acc[at] * (1.0 / whole)).astype(jnp.bfloat16)
            vbuf[o, k, :, (h % 2) * VDIM : (h % 2 + 1) * VDIM] = jnp.dot(
                latent_out, vu[h], preferred_element_type=jnp.float32
            ).astype(jnp.bfloat16)
        for way in ("up", "down", "far", "sib"):
            send(0, k, way).start()

    mix[...] = jnp.zeros_like(mix)

    def project(e):
        depth = heads * VDIM // 2
        term = mix[...]
        for slot in (own_slot(e), sib_slot(e)):
            for k in range(2):
                start = pl.multiple_of((slot * 2 + k) * depth, depth)
                term = term + lax.dot_general(
                    wo[:, pl.ds(start, depth)], vbuf[slot, k], NT,
                    preferred_element_type=jnp.float32,
                )
        mix[...] = term

    came = (
        ((1, 0, "far"), (2, 0, "up"), (4, 0, "up")),
        ((1, 1, "down", "far"), (2, 1), (4, 1, "up")),
        ((3, 0), (5, 0, "down"), (3, 1)),
        ((6, 0), (5, 1, "down")),
        ((6, 1),),
        ((7, 0),),
        ((7, 1),),
    )

    def event(t, carry):
        for n, items in enumerate(came):
            @pl.when(t == n)
            def _():
                for e, k, *ways in items:
                    v_arrived(own_slot(e), k)
                    for way in (*ways, "sib"):
                        send(e, k, way).start()

        @pl.when(t == 0)
        def _():
            locals_[8].wait()

        for k in range(2):
            v_arrived(sib_slot(t), k)
        project(t)
        return carry

    lax.fori_loop(0, 8, event, 0)
    out_ref[...] = mix[...].astype(jnp.bfloat16)

    for k in range(2):
        for way in ("up", "down", "far", "sib"):
            send(0, k, way).wait_send()
    for items in came:
        for e, k, *ways in items:
            for way in (*ways, "sib"):
                send(e, k, way).wait_send()

    def drain(n, carry):
        d, k = div(n, 2), rem(n, 2)
        for side in range(2):
            @pl.when(z_forwards(d, side, k))
            def _():
                z_send(d, side, k).wait_send()

            @pl.when((yl == 0) & held_b(d, side, k))
            def _():
                y_send(d, side, k).wait_send()

            @pl.when((d >= 1) & held_a(d, side, k) & (yl * NZ + ring(d, side) < i))
            def _():
                sib_a_send(d, side, k).wait_send()

            @pl.when((yl == 1) & held_b(d, side, k))
            def _():
                sib_b_send(d, side, k).wait_send()

        return carry

    lax.fori_loop(0, 10, drain, 0)


def on_device(q_nope, q_rope, absorb_key, kv_latent, value_up, out_proj):
    rows = q_nope.shape[0]
    heads = absorb_key.shape[0]
    columns = out_proj.shape[1]
    kv_parts = kv_latent.T.reshape(4, WIDE // 4, rows)
    out_proj = out_proj.T
    dma = pltpu.SemaphoreType.DMA
    mixed = pl.pallas_call(
        kernel,
        out_shape=jax.ShapeDtypeStruct((columns, rows), jnp.bfloat16),
        in_specs=[pl.BlockSpec(memory_space=pl.ANY)] * 6,
        out_specs=pl.BlockSpec(memory_space=pltpu.VMEM),
        scratch_shapes=[
            pltpu.VMEM(q_nope.shape, jnp.bfloat16),
            pltpu.VMEM(q_rope.shape, jnp.bfloat16),
            pltpu.VMEM(absorb_key.shape, jnp.bfloat16),
            pltpu.VMEM(value_up.shape, jnp.bfloat16),
            pltpu.VMEM(out_proj.shape, jnp.bfloat16),
            pltpu.VMEM((16, 4, WIDE // 4, rows), jnp.bfloat16),
            pltpu.VMEM((16, 2, rows, heads * VDIM // 2), jnp.bfloat16),
            pltpu.VMEM((heads * rows, WIDE), jnp.bfloat16),
            pltpu.VMEM((heads * rows, 128), jnp.float32),
            pltpu.VMEM((heads * rows, 128), jnp.float32),
            pltpu.VMEM((heads * rows, LAT), jnp.float32),
            pltpu.VMEM((columns, rows), jnp.float32),
            dma((9,)),
            dma((16, 4)),
            dma((2, 4, 2)),
            dma((2, 5, 2)),
            dma((2, 5, 2)),
            dma((2, 5, 2)),
            dma((16, 2)),
            dma((8, 2, 2)),
            dma((2, 2)),
            dma((8, 2)),
        ],
        compiler_params=pltpu.CompilerParams(
            collective_id=0, has_side_effects=True, vmem_limit_bytes=56 * 1024 * 1024
        ),
        cost_estimate=pl.CostEstimate(
            flops=12 * 10**9, bytes_accessed=10 * 10**6, transcendentals=4 * 10**6
        ),
    )(q_nope, q_rope, absorb_key, kv_parts, value_up, out_proj)
    return mixed.T


def solution(mesh):
    placed = (
        P("inner", "outer"),
        P("inner", "outer"),
        P("outer", None, None),
        P("inner", None),
        P("outer", None, None),
        P(None, "outer"),
    )
    return jax.shard_map(
        on_device, mesh=mesh, in_specs=placed, out_specs=P("inner", "outer"), check_vma=False
    )
```

```python
import math

import jax
import jax.numpy as jnp
from jax import lax
from jax.experimental import pallas as pl
from jax.experimental.pallas import tpu as pltpu
from jax.sharding import PartitionSpec as P

NOPE = 128
ROPE = 64
VDIM = 128
LAT = 512
WIDE = LAT + ROPE
MESH = pl.DeviceIdType.MESH
NT = (((1,), (1,)), ((), ()))
SCALE = math.log2(math.e) / math.sqrt(NOPE + ROPE)
NX, NZ = 4, 8


def div(a, b):
    return a // b if isinstance(a, int) else lax.div(a, b)


def rem(a, b):
    return a % b if isinstance(a, int) else lax.rem(a, b)


def kernel(
    qn_hbm, qr_hbm, ak_hbm, kv_hbm, vu_hbm, wo_hbm, out_ref,
    qn, qr, ak, vu, wo, kvbuf, vbuf, query, peak, total, acc, mix, out_away, out_here,
    local_sem, q_sem, kv_recv, send_z, send_y, sib_a, sib_b, v_recv, send_x, send_c, sib_v, out_sem,
):
    heads, rows = ak.shape[0], qn.shape[1]
    span = 2 * rows
    o, i = lax.axis_index("outer"), lax.axis_index("inner")
    core, yh, x = rem(o, 2), rem(div(o, 2), 2), div(o, 4)
    yl, z = div(i, NZ), rem(i, NZ)

    def outer_of(x_, yh_, core_):
        return (x_ * 2 + yh_) * 2 + core_

    sibling = (outer_of(x, yh, 1 - core), i)
    z_up = (o, yl * NZ + rem(z + 1, NZ))
    z_down = (o, yl * NZ + rem(z + NZ - 1, NZ))
    y_up = (outer_of(x, rem(yh + yl, 2), core), (1 - yl) * NZ + z)
    y_down = (outer_of(x, rem(yh + 1 - yl, 2), core), (1 - yl) * NZ + z)
    y_far = (outer_of(x, 1 - yh, core), i)
    x_up = (outer_of(rem(x + 1, NX), yh, core), i)
    x_down = (outer_of(rem(x + NX - 1, NX), yh, core), i)
    partner = (o, (1 - yl) * NZ + z)

    locals_ = [
        pltpu.make_async_copy(src, dst, local_sem.at[n])
        for n, (src, dst) in enumerate(
            [
                (kv_hbm, kvbuf.at[i]), (qn_hbm.at[yl], qn.at[yl]), (qr_hbm.at[yl], qr.at[yl]),
                (ak_hbm, ak), (vu_hbm, vu), (wo_hbm, wo),
            ]
        )
    ]
    for copy in locals_:
        copy.start()
    peak[...] = jnp.full_like(peak, -1e30)
    total[...] = jnp.zeros_like(total)
    acc[...] = jnp.zeros_like(acc)
    mix[...] = jnp.zeros_like(mix)

    barrier = pltpu.get_barrier_semaphore()
    others = (sibling, z_up, z_down, y_up, y_down, y_far, x_up, x_down)
    for other in others:
        pl.semaphore_signal(barrier, inc=1, device_id=other, device_id_type=MESH)
    pl.semaphore_wait(barrier, len(others))

    def remote(src, dst, send_sem, recv_sem, target):
        return pltpu.make_async_remote_copy(
            src_ref=src, dst_ref=dst, send_sem=send_sem, recv_sem=recv_sem,
            device_id=target, device_id_type=MESH,
        )

    q_swap = [
        remote(src.at[1 - yl], dst.at[yl], q_sem.at[n, 0], q_sem.at[n, 1], partner)
        for n, (src, dst) in enumerate([(qn_hbm, qn), (qr_hbm, qr)])
    ]

    def kv_copy(j, k, send_sem, target):
        piece = kvbuf.at[j, 2 * core + k]
        return remote(piece, piece, send_sem, kv_recv.at[j, 2 * core + k], target)

    def kv_arrived(j, part):
        piece = kvbuf.at[j, part]
        remote(piece, piece, send_z.at[0, 0, 0], kv_recv.at[j, part], sibling).wait_recv()

    def ring(d, side):
        return rem(z + (d if side else NZ - d), NZ)

    def z_forwards(d, side, k):
        return (d <= 2) | ((d == 3) & (k == side))

    def held_a(d, side, k):
        return (d <= 3) | ((d == 4) & (k == side))

    def held_b(d, side, k):
        return ((d == 0) & (side == 0)) | ((d >= 1) & (d <= 3)) | ((d == 4) & (k == side))

    def need_a(zz):
        return (yl == 0) | (zz <= z)

    def need_b(zz):
        return (yl == 1) | (zz <= z)

    def z_send(d, side, k):
        return kv_copy(yl * NZ + ring(d, side), k, send_z.at[side, d, k], (z_up, z_down)[side])

    def y_send(d, side, k):
        yh_there = rem(yh + yl + k * (1 - 2 * yl) + 2, 2)
        target = (outer_of(x, yh_there, core), (1 - yl) * NZ + z)
        return kv_copy(yl * NZ + ring(d, side), k, send_y.at[side, d, k], target)

    def sib_a_send(d, side, k):
        return kv_copy(yl * NZ + ring(d, side), k, sib_a.at[side, d, k], sibling)

    def sib_b_send(d, side, k):
        return kv_copy((1 - yl) * NZ + ring(d, side), k, sib_b.at[side, d, k], sibling)

    def relay_a(d, k):
        for side in range(2):
            zz = ring(d, side)

            @pl.when(held_a(d, side, k))
            def _():
                kv_arrived(yl * NZ + zz, 2 * core + k)

                @pl.when(z_forwards(d, side, k))
                def _():
                    z_send(d, side, k).start()

                @pl.when(need_a(zz))
                def _():
                    y_send(d, side, k).start()
                    sib_a_send(d, side, k).start()

    def relay_b(d, k):
        for side in range(2):
            zz = ring(d, side)

            @pl.when(held_b(d, side, k) & need_b(zz))
            def _():
                kv_arrived((1 - yl) * NZ + zz, 2 * core + k)
                sib_b_send(d, side, k).start()

    def own(k):
        for side in range(2):
            z_send(0, side, k).start()
        y_send(0, 0, k).start()

    locals_[0].wait()
    own(0)
    for copy in q_swap:
        copy.start()

    def absorb(g):
        for h in range(heads):
            query[g, h * rows : (h + 1) * rows, :LAT] = jnp.dot(
                qn[g, :, h * NOPE : (h + 1) * NOPE], ak[h], preferred_element_type=jnp.float32
            ).astype(jnp.bfloat16)
            query[g, h * rows : (h + 1) * rows, LAT:] = qr[g, :, h * ROPE : (h + 1) * ROPE]

    def attend(j, g, masked):
        keys = kvbuf[j].reshape(WIDE, span)
        latent = keys[:LAT].T
        half = heads // 2 * rows

        def scores(pair):
            own_rows = query[g, pair * half : (pair + 1) * half]
            s = jnp.dot(own_rows, keys, preferred_element_type=jnp.float32) * SCALE
            if masked:
                row = rem(lax.broadcasted_iota(jnp.int32, s.shape, 0), rows) + yl * rows
                col = lax.broadcasted_iota(jnp.int32, s.shape, 1)
                s = jnp.where(col <= row, s, jnp.float32(-1e30))
            return s

        def fold(pair, s):
            at = slice(pair * half, (pair + 1) * half)
            old = peak[g, at]
            new = jnp.maximum(old, jnp.max(s, axis=1, keepdims=True))
            shrink = jnp.exp2(old - new)
            w = jnp.exp2(s - jnp.concatenate([new] * (span // 128), axis=1))
            part = w[:, :128]
            for n in range(1, span // 128):
                part = part + w[:, n * 128 : (n + 1) * 128]
            update = jnp.dot(w.astype(jnp.bfloat16), latent, preferred_element_type=jnp.float32)
            peak[g, at] = new
            total[g, at] = total[g, at] * shrink + part
            acc[g, at] = acc[g, at] * jnp.concatenate([shrink] * (LAT // 128), axis=1) + update

        s = [scores(0), scores(1)]
        for pair in range(2):
            fold(pair, s[pair])

    locals_[1].wait()
    locals_[2].wait()
    locals_[3].wait()
    absorb(yl)
    own(1)
    locals_[4].wait()

    def block(e):
        n, dy = rem(e, 4), div(e, 4)
        dx = n + div(n, 2) * (1 - 2 * rem(n, 2))
        return rem(x + dx, NX), rem(yh + dy, 2)

    def own_slot(e):
        xx, yy = block(e)
        return outer_of(xx, yy, core)

    def sib_slot(e):
        xx, yy = block(e)
        return outer_of(xx, yy, 1 - core)

    def v_arrived(slot, g):
        piece = vbuf.at[slot, g]
        remote(piece, piece, send_c.at[0, 0], v_recv.at[slot, g], sibling).wait_recv()

    def send(e, g, way):
        sem = {
            "far": lambda: send_c.at[e, g], "up": lambda: send_x.at[e, g, 0],
            "down": lambda: send_x.at[e, g, 1], "sib": lambda: sib_v.at[e, g],
        }[way]()
        target = {"far": y_far, "up": x_up, "down": x_down, "sib": sibling}[way]
        slot = own_slot(e)
        piece = vbuf.at[slot, g]
        return remote(piece, piece, sem, v_recv.at[slot, g], target)

    came = (((1, "far"), (2,), (4, "up")), ((3,), (5, "down"), (6,)), ((7,),))

    def relay_v(g, items):
        for e, *ways in items:
            v_arrived(own_slot(e), g)
            if e == 1:
                @pl.when(core == 1)
                def _():
                    send(1, g, "down").start()
            if e == 2:
                @pl.when(core == 0)
                def _():
                    send(2, g, "up").start()
            for way in (*ways, "sib"):
                send(e, g, way).start()

    def finish(g):
        for h in range(heads):
            at = slice(h * rows, (h + 1) * rows)
            whole = jnp.sum(total[g, at], axis=1, keepdims=True)
            latent_out = (acc[g, at] * (1.0 / whole)).astype(jnp.bfloat16)
            vbuf[o, g, :, h * VDIM : (h + 1) * VDIM] = jnp.dot(
                latent_out, vu[h], preferred_element_type=jnp.float32
            ).astype(jnp.bfloat16)
        for way in ("up", "down", "far", "sib"):
            send(0, g, way).start()

    def project(g, e):
        depth = heads * VDIM
        term = mix[g]
        for slot in (own_slot(e), sib_slot(e)):
            start = pl.multiple_of(slot * depth, depth)
            term = term + lax.dot_general(
                wo[:, pl.ds(start, depth)], vbuf[slot, g], NT, preferred_element_type=jnp.float32
            )
        mix[g] = term

    out_swap = remote(out_away, out_here, out_sem.at[0], out_sem.at[1], partner)

    def deliver(g):
        @pl.when(g == yl)
        def _():
            out_ref[:, pl.ds(pl.multiple_of(yl * rows, rows), rows)] = mix[g].astype(jnp.bfloat16)

        @pl.when(g != yl)
        def _():
            out_away[...] = mix[g].astype(jnp.bfloat16)
            out_swap.start()

    far_hop = jnp.minimum(z, 4)
    early_step, late_step = 2 * far_hop + 2 * yl, 10

    def step_of(g):
        return (1 - g) * early_step + g * late_step

    def values_step(g, n):
        since = n - step_of(g)
        for stage, items in enumerate(came):
            @pl.when(since == 2 + 2 * stage)
            def _():
                relay_v(g, items)

    def project_step(g, n):
        since = n - step_of(g)
        stage = div(since - 3 + 16, 2) - 8
        active = (since >= 3) & (since <= 7) & (rem(since + 16, 2) == 1)

        @pl.when(active)
        def _():
            def one(e, carry):
                v_arrived(sib_slot(e), g)
                project(g, e)
                return carry

            first = 3 * jnp.minimum(stage, 1) + 4 * (stage - jnp.minimum(stage, 1))
            count = 3 + jnp.minimum(stage, 1) - 3 * (stage - jnp.minimum(stage, 1))
            lax.fori_loop(first, first + count, one, 0)

        @pl.when(since == 8)
        def _():
            deliver(g)

    def step(n, carry):
        d, k = div(n, 2) + 1, rem(n, 2)

        @pl.when(d <= 4)
        def _():
            relay_a(d, k)

        def values_of(g, carry):
            values_step(g, n)
            return carry

        lax.fori_loop(0, 2, values_of, 0)

        @pl.when(n == 2)
        def _():
            for copy in q_swap:
                copy.wait_recv()
            absorb(1 - yl)
            locals_[5].wait()

        def source(ab, carry):
            dd = d - 1 - rem(ab, 2)
            key_group = yl + rem(ab, 2) * (1 - 2 * yl)
            zz = rem(z + dd * (2 * k - 1) + NZ, NZ)
            zz = jnp.where(ab == 2, z, zz)
            j = key_group * NZ + zz
            middle = (dd >= 1) & (dd <= 3)
            in_a = (ab == 0) & (middle | ((dd == 4) & (k == 0)))
            in_b = (ab == 1) & (middle | (((dd == 0) | (dd == 4)) & (k == 0)))
            in_own = (ab == 2) & (n == 2)

            @pl.when((in_a & need_a(zz)) | (in_b & need_b(zz)))
            def _():
                for part in range(2):
                    kv_arrived(j, 2 * (1 - core) + part)

            @pl.when((ab <= 1) & (dd == 0) & (k == 0))
            def _():
                attend(j, key_group, True)

            def group(g, carry):
                below = (key_group == 0) & (g == 1)

                @pl.when((in_a | in_b | in_own) & (below | ((zz < z) & (g >= key_group))))
                def _():
                    attend(j, g, False)

                @pl.when((n == step_of(g)) & (ab == jnp.maximum(g, yl)))
                def _():
                    finish(g)

                return carry

            lax.fori_loop(0, 2, group, 0)

            @pl.when((ab == 1) & (d <= 5))
            def _():
                relay_b(d - 1, k)

            return carry

        lax.fori_loop(0, 3, source, 0)

        def project_of(g, carry):
            project_step(g, n)
            return carry

        lax.fori_loop(0, 2, project_of, 0)
        return carry

    lax.fori_loop(0, late_step + 9, step, 0)

    out_swap.wait_recv()
    out_ref[:, pl.ds(pl.multiple_of((1 - yl) * rows, rows), rows)] = out_here[...]

    out_swap.wait_send()
    for copy in q_swap:
        copy.wait_send()

    def drain_v(g, carry):
        for way in ("up", "down", "far", "sib"):
            send(0, g, way).wait_send()
        for items in came:
            for e, *ways in items:
                if e == 1:
                    @pl.when(core == 1)
                    def _():
                        send(1, g, "down").wait_send()
                if e == 2:
                    @pl.when(core == 0)
                    def _():
                        send(2, g, "up").wait_send()
                for way in (*ways, "sib"):
                    send(e, g, way).wait_send()
        return carry

    lax.fori_loop(0, 2, drain_v, 0)

    def drain(n, carry):
        d, k = div(n, 2), rem(n, 2)
        for side in range(2):
            zz = ring(d, side)

            @pl.when(z_forwards(d, side, k))
            def _():
                z_send(d, side, k).wait_send()

            @pl.when(held_b(d, side, k) & need_a(zz))
            def _():
                y_send(d, side, k).wait_send()

            @pl.when((d >= 1) & held_a(d, side, k) & need_a(zz))
            def _():
                sib_a_send(d, side, k).wait_send()

            @pl.when(held_b(d, side, k) & need_b(zz))
            def _():
                sib_b_send(d, side, k).wait_send()

        return carry

    lax.fori_loop(0, 10, drain, 0)


def on_device(q_nope, q_rope, absorb_key, kv_latent, value_up, out_proj):
    rows = q_nope.shape[0]
    half = rows // 2
    heads = absorb_key.shape[0]
    columns = out_proj.shape[1]
    kv_parts = kv_latent.T.reshape(4, WIDE // 4, rows)
    out_proj = out_proj.T
    q_nope = q_nope.reshape(2, half, heads * NOPE)
    q_rope = q_rope.reshape(2, half, heads * ROPE)
    dma = pltpu.SemaphoreType.DMA
    bf16, f32 = jnp.bfloat16, jnp.float32
    mixed = pl.pallas_call(
        kernel,
        out_shape=jax.ShapeDtypeStruct((columns, rows), bf16),
        in_specs=[pl.BlockSpec(memory_space=pl.ANY)] * 6,
        out_specs=pl.BlockSpec(memory_space=pltpu.VMEM),
        scratch_shapes=[
            pltpu.VMEM(q_nope.shape, bf16),
            pltpu.VMEM(q_rope.shape, bf16),
            pltpu.VMEM(absorb_key.shape, bf16),
            pltpu.VMEM(value_up.shape, bf16),
            pltpu.VMEM(out_proj.shape, bf16),
            pltpu.VMEM((16, 4, WIDE // 4, rows), bf16),
            pltpu.VMEM((16, 2, half, heads * VDIM), bf16),
            pltpu.VMEM((2, heads * half, WIDE), bf16),
            pltpu.VMEM((2, heads * half, 128), f32),
            pltpu.VMEM((2, heads * half, 128), f32),
            pltpu.VMEM((2, heads * half, LAT), f32),
            pltpu.VMEM((2, columns, half), f32),
            pltpu.VMEM((columns, half), bf16),
            pltpu.VMEM((columns, half), bf16),
            dma((6,)),
            dma((2, 2)),
            dma((16, 4)),
            dma((2, 4, 2)),
            dma((2, 5, 2)),
            dma((2, 5, 2)),
            dma((2, 5, 2)),
            dma((16, 2)),
            dma((8, 2, 2)),
            dma((2, 2)),
            dma((8, 2)),
            dma((2,)),
        ],
        compiler_params=pltpu.CompilerParams(
            collective_id=0, has_side_effects=True, vmem_limit_bytes=56 * 1024 * 1024
        ),
        cost_estimate=pl.CostEstimate(
            flops=12 * 10**9, bytes_accessed=10 * 10**6, transcendentals=4 * 10**6
        ),
    )(q_nope, q_rope, absorb_key, kv_parts, value_up, out_proj)
    return mixed.T


def solution(mesh):
    placed = (
        P("inner", "outer"),
        P("inner", "outer"),
        P("outer", None, None),
        P("inner", None),
        P("outer", None, None),
        P(None, "outer"),
    )
    return jax.shard_map(
        on_device, mesh=mesh, in_specs=placed, out_specs=P("inner", "outer"), check_vma=False
    )
```

```python
import math

import jax
import jax.numpy as jnp
from jax import lax
from jax.experimental import pallas as pl
from jax.experimental.pallas import tpu as pltpu
from jax.sharding import PartitionSpec as P

NOPE = 128
ROPE = 64
VDIM = 128
LAT = 512
WIDE = LAT + ROPE
MESH = pl.DeviceIdType.MESH
SCALE = math.log2(math.e) / math.sqrt(NOPE + ROPE)
NX, NZ = 4, 8


def div(a, b):
    return a // b if isinstance(a, int) else lax.div(a, b)


def rem(a, b):
    return a % b if isinstance(a, int) else lax.rem(a, b)


def kernel(
    qn_hbm, qr_hbm, ak_hbm, kv_hbm, vu_hbm, wo_hbm, out_ref,
    qn, qr, ak, vu, wo, kvbuf, vbuf, query, peak, total, acc, mix,
    local_sem, kv_recv, send_z, send_y, sib_a, sib_b, v_recv, send_x, send_c, sib_v,
):
    heads, rows = ak.shape[0], qn.shape[0]
    o, i = lax.axis_index("outer"), lax.axis_index("inner")
    core, yh, x = rem(o, 2), rem(div(o, 2), 2), div(o, 4)
    yl, z = div(i, NZ), rem(i, NZ)

    def outer_of(x_, yh_, core_):
        return (x_ * 2 + yh_) * 2 + core_

    sibling = (outer_of(x, yh, 1 - core), i)
    z_up = (o, yl * NZ + rem(z + 1, NZ))
    z_down = (o, yl * NZ + rem(z + NZ - 1, NZ))
    y_up = (outer_of(x, rem(yh + yl, 2), core), (1 - yl) * NZ + z)
    y_down = (outer_of(x, rem(yh + 1 - yl, 2), core), (1 - yl) * NZ + z)
    y_far = (outer_of(x, 1 - yh, core), i)
    x_up = (outer_of(rem(x + 1, NX), yh, core), i)
    x_down = (outer_of(rem(x + NX - 1, NX), yh, core), i)

    locals_ = [
        pltpu.make_async_copy(kv_hbm.at[part], kvbuf.at[i, part], local_sem.at[part])
        for part in range(4)
    ]
    for n, (src, dst) in enumerate(
        [(qn_hbm, qn), (ak_hbm, ak), (qr_hbm, qr), (vu_hbm, vu), (wo_hbm, wo)]
    ):
        locals_.append(pltpu.make_async_copy(src, dst, local_sem.at[4 + n]))
    for copy in locals_:
        copy.start()

    barrier = pltpu.get_barrier_semaphore()
    partners = (sibling, z_up, z_down, y_up, y_down, y_far, x_up, x_down)
    for partner in partners:
        pl.semaphore_signal(barrier, inc=1, device_id=partner, device_id_type=MESH)
    pl.semaphore_wait(barrier, len(partners))

    def kv_copy(j, k, send_sem, target):
        piece = kvbuf.at[j, 2 * core + k]
        return pltpu.make_async_remote_copy(
            src_ref=piece, dst_ref=piece, send_sem=send_sem,
            recv_sem=kv_recv.at[j, 2 * core + k], device_id=target, device_id_type=MESH,
        )

    def kv_arrived(j, part):
        piece = kvbuf.at[j, part]
        pltpu.make_async_remote_copy(
            src_ref=piece, dst_ref=piece, send_sem=send_z.at[0, 0, 0],
            recv_sem=kv_recv.at[j, part], device_id=sibling, device_id_type=MESH,
        ).wait_recv()

    def ring(d, side):
        return rem(z + (d if side else NZ - d), NZ)

    def z_forwards(d, side, k):
        return (d <= 2) | ((d == 3) & (k == side))

    def held_a(d, side, k):
        return (d <= 3) | ((d == 4) & (k == side))

    def held_b(d, side, k):
        return ((d == 0) & (side == 0)) | ((d >= 1) & (d <= 3)) | ((d == 4) & (k == side))

    def z_send(d, side, k):
        return kv_copy(yl * NZ + ring(d, side), k, send_z.at[side, d, k], (z_up, z_down)[side])

    def y_send(d, side, k):
        target = (outer_of(x, rem(yh + k, 2), core), NZ + z)
        return kv_copy(ring(d, side), k, send_y.at[side, d, k], target)

    def sib_a_send(d, side, k):
        return kv_copy(yl * NZ + ring(d, side), k, sib_a.at[side, d, k], sibling)

    def sib_b_send(d, side, k):
        return kv_copy(ring(d, side), k, sib_b.at[side, d, k], sibling)

    def relay_a(d, k):
        for side in range(2):
            j = yl * NZ + ring(d, side)

            @pl.when(held_a(d, side, k))
            def _():
                kv_arrived(j, 2 * core + k)

                @pl.when(z_forwards(d, side, k))
                def _():
                    z_send(d, side, k).start()

                @pl.when(yl == 0)
                def _():
                    y_send(d, side, k).start()

                @pl.when(j < i)
                def _():
                    sib_a_send(d, side, k).start()

    def relay_b(d, k):
        for side in range(2):
            @pl.when(held_b(d, side, k))
            def _():
                kv_arrived(ring(d, side), 2 * core + k)
                sib_b_send(d, side, k).start()

    for part in range(4):
        locals_[part].wait()

    def own(k):
        for side in range(2):
            z_send(0, side, k).start()

        @pl.when(yl == 0)
        def _():
            y_send(0, 0, k).start()

    own(0)

    locals_[4].wait()
    locals_[5].wait()
    locals_[6].wait()
    qr_across = qr[...].T
    for h in range(heads):
        at = slice(h * rows, (h + 1) * rows)
        query[:LAT, at] = jnp.dot(
            qn[:, h * NOPE : (h + 1) * NOPE], ak[h], preferred_element_type=jnp.float32
        ).astype(jnp.bfloat16).T
        query[LAT:, at] = qr_across[h * ROPE : (h + 1) * ROPE]

    def attend(j, first, pairs):
        latent = kvbuf[j].reshape(WIDE, rows)
        keys = latent.T
        width = 2 * rows

        def scores(pair):
            at = slice(pair * width, (pair + 1) * width)
            s = jnp.dot(keys, query[:, at], preferred_element_type=jnp.float32) * SCALE
            if first:
                key = lax.broadcasted_iota(jnp.int32, s.shape, 0)
                row = rem(lax.broadcasted_iota(jnp.int32, s.shape, 1), rows)
                s = jnp.where(key <= row, s, jnp.float32(-1e30))
            return s.reshape(rows // 8, 8, width)

        def fold(pair, s):
            at = slice(pair * width, (pair + 1) * width)
            top = jnp.max(jnp.max(s, axis=0), axis=0, keepdims=True)
            if first:
                new = jnp.broadcast_to(top, (8, width))
            else:
                old = peak[:, at]
                new = jnp.maximum(old, top)
            w = jnp.exp2(s - new[None])
            part = jnp.sum(w, axis=0)
            update = jnp.dot(
                latent[:LAT], w.reshape(rows, width).astype(jnp.bfloat16),
                preferred_element_type=jnp.float32,
            )
            peak[:, at] = new
            if first:
                total[:, at] = part
                acc[:, at] = update
            else:
                shrink = jnp.exp2(old - new)
                total[:, at] = total[:, at] * shrink + part
                grown = acc[:, at].reshape(LAT // 8, 8, width) * shrink[None]
                acc[:, at] = grown.reshape(LAT, width) + update

        s = [scores(pair) for pair in pairs]
        for pair, pair_scores in zip(pairs, s):
            fold(pair, pair_scores)

    own(1)
    attend(i, True, (0, 1))

    def swapped(j):
        for k in range(2):
            kv_arrived(j, 2 * (1 - core) + k)

    def half_step(n, carry):
        d, k = div(n, 2) + 1, rem(n, 2)

        @pl.when(d <= 4)
        def _():
            relay_a(d, k)

        def group(ab, carry):
            @pl.when((ab == 1) & (yl == 1))
            def _():
                relay_b(d - 1, k)

            dd = d - 1 - ab
            j = (1 - ab) * (yl * NZ) + rem(z + dd * (2 * k - 1) + NZ, NZ)
            in_a = (ab == 0) & (((dd >= 1) & (dd <= 3)) | ((dd == 4) & (k == 0) & (yl == 1)))
            in_b = (ab == 1) & (yl == 1) & (((dd >= 1) & (dd <= 3)) | ((dd == 0) & (k == 0)))

            @pl.when((in_a | in_b) & (j < i))
            def _():
                swapped(j)
                attend(j, False, (0, 1))

            return carry

        return lax.fori_loop(0, 2, group, carry)

    lax.fori_loop(0, 10, half_step, 0)
    last = rem(z + 4, NZ)

    def block(e):
        n, dy = rem(e, 4), div(e, 4)
        dx = n + div(n, 2) * (1 - 2 * rem(n, 2))
        return rem(x + dx, NX), rem(yh + dy, 2)

    def v_copy(e, k, send_sem, target):
        xx, yy = block(e)
        slot = outer_of(xx, yy, core)
        piece = vbuf.at[slot, k]
        return pltpu.make_async_remote_copy(
            src_ref=piece, dst_ref=piece, send_sem=send_sem,
            recv_sem=v_recv.at[slot, k], device_id=target, device_id_type=MESH,
        )

    def v_arrived(slot, k):
        piece = vbuf.at[slot, k]
        pltpu.make_async_remote_copy(
            src_ref=piece, dst_ref=piece, send_sem=send_c.at[0, 0],
            recv_sem=v_recv.at[slot, k], device_id=sibling, device_id_type=MESH,
        ).wait_recv()

    def own_slot(e):
        xx, yy = block(e)
        return outer_of(xx, yy, core)

    def sib_slot(e):
        xx, yy = block(e)
        return outer_of(xx, yy, 1 - core)

    locals_[7].wait()

    def send(e, k, way):
        sem = {
            "far": lambda: send_c.at[e, k], "up": lambda: send_x.at[e, k, 0],
            "down": lambda: send_x.at[e, k, 1], "sib": lambda: sib_v.at[e, k],
        }[way]()
        target = {"far": y_far, "up": x_up, "down": x_down, "sib": sibling}[way]
        return v_copy(e, k, sem, target)

    for k in range(2):
        pair = (2 * k, 2 * k + 1)

        @pl.when(last < i)
        def _():
            if k == 0:
                swapped(last)
            attend(last, False, (k,))

        for h in pair:
            at = slice(h * rows, (h + 1) * rows)
            whole = jnp.sum(total[:, at], axis=0, keepdims=True)
            latent_out = (acc[:, at] * (1.0 / whole)).astype(jnp.bfloat16)
            vbuf[o, k, (h % 2) * VDIM : (h % 2 + 1) * VDIM, :] = jnp.dot(
                vu[h].T, latent_out, preferred_element_type=jnp.float32
            ).astype(jnp.bfloat16)
        for way in ("up", "down", "far", "sib"):
            send(0, k, way).start()

    mix[...] = jnp.zeros_like(mix)

    def project(e):
        depth = heads * VDIM
        term = mix[...]
        for slot in (own_slot(e), sib_slot(e)):
            start = pl.multiple_of(slot * depth, depth)
            term = term + jnp.dot(
                wo[:, pl.ds(start, depth)], vbuf[slot].reshape(depth, rows),
                preferred_element_type=jnp.float32,
            )
        mix[...] = term

    came = (
        ((1, 0, "far"), (2, 0, "up"), (4, 0, "up")),
        ((1, 1, "down", "far"), (2, 1), (4, 1, "up")),
        ((3, 0), (5, 0, "down"), (3, 1)),
        ((6, 0), (5, 1, "down")),
        ((6, 1),),
        ((7, 0),),
        ((7, 1),),
    )

    def event(t, carry):
        for n, items in enumerate(came):
            @pl.when(t == n)
            def _():
                for e, k, *ways in items:
                    v_arrived(own_slot(e), k)
                    for way in (*ways, "sib"):
                        send(e, k, way).start()

        @pl.when(t == 0)
        def _():
            locals_[8].wait()

        for k in range(2):
            v_arrived(sib_slot(t), k)
        project(t)
        return carry

    lax.fori_loop(0, 8, event, 0)
    out_ref[...] = mix[...].astype(jnp.bfloat16)

    for k in range(2):
        for way in ("up", "down", "far", "sib"):
            send(0, k, way).wait_send()
    for items in came:
        for e, k, *ways in items:
            for way in (*ways, "sib"):
                send(e, k, way).wait_send()

    def drain(n, carry):
        d, k = div(n, 2), rem(n, 2)
        for side in range(2):
            @pl.when(z_forwards(d, side, k))
            def _():
                z_send(d, side, k).wait_send()

            @pl.when((yl == 0) & held_b(d, side, k))
            def _():
                y_send(d, side, k).wait_send()

            @pl.when((d >= 1) & held_a(d, side, k) & (yl * NZ + ring(d, side) < i))
            def _():
                sib_a_send(d, side, k).wait_send()

            @pl.when((yl == 1) & held_b(d, side, k))
            def _():
                sib_b_send(d, side, k).wait_send()

        return carry

    lax.fori_loop(0, 10, drain, 0)


def on_device(q_nope, q_rope, absorb_key, kv_latent, value_up, out_proj):
    rows = q_nope.shape[0]
    heads = absorb_key.shape[0]
    columns = out_proj.shape[1]
    kv_parts = kv_latent.T.reshape(4, WIDE // 4, rows)
    out_proj = out_proj.T
    dma = pltpu.SemaphoreType.DMA
    mixed = pl.pallas_call(
        kernel,
        out_shape=jax.ShapeDtypeStruct((columns, rows), jnp.bfloat16),
        in_specs=[pl.BlockSpec(memory_space=pl.ANY)] * 6,
        out_specs=pl.BlockSpec(memory_space=pltpu.VMEM),
        scratch_shapes=[
            pltpu.VMEM(q_nope.shape, jnp.bfloat16),
            pltpu.VMEM(q_rope.shape, jnp.bfloat16),
            pltpu.VMEM(absorb_key.shape, jnp.bfloat16),
            pltpu.VMEM(value_up.shape, jnp.bfloat16),
            pltpu.VMEM(out_proj.shape, jnp.bfloat16),
            pltpu.VMEM((16, 4, WIDE // 4, rows), jnp.bfloat16),
            pltpu.VMEM((16, 2, heads * VDIM // 2, rows), jnp.bfloat16),
            pltpu.VMEM((WIDE, heads * rows), jnp.bfloat16),
            pltpu.VMEM((8, heads * rows), jnp.float32),
            pltpu.VMEM((8, heads * rows), jnp.float32),
            pltpu.VMEM((LAT, heads * rows), jnp.float32),
            pltpu.VMEM((columns, rows), jnp.float32),
            dma((9,)),
            dma((16, 4)),
            dma((2, 4, 2)),
            dma((2, 5, 2)),
            dma((2, 5, 2)),
            dma((2, 5, 2)),
            dma((16, 2)),
            dma((8, 2, 2)),
            dma((2, 2)),
            dma((8, 2)),
        ],
        compiler_params=pltpu.CompilerParams(
            collective_id=0, has_side_effects=True, vmem_limit_bytes=56 * 1024 * 1024
        ),
        cost_estimate=pl.CostEstimate(
            flops=12 * 10**9, bytes_accessed=10 * 10**6, transcendentals=4 * 10**6
        ),
    )(q_nope, q_rope, absorb_key, kv_parts, value_up, out_proj)
    return mixed.T


def solution(mesh):
    placed = (
        P("inner", "outer"),
        P("inner", "outer"),
        P("outer", None, None),
        P("inner", None),
        P("outer", None, None),
        P(None, "outer"),
    )
    return jax.shard_map(
        on_device, mesh=mesh, in_specs=placed, out_specs=P("inner", "outer"), check_vma=False
    )
```

```python
import math

import jax
import jax.numpy as jnp
from jax import lax
from jax.experimental import pallas as pl
from jax.experimental.pallas import tpu as pltpu
from jax.sharding import PartitionSpec as P

NOPE = 128
ROPE = 64
VDIM = 128
LAT = 512
WIDE = LAT + ROPE
MESH = pl.DeviceIdType.MESH
SCALE = math.log2(math.e) / math.sqrt(NOPE + ROPE)
NX, NZ = 4, 8


def div(a, b):
    return a // b if isinstance(a, int) else lax.div(a, b)


def rem(a, b):
    return a % b if isinstance(a, int) else lax.rem(a, b)


def kernel(
    qn_hbm, qr_hbm, ak_hbm, kv_hbm, vu_hbm, wo_hbm, out_ref,
    qn, qr, ak, vu, wo, kvbuf, vbuf, query, peak, total, acc, mix,
    local_sem, kv_recv, send_z, send_y, sib_a, sib_b, v_recv, send_x, send_c, sib_v,
):
    heads, rows = ak.shape[0], qn.shape[0]
    o, i = lax.axis_index("outer"), lax.axis_index("inner")
    core, yh, x = rem(o, 2), rem(div(o, 2), 2), div(o, 4)
    yl, z = div(i, NZ), rem(i, NZ)

    def outer_of(x_, yh_, core_):
        return (x_ * 2 + yh_) * 2 + core_

    def wrap(n, size):
        return jnp.where(n >= size, n - size, n)

    sibling = (outer_of(x, yh, 1 - core), i)
    z_up = (o, yl * NZ + wrap(z + 1, NZ))
    z_down = (o, yl * NZ + wrap(z + NZ - 1, NZ))
    y_up = (outer_of(x, wrap(yh + yl, 2), core), (1 - yl) * NZ + z)
    y_down = (outer_of(x, wrap(yh + 1 - yl, 2), core), (1 - yl) * NZ + z)
    y_far = (outer_of(x, 1 - yh, core), i)
    x_up = (outer_of(wrap(x + 1, NX), yh, core), i)
    x_down = (outer_of(wrap(x + NX - 1, NX), yh, core), i)

    locals_ = [
        pltpu.make_async_copy(kv_hbm.at[part], kvbuf.at[i, part], local_sem.at[part])
        for part in range(4)
    ]
    for n, (src, dst) in enumerate(
        [(qn_hbm, qn), (ak_hbm, ak), (qr_hbm, qr), (vu_hbm, vu), (wo_hbm, wo)]
    ):
        locals_.append(pltpu.make_async_copy(src, dst, local_sem.at[4 + n]))
    for copy in locals_:
        copy.start()

    barrier = pltpu.get_barrier_semaphore()
    partners = (sibling, z_up, z_down, y_up, y_down, y_far, x_up, x_down)
    for partner in partners:
        pl.semaphore_signal(barrier, inc=1, device_id=partner, device_id_type=MESH)
    pl.semaphore_wait(barrier, len(partners))

    mine, others = 2 * core, 2 * (1 - core)

    def kv_copy(j, k, send_sem, target):
        piece = kvbuf.at[j, mine + k]
        return pltpu.make_async_remote_copy(
            src_ref=piece, dst_ref=piece, send_sem=send_sem,
            recv_sem=kv_recv.at[j, mine + k], device_id=target, device_id_type=MESH,
        )

    def kv_arrived(j, part):
        piece = kvbuf.at[j, part]
        pltpu.make_async_remote_copy(
            src_ref=piece, dst_ref=piece, send_sem=send_z.at[0, 0, 0],
            recv_sem=kv_recv.at[j, part], device_id=sibling, device_id_type=MESH,
        ).wait_recv()

    def ring(d, side):
        return wrap(z + (d if side else NZ - d), NZ)

    def z_forwards(d, side, k):
        return (d <= 2) | ((d == 3) & (k == side))

    def held_a(d, side, k):
        return (d <= 3) | ((d == 4) & (k == side))

    def held_b(d, side, k):
        return (d <= 3) | ((d == 4) & (k == side))

    first_a = yl * NZ

    def z_send(j, d, side, k):
        return kv_copy(j, k, send_z.at[side, d, k], (z_up, z_down)[side])

    o_far = outer_of(x, 1 - yh, core)

    def y_send(j, d, side, k):
        return kv_copy(j, k, send_y.at[side, d, k], (jnp.where(k == 0, o, o_far), NZ + z))

    def sib_a_send(j, d, side, k):
        return kv_copy(j, k, sib_a.at[side, d, k], sibling)

    def sib_b_send(j, d, side, k):
        return kv_copy(j, k, sib_b.at[side, d, k], sibling)

    def relay_a(d, k):
        for side in range(2):
            @pl.when(held_a(d, side, k))
            def _():
                j = first_a + ring(d, side)
                kv_arrived(j, mine + k)

                @pl.when(z_forwards(d, side, k))
                def _():
                    z_send(j, d, side, k).start()

                @pl.when(yl == 0)
                def _():
                    y_send(j, d, side, k).start()

                @pl.when(j < i)
                def _():
                    sib_a_send(j, d, side, k).start()

    def relay_b(d, k):
        @pl.when(d == 0)
        def _():
            kv_arrived(z, mine + k)
            sib_b_send(z, 0, 0, k).start()

        for side in range(2):
            @pl.when((d >= 1) & held_b(d, side, k))
            def _():
                j = ring(d, side)
                kv_arrived(j, mine + k)
                sib_b_send(j, d, side, k).start()

    for part in range(4):
        locals_[part].wait()

    def own(k):
        for side in range(2):
            z_send(i, 0, side, k).start()

        @pl.when(yl == 0)
        def _():
            y_send(i, 0, 0, k).start()

    own(0)

    locals_[4].wait()
    locals_[5].wait()
    locals_[6].wait()
    qr_across = qr[...].T
    for h in range(heads):
        at = slice(h * rows, (h + 1) * rows)
        query[:LAT, at] = jnp.dot(
            qn[:, h * NOPE : (h + 1) * NOPE], ak[h], preferred_element_type=jnp.float32
        ).astype(jnp.bfloat16).T
        query[LAT:, at] = qr_across[h * ROPE : (h + 1) * ROPE]

    def attend(j, first, pairs):
        latent = kvbuf[j].reshape(WIDE, rows)
        keys = latent.T
        width = 2 * rows

        def scores(pair):
            at = slice(pair * width, (pair + 1) * width)
            s = jnp.dot(keys, query[:, at], preferred_element_type=jnp.float32) * SCALE
            if first:
                key = lax.broadcasted_iota(jnp.int32, s.shape, 0)
                row = lax.broadcasted_iota(jnp.int32, s.shape, 1)
                s = jnp.where(key <= jnp.where(row >= rows, row - rows, row), s, jnp.float32(-1e30))
            return s.reshape(rows // 8, 8, width)

        def fold(pair, s):
            at = slice(pair * width, (pair + 1) * width)
            top = jnp.max(jnp.max(s, axis=0), axis=0, keepdims=True)
            if first:
                new = jnp.broadcast_to(top, (8, width))
            else:
                old = peak[:, at]
                new = jnp.maximum(old, top)
            w = jnp.exp2(s - new[None])
            part = jnp.sum(w, axis=0)
            update = jnp.dot(
                latent[:LAT], w.reshape(rows, width).astype(jnp.bfloat16),
                preferred_element_type=jnp.float32,
            )
            peak[:, at] = new
            if first:
                total[:, at] = part
                acc[:, at] = update
            else:
                shrink = jnp.exp2(old - new)
                total[:, at] = total[:, at] * shrink + part
                grown = acc[:, at].reshape(LAT // 8, 8, width) * shrink[None]
                acc[:, at] = grown.reshape(LAT, width) + update

        s = [scores(pair) for pair in pairs]
        for pair, pair_scores in zip(pairs, s):
            fold(pair, pair_scores)

    own(1)
    attend(i, True, (0, 1))

    def swapped(j):
        for k in range(2):
            kv_arrived(j, others + k)

    def hop(d, carry):
        def half_step(k, carry):
            @pl.when(d <= 4)
            def _():
                relay_a(d, k)

            def group(ab, carry):
                @pl.when((ab == 1) & (yl == 1))
                def _():
                    relay_b(d - 1, k)

                dd = d - 1 - ab
                j = jnp.where(ab == 0, first_a, 0) + wrap(jnp.where(k == 0, z + NZ - dd, z + dd), NZ)
                in_a = (ab == 0) & (((dd >= 1) & (dd <= 3)) | ((dd == 4) & (k == 0) & (yl == 1)))
                in_b = (ab == 1) & (yl == 1) & (((dd >= 1) & (dd <= 3)) | ((dd == 0) & (k == 0)))

                @pl.when((in_a | in_b) & (j < i))
                def _():
                    swapped(j)
                    attend(j, False, (0, 1))

                return carry

            return lax.fori_loop(0, 2, group, carry)

        return lax.fori_loop(0, 2, half_step, carry)

    lax.fori_loop(1, 6, hop, 0)
    last = wrap(z + 4, NZ)

    own_slots, sib_slots = [], []
    for there in (yh, 1 - yh):
        for dx in (0, 1, 3, 2):
            place = outer_of(wrap(x + dx, NX), there, 0)
            own_slots.append(place + core)
            sib_slots.append(place + 1 - core)

    def v_arrived(slot, k):
        piece = vbuf.at[slot, k]
        pltpu.make_async_remote_copy(
            src_ref=piece, dst_ref=piece, send_sem=send_c.at[0, 0],
            recv_sem=v_recv.at[slot, k], device_id=sibling, device_id_type=MESH,
        ).wait_recv()

    locals_[7].wait()

    def send(e, k, way):
        sem = {
            "far": lambda: send_c.at[e, k], "up": lambda: send_x.at[e, k, 0],
            "down": lambda: send_x.at[e, k, 1], "sib": lambda: sib_v.at[e, k],
        }[way]()
        target = {"far": y_far, "up": x_up, "down": x_down, "sib": sibling}[way]
        piece = vbuf.at[own_slots[e], k]
        return pltpu.make_async_remote_copy(
            src_ref=piece, dst_ref=piece, send_sem=sem,
            recv_sem=v_recv.at[own_slots[e], k], device_id=target, device_id_type=MESH,
        )

    for k in range(2):
        pair = (2 * k, 2 * k + 1)

        @pl.when(last < i)
        def _():
            if k == 0:
                swapped(last)
            attend(last, False, (k,))

        for h in pair:
            at = slice(h * rows, (h + 1) * rows)
            whole = jnp.sum(total[:, at], axis=0, keepdims=True)
            latent_out = (acc[:, at] * (1.0 / whole)).astype(jnp.bfloat16)
            vbuf[o, k, (h % 2) * VDIM : (h % 2 + 1) * VDIM, :] = jnp.dot(
                vu[h].T, latent_out, preferred_element_type=jnp.float32
            ).astype(jnp.bfloat16)
        for way in ("up", "down", "far", "sib"):
            send(0, k, way).start()

    mix[...] = jnp.zeros_like(mix)

    def project(slots):
        depth = heads * VDIM
        term = mix[...]
        for slot in slots:
            start = pl.multiple_of(slot * depth, depth)
            term = term + jnp.dot(
                wo[:, pl.ds(start, depth)], vbuf[slot].reshape(depth, rows),
                preferred_element_type=jnp.float32,
            )
        mix[...] = term

    came = (
        ((1, 0, "far"), (2, 0, "up"), (4, 0, "up")),
        ((1, 1, "down", "far"), (2, 1), (4, 1, "up")),
        ((3, 0), (5, 0, "down"), (3, 1)),
        ((6, 0), (5, 1, "down")),
        ((6, 1),),
        ((7, 0),),
        ((7, 1),),
    )

    def event(t, carry):
        for n, items in enumerate(came):
            @pl.when(t == n)
            def _():
                for e, k, *ways in items:
                    v_arrived(own_slots[e], k)
                    for way in (*ways, "sib"):
                        send(e, k, way).start()

        @pl.when(t == 0)
        def _():
            locals_[8].wait()

        n = jnp.where(t >= 4, t - 4, t)
        dx = jnp.where(n == 2, 3, jnp.where(n == 3, 2, n))
        place = outer_of(wrap(x + dx, NX), jnp.where(t >= 4, 1 - yh, yh), 0)
        for k in range(2):
            v_arrived(place + 1 - core, k)
        project((place + core, place + 1 - core))
        return carry

    lax.fori_loop(0, 8, event, 0)
    out_ref[...] = mix[...].astype(jnp.bfloat16)

    for k in range(2):
        for way in ("up", "down", "far", "sib"):
            send(0, k, way).wait_send()
    for items in came:
        for e, k, *ways in items:
            for way in (*ways, "sib"):
                send(e, k, way).wait_send()

    for k in range(2):
        for side in range(2):
            z_send(i, 0, side, k).wait_send()

        @pl.when(yl == 0)
        def _():
            y_send(i, 0, 0, k).wait_send()

        @pl.when(yl == 1)
        def _():
            sib_b_send(z, 0, 0, k).wait_send()

    def drain(d, carry):
        for k in range(2):
            for side in range(2):
                @pl.when(held_a(d, side, k))
                def _():
                    zz = ring(d, side)
                    j = first_a + zz

                    @pl.when(z_forwards(d, side, k))
                    def _():
                        z_send(j, d, side, k).wait_send()

                    @pl.when(yl == 0)
                    def _():
                        y_send(j, d, side, k).wait_send()

                    @pl.when(j < i)
                    def _():
                        sib_a_send(j, d, side, k).wait_send()

                    @pl.when(yl == 1)
                    def _():
                        sib_b_send(zz, d, side, k).wait_send()

        return carry

    lax.fori_loop(1, 5, drain, 0)


def on_device(q_nope, q_rope, absorb_key, kv_latent, value_up, out_proj):
    rows = q_nope.shape[0]
    heads = absorb_key.shape[0]
    columns = out_proj.shape[1]
    kv_parts = kv_latent.T.reshape(4, WIDE // 4, rows)
    out_proj = out_proj.T
    dma = pltpu.SemaphoreType.DMA
    mixed = pl.pallas_call(
        kernel,
        out_shape=jax.ShapeDtypeStruct((columns, rows), jnp.bfloat16),
        in_specs=[pl.BlockSpec(memory_space=pl.ANY)] * 6,
        out_specs=pl.BlockSpec(memory_space=pltpu.VMEM),
        scratch_shapes=[
            pltpu.VMEM(q_nope.shape, jnp.bfloat16),
            pltpu.VMEM(q_rope.shape, jnp.bfloat16),
            pltpu.VMEM(absorb_key.shape, jnp.bfloat16),
            pltpu.VMEM(value_up.shape, jnp.bfloat16),
            pltpu.VMEM(out_proj.shape, jnp.bfloat16),
            pltpu.VMEM((16, 4, WIDE // 4, rows), jnp.bfloat16),
            pltpu.VMEM((16, 2, heads * VDIM // 2, rows), jnp.bfloat16),
            pltpu.VMEM((WIDE, heads * rows), jnp.bfloat16),
            pltpu.VMEM((8, heads * rows), jnp.float32),
            pltpu.VMEM((8, heads * rows), jnp.float32),
            pltpu.VMEM((LAT, heads * rows), jnp.float32),
            pltpu.VMEM((columns, rows), jnp.float32),
            dma((9,)),
            dma((16, 4)),
            dma((2, 4, 2)),
            dma((2, 5, 2)),
            dma((2, 5, 2)),
            dma((2, 5, 2)),
            dma((16, 2)),
            dma((8, 2, 2)),
            dma((2, 2)),
            dma((8, 2)),
        ],
        compiler_params=pltpu.CompilerParams(
            collective_id=0, has_side_effects=True, vmem_limit_bytes=56 * 1024 * 1024
        ),
        cost_estimate=pl.CostEstimate(
            flops=12 * 10**9, bytes_accessed=10 * 10**6, transcendentals=4 * 10**6
        ),
    )(q_nope, q_rope, absorb_key, kv_parts, value_up, out_proj)
    return mixed.T


def solution(mesh):
    placed = (
        P("inner", "outer"),
        P("inner", "outer"),
        P("outer", None, None),
        P("inner", None),
        P("outer", None, None),
        P(None, "outer"),
    )
    return jax.shard_map(
        on_device, mesh=mesh, in_specs=placed, out_specs=P("inner", "outer"), check_vma=False
    )
```

```python
import math

import jax
import jax.numpy as jnp
from jax import lax
from jax.experimental import pallas as pl
from jax.experimental.pallas import tpu as pltpu
from jax.sharding import PartitionSpec as P

NOPE = 128
ROPE = 64
VDIM = 128
LAT = 512
WIDE = LAT + ROPE
MESH = pl.DeviceIdType.MESH
SCALE = math.log2(math.e) / math.sqrt(NOPE + ROPE)
NX, NZ = 4, 8


def div(a, b):
    return a // b if isinstance(a, int) else lax.div(a, b)


def rem(a, b):
    return a % b if isinstance(a, int) else lax.rem(a, b)


def kernel(
    qn_hbm, qr_hbm, ak_hbm, kv_hbm, vu_hbm, wo_hbm, out_ref,
    qn, qr, ak, vu, wo, kvbuf, vbuf, query, peak, total, acc, mix,
    local_sem, kv_recv, send_z, send_y, sib_a, sib_b, v_recv, send_x, send_c, sib_v,
):
    heads, rows = ak.shape[0], qn.shape[0]
    o, i = lax.axis_index("outer"), lax.axis_index("inner")
    core, yh, x = rem(o, 2), rem(div(o, 2), 2), div(o, 4)
    yl, z = div(i, NZ), rem(i, NZ)

    def outer_of(x_, yh_, core_):
        return (x_ * 2 + yh_) * 2 + core_

    def wrap(n, size):
        return jnp.where(n >= size, n - size, n)

    sibling = (outer_of(x, yh, 1 - core), i)
    z_up = (o, yl * NZ + wrap(z + 1, NZ))
    z_down = (o, yl * NZ + wrap(z + NZ - 1, NZ))
    y_up = (outer_of(x, wrap(yh + yl, 2), core), (1 - yl) * NZ + z)
    y_down = (outer_of(x, wrap(yh + 1 - yl, 2), core), (1 - yl) * NZ + z)
    y_far = (outer_of(x, 1 - yh, core), i)
    x_up = (outer_of(wrap(x + 1, NX), yh, core), i)
    x_down = (outer_of(wrap(x + NX - 1, NX), yh, core), i)

    locals_ = [
        pltpu.make_async_copy(kv_hbm.at[part], kvbuf.at[i, part], local_sem.at[part])
        for part in range(4)
    ]
    for n, (src, dst) in enumerate(
        [(qn_hbm, qn), (ak_hbm, ak), (qr_hbm, qr), (vu_hbm, vu), (wo_hbm, wo)]
    ):
        locals_.append(pltpu.make_async_copy(src, dst, local_sem.at[4 + n]))
    for copy in locals_:
        copy.start()

    barrier = pltpu.get_barrier_semaphore()
    partners = (sibling, z_up, z_down, y_up, y_down, y_far, x_up, x_down)
    for partner in partners:
        pl.semaphore_signal(barrier, inc=1, device_id=partner, device_id_type=MESH)
    pl.semaphore_wait(barrier, len(partners))

    mine, others = 2 * core, 2 * (1 - core)

    def kv_copy(j, k, send_sem, target):
        piece = kvbuf.at[j, mine + k]
        return pltpu.make_async_remote_copy(
            src_ref=piece, dst_ref=piece, send_sem=send_sem,
            recv_sem=kv_recv.at[j, mine + k], device_id=target, device_id_type=MESH,
        )

    def kv_arrived(j, part):
        piece = kvbuf.at[j, part]
        pltpu.make_async_remote_copy(
            src_ref=piece, dst_ref=piece, send_sem=send_z.at[0, 0, 0],
            recv_sem=kv_recv.at[j, part], device_id=sibling, device_id_type=MESH,
        ).wait_recv()

    def ring(d, side):
        return wrap(z + (d if side else NZ - d), NZ)

    def z_forwards(d, side, k):
        return (d <= 2) | ((d == 3) & (k == side))

    def held_a(d, side, k):
        return (d <= 3) | ((d == 4) & (k == side))

    def held_b(d, side, k):
        return (d <= 3) | ((d == 4) & (k == side))

    first_a = yl * NZ

    def z_send(j, d, side, k):
        return kv_copy(j, k, send_z.at[side, d, k], (z_up, z_down)[side])

    o_far = outer_of(x, 1 - yh, core)

    def y_send(j, d, side, k):
        return kv_copy(j, k, send_y.at[side, d, k], (jnp.where(k == 0, o, o_far), NZ + z))

    def sib_a_send(j, d, side, k):
        return kv_copy(j, k, sib_a.at[side, d, k], sibling)

    def sib_b_send(j, d, side, k):
        return kv_copy(j, k, sib_b.at[side, d, k], sibling)

    def relay_a(d, k):
        for side in range(2):
            @pl.when(held_a(d, side, k))
            def _():
                j = first_a + ring(d, side)
                kv_arrived(j, mine + k)

                @pl.when(z_forwards(d, side, k))
                def _():
                    z_send(j, d, side, k).start()

                @pl.when(yl == 0)
                def _():
                    y_send(j, d, side, k).start()

                @pl.when(j < i)
                def _():
                    sib_a_send(j, d, side, k).start()

    def relay_b(d, k):
        @pl.when(d == 0)
        def _():
            kv_arrived(z, mine + k)
            sib_b_send(z, 0, 0, k).start()

        for side in range(2):
            @pl.when((d >= 1) & held_b(d, side, k))
            def _():
                j = ring(d, side)
                kv_arrived(j, mine + k)
                sib_b_send(j, d, side, k).start()

    for part in range(4):
        locals_[part].wait()

    def own(k):
        for side in range(2):
            z_send(i, 0, side, k).start()

        @pl.when(yl == 0)
        def _():
            y_send(i, 0, 0, k).start()

    own(0)

    locals_[4].wait()
    locals_[5].wait()
    locals_[6].wait()
    qr_across = qr[...].T
    for h in range(heads):
        at = slice(h * rows, (h + 1) * rows)
        query[:LAT, at] = jnp.dot(
            qn[:, h * NOPE : (h + 1) * NOPE], ak[h], preferred_element_type=jnp.float32
        ).astype(jnp.bfloat16).T
        query[LAT:, at] = qr_across[h * ROPE : (h + 1) * ROPE]

    def attend(j, first, pairs):
        latent = kvbuf[j].reshape(WIDE, rows)
        keys = latent.T
        width = 2 * rows

        def scores(pair):
            at = slice(pair * width, (pair + 1) * width)
            s = jnp.dot(keys, query[:, at], preferred_element_type=jnp.float32) * SCALE
            if first:
                key = lax.broadcasted_iota(jnp.int32, s.shape, 0)
                row = lax.broadcasted_iota(jnp.int32, s.shape, 1)
                s = jnp.where(key <= jnp.where(row >= rows, row - rows, row), s, jnp.float32(-1e30))
            return s.reshape(rows // 8, 8, width)

        def fold(pair, s):
            at = slice(pair * width, (pair + 1) * width)
            top = jnp.max(jnp.max(s, axis=0), axis=0, keepdims=True)
            if first:
                new = jnp.broadcast_to(top, (8, width))
            else:
                old = peak[:, at]
                new = jnp.maximum(old, top)
            w = jnp.exp2(s - new[None])
            part = jnp.sum(w, axis=0)
            update = jnp.dot(
                latent[:LAT], w.reshape(rows, width).astype(jnp.bfloat16),
                preferred_element_type=jnp.float32,
            )
            peak[:, at] = new
            if first:
                total[:, at] = part
                acc[:, at] = update
            else:
                shrink = jnp.exp2(old - new)
                total[:, at] = total[:, at] * shrink + part
                grown = acc[:, at].reshape(LAT // 8, 8, width) * shrink[None]
                acc[:, at] = grown.reshape(LAT, width) + update

        s = [scores(pair) for pair in pairs]
        for pair, pair_scores in zip(pairs, s):
            fold(pair, pair_scores)

    own(1)
    attend(i, True, (0, 1))

    def swapped(j):
        for k in range(2):
            kv_arrived(j, others + k)

    def hop(d, carry):
        def half_step(k, carry):
            @pl.when(d <= 4)
            def _():
                relay_a(d, k)

            def group(ab, carry):
                dd = d - 1 - ab
                j = jnp.where(ab == 0, first_a, 0) + wrap(jnp.where(k == 0, z + NZ - dd, z + dd), NZ)
                in_a = (ab == 0) & (((dd >= 1) & (dd <= 3)) | ((dd == 4) & (k == 0) & (yl == 1)))
                in_b = (ab == 1) & (yl == 1) & (((dd >= 1) & (dd <= 3)) | ((dd == 0) & (k == 0)))

                @pl.when((in_a | in_b) & (j < i))
                def _():
                    swapped(j)
                    attend(j, False, (0, 1))

                @pl.when((ab == 1) & (yl == 1))
                def _():
                    relay_b(d - 1, k)

                return carry

            return lax.fori_loop(0, 2, group, carry)

        return lax.fori_loop(0, 2, half_step, carry)

    lax.fori_loop(1, 6, hop, 0)
    last = wrap(z + 4, NZ)

    own_slots, sib_slots = [], []
    for there in (yh, 1 - yh):
        for dx in (0, 1, 3, 2):
            place = outer_of(wrap(x + dx, NX), there, 0)
            own_slots.append(place + core)
            sib_slots.append(place + 1 - core)

    def v_arrived(slot, k):
        piece = vbuf.at[slot, k]
        pltpu.make_async_remote_copy(
            src_ref=piece, dst_ref=piece, send_sem=send_c.at[0, 0],
            recv_sem=v_recv.at[slot, k], device_id=sibling, device_id_type=MESH,
        ).wait_recv()

    locals_[7].wait()

    def send(e, k, way):
        sem = {
            "far": lambda: send_c.at[e, k], "up": lambda: send_x.at[e, k, 0],
            "down": lambda: send_x.at[e, k, 1], "sib": lambda: sib_v.at[e, k],
        }[way]()
        target = {"far": y_far, "up": x_up, "down": x_down, "sib": sibling}[way]
        piece = vbuf.at[own_slots[e], k]
        return pltpu.make_async_remote_copy(
            src_ref=piece, dst_ref=piece, send_sem=sem,
            recv_sem=v_recv.at[own_slots[e], k], device_id=target, device_id_type=MESH,
        )

    for k in range(2):
        pair = (2 * k, 2 * k + 1)

        @pl.when(last < i)
        def _():
            if k == 0:
                swapped(last)
            attend(last, False, (k,))

        for h in pair:
            at = slice(h * rows, (h + 1) * rows)
            whole = jnp.sum(total[:, at], axis=0, keepdims=True)
            latent_out = (acc[:, at] * (1.0 / whole)).astype(jnp.bfloat16)
            vbuf[o, h] = jnp.dot(
                vu[h].T, latent_out, preferred_element_type=jnp.float32
            ).astype(jnp.bfloat16)
            for way in ("up", "down", "far", "sib"):
                send(0, h, way).start()

    mix[...] = jnp.zeros_like(mix)

    def project(slots):
        depth = heads * VDIM
        term = mix[...]
        for slot in slots:
            start = pl.multiple_of(slot * depth, depth)
            term = term + jnp.dot(
                wo[:, pl.ds(start, depth)], vbuf[slot].reshape(depth, rows),
                preferred_element_type=jnp.float32,
            )
        mix[...] = term

    def near(k):
        return ((1, k, "far", *(("down",) if k % 2 else ())), (2, k, *(() if k % 2 else ("up",))), (4, k, "up"))

    def middle(k):
        return ((3, k), (5, k, "down"), (6, k))

    came = (
        near(0) + near(1), near(2) + near(3), middle(0), middle(1), middle(2), middle(3) + ((7, 0),),
        ((7, 1),), ((7, 2),), ((7, 3),),
    )
    projected = (0, 1, 2, 4, None, 3, 5, 6, 7)

    def event(t, carry):
        for n, items in enumerate(came):
            @pl.when(t == n)
            def _():
                for e, k, *ways in items:
                    v_arrived(own_slots[e], k)
                    for way in (*ways, "sib"):
                        send(e, k, way).start()

        @pl.when(t == 0)
        def _():
            locals_[8].wait()

        @pl.when((t > 0) & (t != 1 + projected.index(None)))
        def _():
            own_slot, sib_slot = own_slots[0], sib_slots[0]
            for n, e in enumerate(projected):
                if e:
                    own_slot = jnp.where(t == n + 1, own_slots[e], own_slot)
                    sib_slot = jnp.where(t == n + 1, sib_slots[e], sib_slot)
            for k in range(heads):
                v_arrived(sib_slot, k)
            project((own_slot, sib_slot))

        return carry

    lax.fori_loop(0, len(projected) + 1, event, 0)
    out_ref[...] = mix[...].astype(jnp.bfloat16)

    for k in range(heads):
        for way in ("up", "down", "far", "sib"):
            send(0, k, way).wait_send()
    for items in came:
        for e, k, *ways in items:
            for way in (*ways, "sib"):
                send(e, k, way).wait_send()

    for k in range(2):
        for side in range(2):
            z_send(i, 0, side, k).wait_send()

        @pl.when(yl == 0)
        def _():
            y_send(i, 0, 0, k).wait_send()

        @pl.when(yl == 1)
        def _():
            sib_b_send(z, 0, 0, k).wait_send()

    def drain(d, carry):
        for k in range(2):
            for side in range(2):
                @pl.when(held_a(d, side, k))
                def _():
                    zz = ring(d, side)
                    j = first_a + zz

                    @pl.when(z_forwards(d, side, k))
                    def _():
                        z_send(j, d, side, k).wait_send()

                    @pl.when(yl == 0)
                    def _():
                        y_send(j, d, side, k).wait_send()

                    @pl.when(j < i)
                    def _():
                        sib_a_send(j, d, side, k).wait_send()

                    @pl.when(yl == 1)
                    def _():
                        sib_b_send(zz, d, side, k).wait_send()

        return carry

    lax.fori_loop(1, 5, drain, 0)


def on_device(q_nope, q_rope, absorb_key, kv_latent, value_up, out_proj):
    rows = q_nope.shape[0]
    heads = absorb_key.shape[0]
    columns = out_proj.shape[1]
    kv_parts = kv_latent.T.reshape(4, WIDE // 4, rows)
    out_proj = out_proj.T
    dma = pltpu.SemaphoreType.DMA
    mixed = pl.pallas_call(
        kernel,
        out_shape=jax.ShapeDtypeStruct((columns, rows), jnp.bfloat16),
        in_specs=[pl.BlockSpec(memory_space=pl.ANY)] * 6,
        out_specs=pl.BlockSpec(memory_space=pltpu.VMEM),
        scratch_shapes=[
            pltpu.VMEM(q_nope.shape, jnp.bfloat16),
            pltpu.VMEM(q_rope.shape, jnp.bfloat16),
            pltpu.VMEM(absorb_key.shape, jnp.bfloat16),
            pltpu.VMEM(value_up.shape, jnp.bfloat16),
            pltpu.VMEM(out_proj.shape, jnp.bfloat16),
            pltpu.VMEM((16, 4, WIDE // 4, rows), jnp.bfloat16),
            pltpu.VMEM((16, heads, VDIM, rows), jnp.bfloat16),
            pltpu.VMEM((WIDE, heads * rows), jnp.bfloat16),
            pltpu.VMEM((8, heads * rows), jnp.float32),
            pltpu.VMEM((8, heads * rows), jnp.float32),
            pltpu.VMEM((LAT, heads * rows), jnp.float32),
            pltpu.VMEM((columns, rows), jnp.float32),
            dma((9,)),
            dma((16, 4)),
            dma((2, 4, 2)),
            dma((2, 5, 2)),
            dma((2, 5, 2)),
            dma((2, 5, 2)),
            dma((16, heads)),
            dma((8, heads, 2)),
            dma((2, heads)),
            dma((8, heads)),
        ],
        compiler_params=pltpu.CompilerParams(
            collective_id=0, has_side_effects=True, vmem_limit_bytes=56 * 1024 * 1024
        ),
        cost_estimate=pl.CostEstimate(
            flops=12 * 10**9, bytes_accessed=10 * 10**6, transcendentals=4 * 10**6
        ),
    )(q_nope, q_rope, absorb_key, kv_parts, value_up, out_proj)
    return mixed.T


def solution(mesh):
    placed = (
        P("inner", "outer"),
        P("inner", "outer"),
        P("outer", None, None),
        P("inner", None),
        P("outer", None, None),
        P(None, "outer"),
    )
    return jax.shard_map(
        on_device, mesh=mesh, in_specs=placed, out_specs=P("inner", "outer"), check_vma=False
    )
```

```python
import math

import jax
import jax.numpy as jnp
from jax import lax
from jax.experimental import pallas as pl
from jax.experimental.pallas import tpu as pltpu
from jax.sharding import PartitionSpec as P

NOPE = 128
ROPE = 64
VDIM = 128
LAT = 512
WIDE = LAT + ROPE
MESH = pl.DeviceIdType.MESH
SCALE = math.log2(math.e) / math.sqrt(NOPE + ROPE)
NX, NZ = 4, 8


def kernel(
    qn_hbm, qr_hbm, ak_hbm, kv_hbm, vu_hbm, wo_hbm, out_ref,
    qn, qr, ak, vu, wo, kvbuf, vbuf, query, qr_across, keys, peak, total, acc, mix,
    local_sem, kv_recv, send_z, send_y, sib_a, sib_b, v_recv, send_x, send_c, sib_v,
):
    heads, rows = ak.shape[0], qn.shape[0]
    width = 2 * rows
    o, i = lax.axis_index("outer"), lax.axis_index("inner")
    core, yh, x = lax.rem(o, 2), lax.rem(lax.div(o, 2), 2), lax.div(o, 4)
    yl, z = lax.div(i, NZ), lax.rem(i, NZ)

    def outer_of(x_, yh_, core_):
        return (x_ * 2 + yh_) * 2 + core_

    def wrap(n, size):
        return jnp.where(n >= size, n - size, n)

    def loop(first, end, body):
        def step(n, carry):
            body(n)
            return carry

        lax.fori_loop(first, end, step, 0)

    sibling = (outer_of(x, yh, 1 - core), i)
    first_a = yl * NZ
    z_up, z_down = first_a + wrap(z + 1, NZ), first_a + wrap(z + NZ - 1, NZ)
    y_up = (outer_of(x, wrap(yh + yl, 2), core), (1 - yl) * NZ + z)
    y_down = (outer_of(x, wrap(yh + 1 - yl, 2), core), (1 - yl) * NZ + z)
    o_far = outer_of(x, 1 - yh, core)
    y_far = (o_far, i)
    x_up = (outer_of(wrap(x + 1, NX), yh, core), i)
    x_down = (outer_of(wrap(x + NX - 1, NX), yh, core), i)

    locals_ = [
        pltpu.make_async_copy(src, dst, local_sem.at[n])
        for n, (src, dst) in enumerate(
            [(kv_hbm, kvbuf.at[i]), (qn_hbm, qn), (ak_hbm, ak), (qr_hbm, qr), (vu_hbm, vu), (wo_hbm, wo)]
        )
    ]
    for copy in locals_:
        copy.start()

    barrier = pltpu.get_barrier_semaphore()
    partners = (sibling, (o, z_up), (o, z_down), y_up, y_down, y_far, x_up, x_down)
    for partner in partners:
        pl.semaphore_signal(barrier, inc=1, device_id=partner, device_id_type=MESH)
    pl.semaphore_wait(barrier, len(partners))

    mine, others = 2 * core, 2 * (1 - core)

    def kv_copy(j, k, send_sem, target):
        piece = kvbuf.at[j, mine + k]
        return pltpu.make_async_remote_copy(
            src_ref=piece, dst_ref=piece, send_sem=send_sem,
            recv_sem=kv_recv.at[j, mine + k], device_id=target, device_id_type=MESH,
        )

    def kv_arrived(j, part):
        piece = kvbuf.at[j, part]
        pltpu.make_async_remote_copy(
            src_ref=piece, dst_ref=piece, send_sem=send_z.at[0, 0, 0],
            recv_sem=kv_recv.at[j, part], device_id=sibling, device_id_type=MESH,
        ).wait_recv()

    def ring(d, side):
        return wrap(jnp.where(side == 0, z + NZ - d, z + d), NZ)

    def z_forwards(d, side, k):
        return (d <= 2) | ((d == 3) & (k == side))

    def held(d, side, k):
        return ((d <= 3) & ((d >= 1) | (side == 0))) | ((d == 4) & (k == side))

    def z_send(j, d, side, k):
        return kv_copy(j, k, send_z.at[side, d, k], (o, jnp.where(side == 0, z_up, z_down)))

    def y_send(j, d, side, k):
        return kv_copy(j, k, send_y.at[side, d, k], (jnp.where(k == 0, o, o_far), NZ + z))

    def sib_a_send(j, d, side, k):
        return kv_copy(j, k, sib_a.at[side, d, k], sibling)

    def sib_b_send(j, d, side, k):
        return kv_copy(j, k, sib_b.at[side, d, k], sibling)

    def relay_a(d, k):
        def one(side):
            j = first_a + ring(d, side)
            here = held(d, side, k)

            @pl.when(here & (d >= 1))
            def _():
                kv_arrived(j, mine + k)

            @pl.when(z_forwards(d, side, k))
            def _():
                z_send(j, d, side, k).start()

            @pl.when(here & (yl == 0))
            def _():
                y_send(j, d, side, k).start()

            @pl.when(here & (j < i))
            def _():
                sib_a_send(j, d, side, k).start()

        loop(0, 2, one)

    def relay_b(d, k):
        def one(side):
            @pl.when(held(d, side, k))
            def _():
                j = ring(d, side)
                kv_arrived(j, mine + k)
                sib_b_send(j, d, side, k).start()

        loop(0, 2, one)

    def absorb(h):
        across = pl.ds(pl.multiple_of(h * rows, rows), rows)
        query[:LAT, across] = jnp.dot(
            qn[:, pl.ds(pl.multiple_of(h * NOPE, NOPE), NOPE)], ak[h],
            preferred_element_type=jnp.float32,
        ).astype(jnp.bfloat16).T
        query[LAT:, across] = qr_across[pl.ds(pl.multiple_of(h * ROPE, ROPE), ROPE)]

    def attend(j, pair, hidden_from):
        at = pl.ds(pl.multiple_of(pair * width, width), width)
        s = jnp.dot(keys[...], query[:, at], preferred_element_type=jnp.float32) * SCALE
        key = lax.broadcasted_iota(jnp.int32, s.shape, 0)
        row = lax.broadcasted_iota(jnp.int32, s.shape, 1)
        row = jnp.where(row >= rows, row - rows, row) + hidden_from
        s = jnp.where(key < row, s, jnp.float32(-1e30)).reshape(rows // 8, 8, width)
        old = peak[:, at]
        new = jnp.maximum(old, jnp.max(jnp.max(s, axis=0), axis=0, keepdims=True))
        shrink = jnp.exp2(old - new)
        w = jnp.exp2(s - new[None])
        update = jnp.dot(
            kvbuf[j].reshape(WIDE, rows)[:LAT], w.reshape(rows, width).astype(jnp.bfloat16),
            preferred_element_type=jnp.float32,
        )
        peak[:, at] = new
        total[:, at] = total[:, at] * shrink + jnp.sum(w, axis=0)
        grown = acc[:, at].reshape(LAT // 8, 8, width) * shrink[None]
        acc[:, at] = grown.reshape(LAT, width) + update

    def slot_of(e, core_):
        n = jnp.where(e >= 4, e - 4, e)
        dx = jnp.where(n == 2, 3, jnp.where(n == 3, 2, n))
        return outer_of(wrap(x + dx, NX), jnp.where(e >= 4, 1 - yh, yh), core_)

    def goes_far(e, k):
        return e <= 1

    def goes_up(e, k):
        return (e == 0) | (e == 4) | ((e == 2) & (k == 0))

    def goes_down(e, k):
        return (e == 0) | (e == 5) | ((e == 1) & (k == 1))

    def v_copy(e, k, send_sem, target):
        slot = slot_of(e, core)
        piece = vbuf.at[slot, k]
        return pltpu.make_async_remote_copy(
            src_ref=piece, dst_ref=piece, send_sem=send_sem,
            recv_sem=v_recv.at[slot, k], device_id=target, device_id_type=MESH,
        )

    def v_sends(e, k, act):
        @pl.when(goes_far(e, k))
        def _():
            act(v_copy(e, k, send_c.at[e, k], y_far))

        @pl.when(goes_up(e, k))
        def _():
            act(v_copy(e, k, send_x.at[e, k, 0], x_up))

        @pl.when(goes_down(e, k))
        def _():
            act(v_copy(e, k, send_x.at[e, k, 1], x_down))

        act(v_copy(e, k, sib_v.at[e, k], sibling))

    def v_arrived(slot, k):
        piece = vbuf.at[slot, k]
        pltpu.make_async_remote_copy(
            src_ref=piece, dst_ref=piece, send_sem=send_c.at[0, 0],
            recv_sem=v_recv.at[slot, k], device_id=sibling, device_id_type=MESH,
        ).wait_recv()

    def finish(pair):
        def one(n):
            h = 2 * pair + n
            at = pl.ds(pl.multiple_of(h * rows, rows), rows)
            whole = jnp.sum(total[:, at], axis=0, keepdims=True)
            latent_out = (acc[:, at] * (1.0 / whole)).astype(jnp.bfloat16)
            vbuf[o, pair, pl.ds(pl.multiple_of(n * VDIM, VDIM), VDIM), :] = jnp.dot(
                vu[h].T, latent_out, preferred_element_type=jnp.float32
            ).astype(jnp.bfloat16)

        loop(0, 2, one)

    def project(e):
        def one(core_):
            depth = heads * VDIM
            slot = slot_of(e, core_)
            start = pl.multiple_of(slot * depth, depth)
            mix[...] += jnp.dot(
                wo[:, pl.ds(start, depth)], vbuf[slot].reshape(depth, rows),
                preferred_element_type=jnp.float32,
            )

        loop(0, 2, one)

    locals_[0].wait()
    relay_a(0, 0)

    for n in (1, 2, 3):
        locals_[n].wait()
    qr_across[...] = qr[...].T
    loop(0, heads, absorb)
    relay_a(0, 1)

    peak[...] = jnp.full_like(peak, -1e30)
    total[...] = jnp.zeros_like(total)

    def clear(n):
        at = pl.ds(pl.multiple_of(n * 32, 32), 32)
        acc[at, :] = jnp.zeros((32, heads * rows), jnp.float32)

    loop(0, LAT // 32, clear)

    def clear_mix(n):
        at = pl.ds(pl.multiple_of(n * 64, 64), 64)
        mix[at, :] = jnp.zeros((64, rows), jnp.float32)

    loop(0, mix.shape[0] // 64, clear_mix)
    locals_[4].wait()

    def hop(d):
        def half_step(k):
            @pl.when((d >= 1) & (d <= 4))
            def _():
                relay_a(d, k)

            def group(ab):
                @pl.when((ab == 1) & (yl == 1) & (d >= 1) & (d <= 5))
                def _():
                    relay_b(d - 1, k)

                dd = d - 1 - ab
                far_end = wrap(z + 4, NZ)
                first, final = (d == 0) & (k == 0) & (ab == 0), (d == 6) & (k == 0) & (ab == 0)
                j = jnp.where(ab == 0, first_a, 0) + wrap(jnp.where(k == 0, z + NZ - dd, z + dd), NZ)
                j = jnp.where(first, i, jnp.where(final, far_end, j))
                middle = (d <= 5) & (dd >= 1) & (dd <= 3)
                in_a = (ab == 0) & (middle | ((d == 5) & (k == 0) & (yl == 1)))
                in_b = (ab == 1) & (yl == 1) & (middle | ((d == 2) & (k == 0)))
                other = (in_a | in_b | final) & (j < i)

                @pl.when(other)
                def _():
                    for part in range(2):
                        kv_arrived(j, others + part)

                @pl.when(other | first)
                def _():
                    keys[...] = kvbuf[j].reshape(WIDE, rows).T

                @pl.when(other | first | final)
                def _():
                    def each(pair):
                        @pl.when(other | first)
                        def _():
                            attend(j, pair, jnp.where(first, 1, 2 * rows))

                        @pl.when(final)
                        def _():
                            finish(pair)
                            v_sends(0, pair, lambda copy: copy.start())

                    loop(0, 2, each)

            loop(0, 2, group)

        loop(0, 2, half_step)

    loop(0, 7, hop)

    order = (
        (1, 0, None), (2, 0, None), (4, 0, 0), (1, 1, None), (2, 1, None), (4, 1, 1), (3, 0, None), (5, 0, None),
        (3, 1, 2), (6, 0, None), (5, 1, 3), (6, 1, 4), (7, 0, 5), (7, 1, 6), (None, None, 7),
    )
    locals_[5].wait()

    def event(m):
        e, k, done = 0, 0, -1
        for n, (e_, k_, done_) in enumerate(order):
            if e_ is not None:
                e, k = jnp.where(m == n, e_, e), jnp.where(m == n, k_, k)
            if done_ is not None:
                done = jnp.where(m == n, done_, done)

        @pl.when(m < len(order) - 1)
        def _():
            v_arrived(slot_of(e, core), k)
            v_sends(e, k, lambda copy: copy.start())

        @pl.when(done >= 0)
        def _():
            loop(0, 2, lambda k: v_arrived(slot_of(done, 1 - core), k))
            project(done)

    loop(0, len(order), event)
    out_ref[...] = mix[...].astype(jnp.bfloat16)

    loop(0, 8, lambda e: loop(0, 2, lambda k: v_sends(e, k, lambda copy: copy.wait_send())))

    def drain(d, k, side):
        zz = ring(d, side)
        j = first_a + zz
        here = held(d, side, k)

        @pl.when(z_forwards(d, side, k))
        def _():
            z_send(j, d, side, k).wait_send()

        @pl.when(here & (yl == 0))
        def _():
            y_send(j, d, side, k).wait_send()

        @pl.when(here & (j < i))
        def _():
            sib_a_send(j, d, side, k).wait_send()

        @pl.when(here & (yl == 1))
        def _():
            sib_b_send(zz, d, side, k).wait_send()

    loop(0, 5, lambda d: loop(0, 2, lambda k: loop(0, 2, lambda side: drain(d, k, side))))


def on_device(q_nope, q_rope, absorb_key, kv_latent, value_up, out_proj):
    rows = q_nope.shape[0]
    heads = absorb_key.shape[0]
    columns = out_proj.shape[1]
    kv_parts = kv_latent.T.reshape(4, WIDE // 4, rows)
    out_proj = out_proj.T
    dma = pltpu.SemaphoreType.DMA
    mixed = pl.pallas_call(
        kernel,
        out_shape=jax.ShapeDtypeStruct((columns, rows), jnp.bfloat16),
        in_specs=[pl.BlockSpec(memory_space=pl.ANY)] * 6,
        out_specs=pl.BlockSpec(memory_space=pltpu.VMEM),
        scratch_shapes=[
            pltpu.VMEM(q_nope.shape, jnp.bfloat16),
            pltpu.VMEM(q_rope.shape, jnp.bfloat16),
            pltpu.VMEM(absorb_key.shape, jnp.bfloat16),
            pltpu.VMEM(value_up.shape, jnp.bfloat16),
            pltpu.VMEM(out_proj.shape, jnp.bfloat16),
            pltpu.VMEM((16, 4, WIDE // 4, rows), jnp.bfloat16),
            pltpu.VMEM((16, 2, heads * VDIM // 2, rows), jnp.bfloat16),
            pltpu.VMEM((WIDE, heads * rows), jnp.bfloat16),
            pltpu.VMEM((heads * ROPE, rows), jnp.bfloat16),
            pltpu.VMEM((rows, WIDE), jnp.bfloat16),
            pltpu.VMEM((8, heads * rows), jnp.float32),
            pltpu.VMEM((8, heads * rows), jnp.float32),
            pltpu.VMEM((LAT, heads * rows), jnp.float32),
            pltpu.VMEM((columns, rows), jnp.float32),
            dma((6,)),
            dma((16, 4)),
            dma((2, 4, 2)),
            dma((2, 5, 2)),
            dma((2, 5, 2)),
            dma((2, 5, 2)),
            dma((16, 2)),
            dma((8, 2, 2)),
            dma((2, 2)),
            dma((8, 2)),
        ],
        compiler_params=pltpu.CompilerParams(
            collective_id=0, has_side_effects=True, vmem_limit_bytes=56 * 1024 * 1024
        ),
        cost_estimate=pl.CostEstimate(
            flops=12 * 10**9, bytes_accessed=10 * 10**6, transcendentals=4 * 10**6
        ),
    )(q_nope, q_rope, absorb_key, kv_parts, value_up, out_proj)
    return mixed.T


def solution(mesh):
    placed = (
        P("inner", "outer"),
        P("inner", "outer"),
        P("outer", None, None),
        P("inner", None),
        P("outer", None, None),
        P(None, "outer"),
    )
    return jax.shard_map(
        on_device, mesh=mesh, in_specs=placed, out_specs=P("inner", "outer"), check_vma=False
    )
```

```python
import math

import jax
import jax.numpy as jnp
from jax import lax
from jax.experimental import pallas as pl
from jax.experimental.pallas import tpu as pltpu
from jax.sharding import PartitionSpec as P

NOPE = 128
ROPE = 64
VDIM = 128
LAT = 512
WIDE = LAT + ROPE
MESH = pl.DeviceIdType.MESH
SCALE = math.log2(math.e) / math.sqrt(NOPE + ROPE)
NX, NZ = 4, 8


def div(a, b):
    return a // b if isinstance(a, int) else lax.div(a, b)


def rem(a, b):
    return a % b if isinstance(a, int) else lax.rem(a, b)


def kernel(
    qn_hbm, qr_hbm, ak_hbm, kv_hbm, vu_hbm, wo_hbm, out_ref,
    qn, qr, ak, vu, wo, kvbuf, vbuf, query, peak, total, acc, mix, out_here,
    local_sem, kv_recv, send_z, send_y, sib_a, sib_b, v_recv, send_x, send_c, sib_v, out_sem,
):
    heads, rows = ak.shape[0], qn.shape[0]
    o, i = lax.axis_index("outer"), lax.axis_index("inner")
    core, yh, x = rem(o, 2), rem(div(o, 2), 2), div(o, 4)
    yl, z = div(i, NZ), rem(i, NZ)

    def outer_of(x_, yh_, core_):
        return (x_ * 2 + yh_) * 2 + core_

    def wrap(n, size):
        return jnp.where(n >= size, n - size, n)

    sibling = (outer_of(x, yh, 1 - core), i)
    z_up = (o, yl * NZ + wrap(z + 1, NZ))
    z_down = (o, yl * NZ + wrap(z + NZ - 1, NZ))
    y_up = (outer_of(x, wrap(yh + yl, 2), core), (1 - yl) * NZ + z)
    y_down = (outer_of(x, wrap(yh + 1 - yl, 2), core), (1 - yl) * NZ + z)
    y_far = (outer_of(x, 1 - yh, core), i)
    x_up = (outer_of(wrap(x + 1, NX), yh, core), i)
    x_down = (outer_of(wrap(x + NX - 1, NX), yh, core), i)

    locals_ = [
        pltpu.make_async_copy(kv_hbm.at[part], kvbuf.at[i, part], local_sem.at[part])
        for part in range(4)
    ]
    for n, (src, dst) in enumerate(
        [(qn_hbm, qn), (ak_hbm, ak), (qr_hbm, qr), (vu_hbm, vu), (wo_hbm, wo)]
    ):
        locals_.append(pltpu.make_async_copy(src, dst, local_sem.at[4 + n]))
    barrier = pltpu.get_barrier_semaphore()
    partners = (sibling, z_up, z_down, y_up, y_down, y_far, x_up, x_down)
    for partner in partners:
        pl.semaphore_signal(barrier, inc=1, device_id=partner, device_id_type=MESH)
    for copy in locals_:
        copy.start()
    pl.semaphore_wait(barrier, len(partners))

    mine, others = 2 * core, 2 * (1 - core)

    def kv_copy(j, k, send_sem, target):
        piece = kvbuf.at[j, mine + k]
        return pltpu.make_async_remote_copy(
            src_ref=piece, dst_ref=piece, send_sem=send_sem,
            recv_sem=kv_recv.at[j, mine + k], device_id=target, device_id_type=MESH,
        )

    def kv_arrived(j, part):
        piece = kvbuf.at[j, part]
        pltpu.make_async_remote_copy(
            src_ref=piece, dst_ref=piece, send_sem=send_z.at[0, 0, 0],
            recv_sem=kv_recv.at[j, part], device_id=sibling, device_id_type=MESH,
        ).wait_recv()

    def ring(d, side):
        return wrap(z + (d if side else NZ - d), NZ)

    def z_forwards(d, side, k):
        return (d <= 2) | ((d == 3) & (k == side))

    def held_a(d, side, k):
        return (d <= 3) | ((d == 4) & (k == side))

    def held_b(d, side, k):
        return (d <= 3) | ((d == 4) & (k == side))

    first_a = yl * NZ

    def z_send(j, d, side, k):
        return kv_copy(j, k, send_z.at[side, d, k], (z_up, z_down)[side])

    o_far = outer_of(x, 1 - yh, core)

    def y_send(j, d, side, k):
        return kv_copy(j, k, send_y.at[side, d, k], (jnp.where(k == 0, o, o_far), NZ + z))

    def sib_a_send(j, d, side, k):
        return kv_copy(j, k, sib_a.at[side, d, k], sibling)

    def sib_b_send(j, d, side, k):
        return kv_copy(j, k, sib_b.at[side, d, k], sibling)

    def relay_a(d, k):
        for side in range(2):
            @pl.when(held_a(d, side, k))
            def _():
                j = first_a + ring(d, side)
                kv_arrived(j, mine + k)

                @pl.when(z_forwards(d, side, k))
                def _():
                    z_send(j, d, side, k).start()

                @pl.when(yl == 0)
                def _():
                    y_send(j, d, side, k).start()

                @pl.when(j < i)
                def _():
                    sib_a_send(j, d, side, k).start()

    def relay_b(d, k):
        @pl.when(d == 0)
        def _():
            kv_arrived(z, mine + k)
            sib_b_send(z, 0, 0, k).start()

        for side in range(2):
            @pl.when((d >= 1) & held_b(d, side, k))
            def _():
                j = ring(d, side)
                kv_arrived(j, mine + k)
                sib_b_send(j, d, side, k).start()

    for part in range(4):
        locals_[part].wait()

    def own(k):
        for side in range(2):
            z_send(i, 0, side, k).start()

        @pl.when(yl == 0)
        def _():
            y_send(i, 0, 0, k).start()

    own(0)

    locals_[4].wait()
    locals_[5].wait()
    locals_[6].wait()
    qr_across = qr[...].T
    for h in range(heads):
        at = slice(h * rows, (h + 1) * rows)
        query[:LAT, at] = jnp.dot(
            qn[:, h * NOPE : (h + 1) * NOPE], ak[h], preferred_element_type=jnp.float32
        ).astype(jnp.bfloat16).T
        query[LAT:, at] = qr_across[h * ROPE : (h + 1) * ROPE]

    def attend(j, first, pairs):
        latent = kvbuf[j].reshape(WIDE, rows)
        keys = latent.T
        width = 2 * rows

        def scores(pair):
            at = slice(pair * width, (pair + 1) * width)
            s = jnp.dot(keys, query[:, at], preferred_element_type=jnp.float32) * SCALE
            if first:
                key = lax.broadcasted_iota(jnp.int32, s.shape, 0)
                row = lax.broadcasted_iota(jnp.int32, s.shape, 1)
                s = jnp.where(key <= jnp.where(row >= rows, row - rows, row), s, jnp.float32(-1e30))
            return s.reshape(rows // 8, 8, width)

        def fold(pair, s):
            at = slice(pair * width, (pair + 1) * width)
            top = jnp.max(jnp.max(s, axis=0), axis=0, keepdims=True)
            if first:
                new = jnp.broadcast_to(top, (8, width))
            else:
                old = peak[:, at]
                new = jnp.maximum(old, top)
            w = jnp.exp2(s - new[None])
            part = jnp.sum(w, axis=0)
            update = jnp.dot(
                latent[:LAT], w.reshape(rows, width).astype(jnp.bfloat16),
                preferred_element_type=jnp.float32,
            )
            peak[:, at] = new
            if first:
                total[:, at] = part
                acc[:, at] = update
            else:
                shrink = jnp.exp2(old - new)
                total[:, at] = total[:, at] * shrink + part
                grown = acc[:, at].reshape(LAT // 8, 8, width) * shrink[None]
                acc[:, at] = grown.reshape(LAT, width) + update

        s = [scores(pair) for pair in pairs]
        for pair, pair_scores in zip(pairs, s):
            fold(pair, pair_scores)

    own(1)
    attend(i, True, (0, 1))

    def swapped(j):
        for k in range(2):
            kv_arrived(j, others + k)

    def hop(d, carry):
        def half_step(k, carry):
            @pl.when(d <= 4)
            def _():
                relay_a(d, k)

            def group(ab, carry):
                @pl.when((ab == 1) & (yl == 1))
                def _():
                    relay_b(d - 1, k)

                dd = d - 1 - ab
                j = jnp.where(ab == 0, first_a, 0) + wrap(jnp.where(k == 0, z + NZ - dd, z + dd), NZ)
                in_a = (ab == 0) & (((dd >= 1) & (dd <= 3)) | ((dd == 4) & (k == 0) & (yl == 1)))
                in_b = (ab == 1) & (yl == 1) & (((dd >= 1) & (dd <= 3)) | ((dd == 0) & (k == 0)))

                @pl.when((in_a | in_b) & (j < i))
                def _():
                    swapped(j)
                    attend(j, False, (0, 1))

                return carry

            return lax.fori_loop(0, 2, group, carry)

        return lax.fori_loop(0, 2, half_step, carry)

    lax.fori_loop(1, 6, hop, 0)
    last = wrap(z + 4, NZ)

    own_slots, sib_slots = [], []
    for there in (yh, 1 - yh):
        for dx in (0, 1, 3, 2):
            place = outer_of(wrap(x + dx, NX), there, 0)
            own_slots.append(place + core)
            sib_slots.append(place + 1 - core)

    def v_arrived(slot, k):
        piece = vbuf.at[slot, k]
        pltpu.make_async_remote_copy(
            src_ref=piece, dst_ref=piece, send_sem=send_c.at[0, 0],
            recv_sem=v_recv.at[slot, k], device_id=sibling, device_id_type=MESH,
        ).wait_recv()

    locals_[7].wait()

    def send(e, k, way):
        sem = {
            "far": lambda: send_c.at[e, k], "up": lambda: send_x.at[e, k, 0],
            "down": lambda: send_x.at[e, k, 1], "sib": lambda: sib_v.at[e, k],
        }[way]()
        target = {"far": y_far, "up": x_up, "down": x_down, "sib": sibling}[way]
        piece = vbuf.at[own_slots[e], k]
        return pltpu.make_async_remote_copy(
            src_ref=piece, dst_ref=piece, send_sem=sem,
            recv_sem=v_recv.at[own_slots[e], k], device_id=target, device_id_type=MESH,
        )

    for k in range(2):
        pair = (2 * k, 2 * k + 1)

        @pl.when(last < i)
        def _():
            if k == 0:
                swapped(last)
            attend(last, False, (k,))

        for h in pair:
            at = slice(h * rows, (h + 1) * rows)
            whole = jnp.sum(total[:, at], axis=0, keepdims=True)
            latent_out = (acc[:, at] * (1.0 / whole)).astype(jnp.bfloat16)
            vbuf[o, h] = jnp.dot(
                vu[h].T, latent_out, preferred_element_type=jnp.float32
            ).astype(jnp.bfloat16)
            for way in ("up", "down", "far", "sib"):
                send(0, h, way).start()

    for k in range(2):
        for side in range(2):
            z_send(i, 0, side, k).wait_send()

        @pl.when(yl == 0)
        def _():
            y_send(i, 0, 0, k).wait_send()

        @pl.when(yl == 1)
        def _():
            sib_b_send(z, 0, 0, k).wait_send()

    def drain(d, carry):
        for k in range(2):
            for side in range(2):
                @pl.when(held_a(d, side, k))
                def _():
                    zz = ring(d, side)
                    j = first_a + zz

                    @pl.when(z_forwards(d, side, k))
                    def _():
                        z_send(j, d, side, k).wait_send()

                    @pl.when(yl == 0)
                    def _():
                        y_send(j, d, side, k).wait_send()

                    @pl.when(j < i)
                    def _():
                        sib_a_send(j, d, side, k).wait_send()

                    @pl.when(yl == 1)
                    def _():
                        sib_b_send(zz, d, side, k).wait_send()

        return carry

    lax.fori_loop(1, 5, drain, 0)

    mix[...] = jnp.zeros_like(mix)

    def project(slots):
        depth = heads * VDIM
        term = mix[...]
        for slot in slots:
            start = pl.multiple_of(slot * depth, depth)
            term = term + jnp.dot(
                wo[:, pl.ds(start, depth)], vbuf[slot].reshape(depth, rows),
                preferred_element_type=jnp.float32,
            )
        mix[...] = term

    def near(k):
        if k % 2 == 0:
            return ((1, k, "far"), (2, k, "up"), (4, k, "up"))
        return ((2, k, "far"), (1, k, "down"), (4, k, "down"))

    def middle(k):
        if k < 2:
            return ((3, k, "far"), (5 + k % 2, k))
        return ((3, k), (5 + k % 2, k, ("up" if k % 2 else "down")))

    steps = (
        (near(0) + near(1), None),
        (near(2) + near(3), 0),
        (middle(0) + middle(1), None),
        (middle(2) + middle(3), 1),
        ((), 2),
        (((6, 0), (5, 1), (6, 2), (5, 3)), 3),
        ((), 4),
        (((7, 0), (7, 1)), 5),
        ((), 6),
        (((7, 2), (7, 3)), 7),
    )

    def event(t, carry):
        for n, (items, _) in enumerate(steps):
            if items:
                @pl.when(t == n)
                def _():
                    for e, k, *ways in items:
                        v_arrived(own_slots[e], k)
                        for way in (*ways, "sib"):
                            send(e, k, way).start()

        @pl.when(t == 0)
        def _():
            locals_[8].wait()

        @pl.when((t != 0) & (t != 2))
        def _():
            own_slot, sib_slot = own_slots[0], sib_slots[0]
            for n, (_, e) in enumerate(steps):
                if e:
                    own_slot = jnp.where(t == n, own_slots[e], own_slot)
                    sib_slot = jnp.where(t == n, sib_slots[e], sib_slot)
            for k in range(heads):
                v_arrived(sib_slot, k)
            project((own_slot, sib_slot))

        return carry

    lax.fori_loop(0, len(steps), event, 0)
    out_here[...] = mix[...].astype(jnp.bfloat16)
    out_copy = pltpu.make_async_copy(out_here, out_ref, out_sem.at[0])
    out_copy.start()

    for k in range(heads):
        for way in ("up", "down", "far", "sib"):
            send(0, k, way).wait_send()
    for items, _ in steps:
        for e, k, *ways in items:
            for way in (*ways, "sib"):
                send(e, k, way).wait_send()
    out_copy.wait()


def on_device(q_nope, q_rope, absorb_key, kv_latent, value_up, out_proj):
    rows = q_nope.shape[0]
    heads = absorb_key.shape[0]
    columns = out_proj.shape[1]
    kv_parts = kv_latent.T.reshape(4, WIDE // 4, rows)
    out_proj = out_proj.T
    dma = pltpu.SemaphoreType.DMA
    mixed = pl.pallas_call(
        kernel,
        out_shape=jax.ShapeDtypeStruct((columns, rows), jnp.bfloat16),
        in_specs=[pl.BlockSpec(memory_space=pl.ANY)] * 6,
        out_specs=pl.BlockSpec(memory_space=pl.ANY),
        scratch_shapes=[
            pltpu.VMEM(q_nope.shape, jnp.bfloat16),
            pltpu.VMEM(q_rope.shape, jnp.bfloat16),
            pltpu.VMEM(absorb_key.shape, jnp.bfloat16),
            pltpu.VMEM(value_up.shape, jnp.bfloat16),
            pltpu.VMEM(out_proj.shape, jnp.bfloat16),
            pltpu.VMEM((16, 4, WIDE // 4, rows), jnp.bfloat16),
            pltpu.VMEM((16, heads, VDIM, rows), jnp.bfloat16),
            pltpu.VMEM((WIDE, heads * rows), jnp.bfloat16),
            pltpu.VMEM((8, heads * rows), jnp.float32),
            pltpu.VMEM((8, heads * rows), jnp.float32),
            pltpu.VMEM((LAT, heads * rows), jnp.float32),
            pltpu.VMEM((columns, rows), jnp.float32),
            pltpu.VMEM((columns, rows), jnp.bfloat16),
            dma((9,)),
            dma((16, 4)),
            dma((2, 4, 2)),
            dma((2, 5, 2)),
            dma((2, 5, 2)),
            dma((2, 5, 2)),
            dma((16, heads)),
            dma((8, heads, 2)),
            dma((4, heads)),
            dma((8, heads)),
            dma((1,)),
        ],
        compiler_params=pltpu.CompilerParams(
            collective_id=0, has_side_effects=True, vmem_limit_bytes=56 * 1024 * 1024
        ),
        cost_estimate=pl.CostEstimate(
            flops=12 * 10**9, bytes_accessed=10 * 10**6, transcendentals=4 * 10**6
        ),
    )(q_nope, q_rope, absorb_key, kv_parts, value_up, out_proj)
    return mixed.T


def solution(mesh):
    placed = (
        P("inner", "outer"),
        P("inner", "outer"),
        P("outer", None, None),
        P("inner", None),
        P("outer", None, None),
        P(None, "outer"),
    )
    return jax.shard_map(
        on_device, mesh=mesh, in_specs=placed, out_specs=P("inner", "outer"), check_vma=False
    )
```

```python
import math

import jax
import jax.numpy as jnp
from jax import lax
from jax.experimental import pallas as pl
from jax.experimental.pallas import tpu as pltpu
from jax.sharding import PartitionSpec as P

NOPE = 128
ROPE = 64
VDIM = 128
LAT = 512
WIDE = LAT + ROPE
MESH = pl.DeviceIdType.MESH
SCALE = math.log2(math.e) / math.sqrt(NOPE + ROPE)
NX, NZ = 4, 8


def div(a, b):
    return a // b if isinstance(a, int) else lax.div(a, b)


def rem(a, b):
    return a % b if isinstance(a, int) else lax.rem(a, b)


def kernel(
    qn_hbm, qr_hbm, ak_hbm, kv_hbm, vu_hbm, wo_hbm, out_ref,
    qn, qr, ak, vu, wo, kvbuf, vbuf, query, peak, total, acc, mix,
    local_sem, kv_recv, send_z, send_y, sib_a, sib_b, v_recv, send_x, send_c, sib_v,
):
    heads, rows = ak.shape[0], qn.shape[0]
    o, i = lax.axis_index("outer"), lax.axis_index("inner")
    core, yh, x = rem(o, 2), rem(div(o, 2), 2), div(o, 4)
    yl, z = div(i, NZ), rem(i, NZ)

    def outer_of(x_, yh_, core_):
        return (x_ * 2 + yh_) * 2 + core_

    def wrap(n, size):
        return jnp.where(n >= size, n - size, n)

    sibling = (outer_of(x, yh, 1 - core), i)
    z_up = (o, yl * NZ + wrap(z + 1, NZ))
    z_down = (o, yl * NZ + wrap(z + NZ - 1, NZ))
    y_up = (outer_of(x, wrap(yh + yl, 2), core), (1 - yl) * NZ + z)
    y_down = (outer_of(x, wrap(yh + 1 - yl, 2), core), (1 - yl) * NZ + z)
    y_far = (outer_of(x, 1 - yh, core), i)
    x_up = (outer_of(wrap(x + 1, NX), yh, core), i)
    x_down = (outer_of(wrap(x + NX - 1, NX), yh, core), i)

    locals_ = [
        pltpu.make_async_copy(kv_hbm.at[part], kvbuf.at[i, part], local_sem.at[part])
        for part in range(4)
    ]
    for n, (src, dst) in enumerate(
        [(qn_hbm, qn), (ak_hbm, ak), (qr_hbm, qr), (vu_hbm, vu), (wo_hbm, wo)]
    ):
        locals_.append(pltpu.make_async_copy(src, dst, local_sem.at[4 + n]))
    for copy in locals_:
        copy.start()

    barrier = pltpu.get_barrier_semaphore()
    partners = (sibling, z_up, z_down, y_up, y_down, y_far, x_up, x_down)
    for partner in partners:
        pl.semaphore_signal(barrier, inc=1, device_id=partner, device_id_type=MESH)
    pl.semaphore_wait(barrier, len(partners))

    mine, others = 2 * core, 2 * (1 - core)

    def kv_copy(j, k, send_sem, target):
        piece = kvbuf.at[j, mine + k]
        return pltpu.make_async_remote_copy(
            src_ref=piece, dst_ref=piece, send_sem=send_sem,
            recv_sem=kv_recv.at[j, mine + k], device_id=target, device_id_type=MESH,
        )

    def kv_arrived(j, part):
        piece = kvbuf.at[j, part]
        pltpu.make_async_remote_copy(
            src_ref=piece, dst_ref=piece, send_sem=send_z.at[0, 0, 0],
            recv_sem=kv_recv.at[j, part], device_id=sibling, device_id_type=MESH,
        ).wait_recv()

    def ring(d, side):
        return wrap(z + (d if side else NZ - d), NZ)

    def z_forwards(d, side, k, src):
        late = (
            (src <= 2) & ((d <= 2) | ((d == 3) & (src == 0) & (k == 1)))
            if side
            else (z < NZ - 1) & ((d <= 2) | ((d == 3) & ((src > 0) | (k == 0))))
        )
        return ((yl == 0) & ((d <= 2) | ((d == 3) & (k == side)))) | ((yl == 1) & late)

    def held_a(d, side, k, src):
        late = (
            (src <= 2) & ((d <= 3) | ((d == 4) & (src == 0) & (k == 1)))
            if side
            else (z >= d) & ((d <= 3) | ((d == 4) & ((src > 0) | (k == 0))))
        )
        return ((yl == 0) & held_b(d, side, k)) | ((yl == 1) & late)

    def held_b(d, side, k):
        return (d <= 3) | ((d == 4) & (k == side))

    first_a = yl * NZ

    def z_send(j, d, side, k):
        return kv_copy(j, k, send_z.at[side, d, k], (z_up, z_down)[side])

    o_far = outer_of(x, 1 - yh, core)

    def y_send(j, d, side, k):
        return kv_copy(j, k, send_y.at[side, d, k], (jnp.where(k == 0, o, o_far), NZ + z))

    def sib_a_send(j, d, side, k):
        return kv_copy(j, k, sib_a.at[side, d, k], sibling)

    def sib_b_send(j, d, side, k):
        return kv_copy(j, k, sib_b.at[side, d, k], sibling)

    def relay_a(d, k):
        for side in range(2):
            src = ring(d, side)

            @pl.when(held_a(d, side, k, src))
            def _():
                j = first_a + src
                kv_arrived(j, mine + k)

                @pl.when(z_forwards(d, side, k, src))
                def _():
                    z_send(j, d, side, k).start()

                @pl.when(yl == 0)
                def _():
                    y_send(j, d, side, k).start()

                @pl.when(j < i)
                def _():
                    sib_a_send(j, d, side, k).start()

    def relay_b(d, k):
        @pl.when(d == 0)
        def _():
            kv_arrived(z, mine + k)
            sib_b_send(z, 0, 0, k).start()

        for side in range(2):
            @pl.when((d >= 1) & held_b(d, side, k))
            def _():
                j = ring(d, side)
                kv_arrived(j, mine + k)
                sib_b_send(j, d, side, k).start()

    for part in range(4):
        locals_[part].wait()

    def own(k):
        for side in range(2):
            @pl.when(z_forwards(0, side, k, z))
            def _():
                z_send(i, 0, side, k).start()

        @pl.when(yl == 0)
        def _():
            y_send(i, 0, 0, k).start()

    own(0)

    locals_[4].wait()
    locals_[5].wait()
    locals_[6].wait()
    qr_across = qr[...].T
    for h in range(heads):
        at = slice(h * rows, (h + 1) * rows)
        query[:LAT, at] = jnp.dot(
            qn[:, h * NOPE : (h + 1) * NOPE], ak[h], preferred_element_type=jnp.float32
        ).astype(jnp.bfloat16).T
        query[LAT:, at] = qr_across[h * ROPE : (h + 1) * ROPE]

    def attend(j, first, pairs):
        latent = kvbuf[j].reshape(WIDE, rows)
        keys = latent.T
        width = 2 * rows

        def scores(pair):
            at = slice(pair * width, (pair + 1) * width)
            s = jnp.dot(keys, query[:, at], preferred_element_type=jnp.float32) * SCALE
            if first:
                key = lax.broadcasted_iota(jnp.int32, s.shape, 0)
                row = lax.broadcasted_iota(jnp.int32, s.shape, 1)
                s = jnp.where(key <= jnp.where(row >= rows, row - rows, row), s, jnp.float32(-1e30))
            return s.reshape(rows // 8, 8, width)

        def fold(pair, s):
            at = slice(pair * width, (pair + 1) * width)
            top = jnp.max(jnp.max(s, axis=0), axis=0, keepdims=True)
            if first:
                new = jnp.broadcast_to(top, (8, width))
            else:
                old = peak[:, at]
                new = jnp.maximum(old, top)
            w = jnp.exp2(s - new[None])
            part = jnp.sum(w, axis=0)
            update = jnp.dot(
                latent[:LAT], w.reshape(rows, width).astype(jnp.bfloat16),
                preferred_element_type=jnp.float32,
            )
            peak[:, at] = new
            if first:
                total[:, at] = part
                acc[:, at] = update
            else:
                shrink = jnp.exp2(old - new)
                total[:, at] = total[:, at] * shrink + part
                grown = acc[:, at].reshape(LAT // 8, 8, width) * shrink[None]
                acc[:, at] = grown.reshape(LAT, width) + update

        s = [scores(pair) for pair in pairs]
        for pair, pair_scores in zip(pairs, s):
            fold(pair, pair_scores)

    own(1)
    attend(i, True, (0, 1))

    def swapped(j):
        for k in range(2):
            kv_arrived(j, others + k)

    def hop(d, carry):
        def half_step(k, carry):
            @pl.when(d <= 4)
            def _():
                relay_a(d, k)

            def group(ab, carry):
                @pl.when((ab == 1) & (yl == 1))
                def _():
                    relay_b(d - 1, k)

                dd = d - 1 - ab
                j = jnp.where(ab == 0, first_a, 0) + wrap(jnp.where(k == 0, z + NZ - dd, z + dd), NZ)
                in_a = (ab == 0) & (((dd >= 1) & (dd <= 3)) | ((dd == 4) & (k == 0) & (yl == 1)))
                in_b = (ab == 1) & (yl == 1) & (((dd >= 1) & (dd <= 3)) | ((dd == 0) & (k == 0)))

                @pl.when((in_a | in_b) & (j < i))
                def _():
                    swapped(j)
                    attend(j, False, (0, 1))

                return carry

            return lax.fori_loop(0, 2, group, carry)

        return lax.fori_loop(0, 2, half_step, carry)

    lax.fori_loop(1, 6, hop, 0)
    last = wrap(z + 4, NZ)

    own_slots, sib_slots = [], []
    for there in (yh, 1 - yh):
        for dx in (0, 1, 3, 2):
            place = outer_of(wrap(x + dx, NX), there, 0)
            own_slots.append(place + core)
            sib_slots.append(place + 1 - core)

    def v_arrived(slot, k):
        piece = vbuf.at[slot, k]
        pltpu.make_async_remote_copy(
            src_ref=piece, dst_ref=piece, send_sem=send_c.at[0, 0],
            recv_sem=v_recv.at[slot, k], device_id=sibling, device_id_type=MESH,
        ).wait_recv()

    locals_[7].wait()

    def send(e, k, way):
        sem = {
            "far": lambda: send_c.at[e, k], "up": lambda: send_x.at[e, k, 0],
            "down": lambda: send_x.at[e, k, 1], "sib": lambda: sib_v.at[e, k],
        }[way]()
        target = {"far": y_far, "up": x_up, "down": x_down, "sib": sibling}[way]
        piece = vbuf.at[own_slots[e], k]
        return pltpu.make_async_remote_copy(
            src_ref=piece, dst_ref=piece, send_sem=sem,
            recv_sem=v_recv.at[own_slots[e], k], device_id=target, device_id_type=MESH,
        )

    for k in range(2):
        pair = (2 * k, 2 * k + 1)

        @pl.when(last < i)
        def _():
            if k == 0:
                swapped(last)
            attend(last, False, (k,))

        for h in pair:
            at = slice(h * rows, (h + 1) * rows)
            whole = jnp.sum(total[:, at], axis=0, keepdims=True)
            latent_out = (acc[:, at] * (1.0 / whole)).astype(jnp.bfloat16)
            vbuf[o, k, (h % 2) * VDIM : (h % 2 + 1) * VDIM, :] = jnp.dot(
                vu[h].T, latent_out, preferred_element_type=jnp.float32
            ).astype(jnp.bfloat16)
        for way in ("up", "down", "far", "sib"):
            send(0, k, way).start()

    mix[...] = jnp.zeros_like(mix)

    def project(slots):
        depth = heads * VDIM
        term = mix[...]
        for slot in slots:
            start = pl.multiple_of(slot * depth, depth)
            term = term + jnp.dot(
                wo[:, pl.ds(start, depth)], vbuf[slot].reshape(depth, rows),
                preferred_element_type=jnp.float32,
            )
        mix[...] = term

    came = (
        ((1, 0, "far"), (2, 0, "up"), (4, 0, "up")),
        ((1, 1, "down", "far"), (2, 1), (4, 1, "up")),
        ((3, 0), (5, 0, "down"), (3, 1)),
        ((6, 0), (5, 1, "down")),
        ((6, 1),),
        ((7, 0),),
        ((7, 1),),
    )

    def event(t, carry):
        for n, items in enumerate(came):
            @pl.when(t == n)
            def _():
                for e, k, *ways in items:
                    v_arrived(own_slots[e], k)
                    for way in (*ways, "sib"):
                        send(e, k, way).start()

        @pl.when(t == 0)
        def _():
            locals_[8].wait()

        n = jnp.where(t >= 4, t - 4, t)
        dx = jnp.where(n == 2, 3, jnp.where(n == 3, 2, n))
        place = outer_of(wrap(x + dx, NX), jnp.where(t >= 4, 1 - yh, yh), 0)
        for k in range(2):
            v_arrived(place + 1 - core, k)
        project((place + core, place + 1 - core))
        return carry

    lax.fori_loop(0, 8, event, 0)
    out_ref[...] = mix[...].astype(jnp.bfloat16)

    for k in range(2):
        for way in ("up", "down", "far", "sib"):
            send(0, k, way).wait_send()
    for items in came:
        for e, k, *ways in items:
            for way in (*ways, "sib"):
                send(e, k, way).wait_send()

    for k in range(2):
        for side in range(2):
            @pl.when(z_forwards(0, side, k, z))
            def _():
                z_send(i, 0, side, k).wait_send()

        @pl.when(yl == 0)
        def _():
            y_send(i, 0, 0, k).wait_send()

        @pl.when(yl == 1)
        def _():
            sib_b_send(z, 0, 0, k).wait_send()

    def drain(d, carry):
        for k in range(2):
            for side in range(2):
                src = ring(d, side)
                j = first_a + src

                @pl.when(held_a(d, side, k, src))
                def _():
                    @pl.when(z_forwards(d, side, k, src))
                    def _():
                        z_send(j, d, side, k).wait_send()

                    @pl.when(yl == 0)
                    def _():
                        y_send(j, d, side, k).wait_send()

                    @pl.when(j < i)
                    def _():
                        sib_a_send(j, d, side, k).wait_send()

                @pl.when((yl == 1) & held_b(d, side, k))
                def _():
                    sib_b_send(src, d, side, k).wait_send()

        return carry

    lax.fori_loop(1, 5, drain, 0)


def on_device(q_nope, q_rope, absorb_key, kv_latent, value_up, out_proj):
    rows = q_nope.shape[0]
    heads = absorb_key.shape[0]
    columns = out_proj.shape[1]
    kv_parts = kv_latent.T.reshape(4, WIDE // 4, rows)
    out_proj = out_proj.T
    dma = pltpu.SemaphoreType.DMA
    mixed = pl.pallas_call(
        kernel,
        out_shape=pltpu.VMEM((columns, rows), jnp.bfloat16),
        in_specs=[pl.BlockSpec(memory_space=pl.ANY)] * 6,
        out_specs=pl.BlockSpec(memory_space=pltpu.VMEM),
        scratch_shapes=[
            pltpu.VMEM(q_nope.shape, jnp.bfloat16),
            pltpu.VMEM(q_rope.shape, jnp.bfloat16),
            pltpu.VMEM(absorb_key.shape, jnp.bfloat16),
            pltpu.VMEM(value_up.shape, jnp.bfloat16),
            pltpu.VMEM(out_proj.shape, jnp.bfloat16),
            pltpu.VMEM((16, 4, WIDE // 4, rows), jnp.bfloat16),
            pltpu.VMEM((16, 2, heads * VDIM // 2, rows), jnp.bfloat16),
            pltpu.VMEM((WIDE, heads * rows), jnp.bfloat16),
            pltpu.VMEM((8, heads * rows), jnp.float32),
            pltpu.VMEM((8, heads * rows), jnp.float32),
            pltpu.VMEM((LAT, heads * rows), jnp.float32),
            pltpu.VMEM((columns, rows), jnp.float32),
            dma((9,)),
            dma((16, 4)),
            dma((2, 4, 2)),
            dma((2, 5, 2)),
            dma((2, 5, 2)),
            dma((2, 5, 2)),
            dma((16, 2)),
            dma((8, 2, 2)),
            dma((2, 2)),
            dma((8, 2)),
        ],
        compiler_params=pltpu.CompilerParams(
            collective_id=0, has_side_effects=True, vmem_limit_bytes=56 * 1024 * 1024
        ),
        cost_estimate=pl.CostEstimate(
            flops=12 * 10**9, bytes_accessed=10 * 10**6, transcendentals=4 * 10**6
        ),
    )(q_nope, q_rope, absorb_key, kv_parts, value_up, out_proj)
    return mixed.T


def solution(mesh):
    placed = (
        P("inner", "outer"),
        P("inner", "outer"),
        P("outer", None, None),
        P("inner", None),
        P("outer", None, None),
        P(None, "outer"),
    )
    return jax.shard_map(
        on_device, mesh=mesh, in_specs=placed, out_specs=P("inner", "outer"), check_vma=False
    )
```

```python
import math

import jax
import jax.numpy as jnp
from jax import lax
from jax.experimental import pallas as pl
from jax.experimental.pallas import tpu as pltpu
from jax.sharding import PartitionSpec as P

NOPE = 128
ROPE = 64
VDIM = 128
LAT = 512
WIDE = LAT + ROPE
MESH = pl.DeviceIdType.MESH
SCALE = math.log2(math.e) / math.sqrt(NOPE + ROPE)
NX, NZ = 4, 8


def div(a, b):
    return a // b if isinstance(a, int) else lax.div(a, b)


def rem(a, b):
    return a % b if isinstance(a, int) else lax.rem(a, b)


def kernel(
    qn_hbm, qr_hbm, ak_hbm, kv_hbm, vu_hbm, wo_hbm, out_ref,
    qn, qr, ak, vu, wo, kvbuf, vbuf, query, peak, total, acc, mix,
    local_sem, kv_recv, send_z, send_y, sib_a, sib_b, v_recv, send_x, send_c, sib_v,
):
    heads, rows = ak.shape[0], qn.shape[0]
    o, i = lax.axis_index("outer"), lax.axis_index("inner")
    core, yh, x = rem(o, 2), rem(div(o, 2), 2), div(o, 4)
    yl, z = div(i, NZ), rem(i, NZ)

    def outer_of(x_, yh_, core_):
        return (x_ * 2 + yh_) * 2 + core_

    def wrap(n, size):
        return jnp.where(n >= size, n - size, n)

    sibling = (outer_of(x, yh, 1 - core), i)
    z_up = (o, yl * NZ + wrap(z + 1, NZ))
    z_down = (o, yl * NZ + wrap(z + NZ - 1, NZ))
    y_up = (outer_of(x, wrap(yh + yl, 2), core), (1 - yl) * NZ + z)
    y_down = (outer_of(x, wrap(yh + 1 - yl, 2), core), (1 - yl) * NZ + z)
    y_far = (outer_of(x, 1 - yh, core), i)
    x_up = (outer_of(wrap(x + 1, NX), yh, core), i)
    x_down = (outer_of(wrap(x + NX - 1, NX), yh, core), i)

    locals_ = [
        pltpu.make_async_copy(kv_hbm.at[part], kvbuf.at[i, part], local_sem.at[part])
        for part in range(4)
    ]
    for n, (src, dst) in enumerate(
        [(qn_hbm, qn), (ak_hbm, ak), (qr_hbm, qr), (vu_hbm, vu), (wo_hbm, wo)]
    ):
        locals_.append(pltpu.make_async_copy(src, dst, local_sem.at[4 + n]))
    barrier = pltpu.get_barrier_semaphore()
    partners = (sibling, z_up, z_down, y_up, y_down, y_far, x_up, x_down)
    for partner in partners:
        pl.semaphore_signal(barrier, inc=1, device_id=partner, device_id_type=MESH)
    for copy in locals_:
        copy.start()
    pl.semaphore_wait(barrier, len(partners))

    mine, others = 2 * core, 2 * (1 - core)

    def kv_copy(j, k, send_sem, target):
        piece = kvbuf.at[j, mine + k]
        return pltpu.make_async_remote_copy(
            src_ref=piece, dst_ref=piece, send_sem=send_sem,
            recv_sem=kv_recv.at[j, mine + k], device_id=target, device_id_type=MESH,
        )

    def kv_arrived(j, part):
        piece = kvbuf.at[j, part]
        pltpu.make_async_remote_copy(
            src_ref=piece, dst_ref=piece, send_sem=send_z.at[0, 0, 0],
            recv_sem=kv_recv.at[j, part], device_id=sibling, device_id_type=MESH,
        ).wait_recv()

    def ring(d, side):
        return wrap(z + (d if side else NZ - d), NZ)

    def z_forwards(d, side, k, src):
        late = (
            (src <= 2) & ((d <= 2) | ((d == 3) & (src == 0) & (k == 1)))
            if side
            else (z < NZ - 1) & ((d <= 2) | ((d == 3) & ((src > 0) | (k == 0))))
        )
        return ((yl == 0) & ((d <= 2) | ((d == 3) & (k == side)))) | ((yl == 1) & late)

    def held_a(d, side, k, src):
        late = (
            (src <= 2) & ((d <= 3) | ((d == 4) & (src == 0) & (k == 1)))
            if side
            else (z >= d) & ((d <= 3) | ((d == 4) & ((src > 0) | (k == 0))))
        )
        return ((yl == 0) & held_b(d, side, k)) | ((yl == 1) & late)

    def held_b(d, side, k):
        return (d <= 3) | ((d == 4) & (k == side))

    first_a = yl * NZ

    def z_send(j, d, side, k):
        return kv_copy(j, k, send_z.at[side, d, k], (z_up, z_down)[side])

    o_far = outer_of(x, 1 - yh, core)

    def y_send(j, d, side, k):
        return kv_copy(j, k, send_y.at[side, d, k], (jnp.where(k == 0, o, o_far), NZ + z))

    def sib_a_send(j, d, side, k):
        return kv_copy(j, k, sib_a.at[side, d, k], sibling)

    def sib_b_send(j, d, side, k):
        return kv_copy(j, k, sib_b.at[side, d, k], sibling)

    def relay_a(d, k):
        for side in range(2):
            src = ring(d, side)

            @pl.when(held_a(d, side, k, src))
            def _():
                j = first_a + src
                kv_arrived(j, mine + k)

                @pl.when(z_forwards(d, side, k, src))
                def _():
                    z_send(j, d, side, k).start()

                @pl.when(yl == 0)
                def _():
                    y_send(j, d, side, k).start()

                @pl.when(j < i)
                def _():
                    sib_a_send(j, d, side, k).start()

    def relay_b(d, k):
        @pl.when(d == 0)
        def _():
            kv_arrived(z, mine + k)
            sib_b_send(z, 0, 0, k).start()

        for side in range(2):
            @pl.when((d >= 1) & held_b(d, side, k))
            def _():
                j = ring(d, side)
                kv_arrived(j, mine + k)
                sib_b_send(j, d, side, k).start()

    for part in range(4):
        locals_[part].wait()

    def own(k):
        for side in range(2):
            @pl.when(z_forwards(0, side, k, z))
            def _():
                z_send(i, 0, side, k).start()

        @pl.when(yl == 0)
        def _():
            y_send(i, 0, 0, k).start()

    own(0)

    locals_[4].wait()
    locals_[5].wait()
    locals_[6].wait()
    qr_across = qr[...].T
    for h in range(heads):
        at = slice(h * rows, (h + 1) * rows)
        query[:LAT, at] = jnp.dot(
            qn[:, h * NOPE : (h + 1) * NOPE], ak[h], preferred_element_type=jnp.float32
        ).astype(jnp.bfloat16).T
        query[LAT:, at] = qr_across[h * ROPE : (h + 1) * ROPE]

    def attend(j, first, pairs):
        latent = kvbuf[j].reshape(WIDE, rows)
        keys = latent.T
        width = 2 * rows

        def scores(pair):
            at = slice(pair * width, (pair + 1) * width)
            s = jnp.dot(keys, query[:, at], preferred_element_type=jnp.float32) * SCALE
            if first:
                key = lax.broadcasted_iota(jnp.int32, s.shape, 0)
                row = lax.broadcasted_iota(jnp.int32, s.shape, 1)
                s = jnp.where(key <= jnp.where(row >= rows, row - rows, row), s, jnp.float32(-1e30))
            return s.reshape(rows // 8, 8, width)

        def fold(pair, s):
            at = slice(pair * width, (pair + 1) * width)
            top = jnp.max(jnp.max(s, axis=0), axis=0, keepdims=True)
            if first:
                new = jnp.broadcast_to(top, (8, width))
            else:
                old = peak[:, at]
                new = jnp.maximum(old, top)
            w = jnp.exp2(s - new[None])
            part = jnp.sum(w, axis=0)
            update = jnp.dot(
                latent[:LAT], w.reshape(rows, width).astype(jnp.bfloat16),
                preferred_element_type=jnp.float32,
            )
            peak[:, at] = new
            if first:
                total[:, at] = part
                acc[:, at] = update
            else:
                shrink = jnp.exp2(old - new)
                total[:, at] = total[:, at] * shrink + part
                grown = acc[:, at].reshape(LAT // 8, 8, width) * shrink[None]
                acc[:, at] = grown.reshape(LAT, width) + update

        s = [scores(pair) for pair in pairs]
        for pair, pair_scores in zip(pairs, s):
            fold(pair, pair_scores)

    own(1)
    attend(i, True, (0, 1))

    def swapped(j):
        for k in range(2):
            kv_arrived(j, others + k)

    def hop(d, carry):
        def half_step(k, carry):
            @pl.when(d <= 4)
            def _():
                relay_a(d, k)

            def group(ab, carry):
                @pl.when((ab == 1) & (yl == 1))
                def _():
                    relay_b(d - 1, k)

                dd = d - 1 - ab
                j = jnp.where(ab == 0, first_a, 0) + wrap(jnp.where(k == 0, z + NZ - dd, z + dd), NZ)
                in_a = (ab == 0) & (((dd >= 1) & (dd <= 3)) | ((dd == 4) & (k == 0) & (yl == 1)))
                in_b = (ab == 1) & (yl == 1) & (((dd >= 1) & (dd <= 3)) | ((dd == 0) & (k == 0)))

                @pl.when((in_a | in_b) & (j < i))
                def _():
                    swapped(j)
                    attend(j, False, (0, 1))

                return carry

            return lax.fori_loop(0, 2, group, carry)

        return lax.fori_loop(0, 2, half_step, carry)

    lax.fori_loop(1, 6, hop, 0)
    last = wrap(z + 4, NZ)

    own_slots, sib_slots = [], []
    for there in (yh, 1 - yh):
        for dx in (0, 1, 3, 2):
            place = outer_of(wrap(x + dx, NX), there, 0)
            own_slots.append(place + core)
            sib_slots.append(place + 1 - core)

    def v_arrived(slot, k):
        piece = vbuf.at[slot, k]
        pltpu.make_async_remote_copy(
            src_ref=piece, dst_ref=piece, send_sem=send_c.at[0, 0],
            recv_sem=v_recv.at[slot, k], device_id=sibling, device_id_type=MESH,
        ).wait_recv()

    locals_[7].wait()

    def send(e, k, way):
        sem = {
            "far": lambda: send_c.at[e, k], "up": lambda: send_x.at[e, k, 0],
            "down": lambda: send_x.at[e, k, 1], "sib": lambda: sib_v.at[e, k],
        }[way]()
        target = {"far": y_far, "up": x_up, "down": x_down, "sib": sibling}[way]
        piece = vbuf.at[own_slots[e], k]
        return pltpu.make_async_remote_copy(
            src_ref=piece, dst_ref=piece, send_sem=sem,
            recv_sem=v_recv.at[own_slots[e], k], device_id=target, device_id_type=MESH,
        )

    for k in range(2):
        pair = (2 * k, 2 * k + 1)

        @pl.when(last < i)
        def _():
            if k == 0:
                swapped(last)
            attend(last, False, (k,))

        for h in pair:
            at = slice(h * rows, (h + 1) * rows)
            whole = jnp.sum(total[:, at], axis=0, keepdims=True)
            latent_out = (acc[:, at] * (1.0 / whole)).astype(jnp.bfloat16)
            vbuf[o, k, (h % 2) * VDIM : (h % 2 + 1) * VDIM, :] = jnp.dot(
                vu[h].T, latent_out, preferred_element_type=jnp.float32
            ).astype(jnp.bfloat16)
        for way in ("up", "down", "far", "sib"):
            send(0, k, way).start()

    for k in range(2):
        for side in range(2):
            @pl.when(z_forwards(0, side, k, z))
            def _():
                z_send(i, 0, side, k).wait_send()

        @pl.when(yl == 0)
        def _():
            y_send(i, 0, 0, k).wait_send()

        @pl.when(yl == 1)
        def _():
            sib_b_send(z, 0, 0, k).wait_send()

    def drain(d, carry):
        for k in range(2):
            for side in range(2):
                src = ring(d, side)
                j = first_a + src

                @pl.when(held_a(d, side, k, src))
                def _():
                    @pl.when(z_forwards(d, side, k, src))
                    def _():
                        z_send(j, d, side, k).wait_send()

                    @pl.when(yl == 0)
                    def _():
                        y_send(j, d, side, k).wait_send()

                    @pl.when(j < i)
                    def _():
                        sib_a_send(j, d, side, k).wait_send()

                @pl.when((yl == 1) & held_b(d, side, k))
                def _():
                    sib_b_send(src, d, side, k).wait_send()

        return carry

    lax.fori_loop(1, 5, drain, 0)

    mix[...] = jnp.zeros_like(mix)

    def project(slots):
        depth = heads * VDIM
        term = mix[...]
        for slot in slots:
            start = pl.multiple_of(slot * depth, depth)
            term = term + jnp.dot(
                wo[:, pl.ds(start, depth)], vbuf[slot].reshape(depth, rows),
                preferred_element_type=jnp.float32,
            )
        mix[...] = term

    came = (
        ((1, 0, "far"), (2, 0, "up"), (4, 0, "up")),
        ((1, 1, "down", "far"), (2, 1), (4, 1, "up")),
        ((3, 0), (5, 0, "down"), (3, 1)),
        ((6, 0), (5, 1, "down")),
        ((6, 1),),
        ((7, 0),),
        ((7, 1),),
    )

    def event(t, carry):
        for n, items in enumerate(came):
            @pl.when(t == n)
            def _():
                for e, k, *ways in items:
                    v_arrived(own_slots[e], k)
                    for way in (*ways, "sib"):
                        send(e, k, way).start()

        @pl.when(t == 0)
        def _():
            locals_[8].wait()

        @pl.when(t == 7)
        def _():
            for k in range(2):
                for way in ("up", "down", "far", "sib"):
                    send(0, k, way).wait_send()
            for items in came:
                for e, k, *ways in items:
                    for way in (*ways, *(("sib",) if e < 7 else ())):
                        send(e, k, way).wait_send()

        n = jnp.where(t >= 4, t - 4, t)
        dx = jnp.where(n == 2, 3, jnp.where(n == 3, 2, n))
        place = outer_of(wrap(x + dx, NX), jnp.where(t >= 4, 1 - yh, yh), 0)
        for k in range(2):
            v_arrived(place + 1 - core, k)
        project((place + core, place + 1 - core))
        return carry

    lax.fori_loop(0, 8, event, 0)
    out_ref[...] = mix[...].astype(jnp.bfloat16)

    for k in range(2):
        send(7, k, "sib").wait_send()


def on_device(q_nope, q_rope, absorb_key, kv_latent, value_up, out_proj):
    rows = q_nope.shape[0]
    heads = absorb_key.shape[0]
    columns = out_proj.shape[1]
    kv_parts = kv_latent.T.reshape(4, WIDE // 4, rows)
    out_proj = out_proj.T
    dma = pltpu.SemaphoreType.DMA
    mixed = pl.pallas_call(
        kernel,
        out_shape=pltpu.VMEM((columns, rows), jnp.bfloat16),
        in_specs=[pl.BlockSpec(memory_space=pl.ANY)] * 6,
        out_specs=pl.BlockSpec(memory_space=pltpu.VMEM),
        scratch_shapes=[
            pltpu.VMEM(q_nope.shape, jnp.bfloat16),
            pltpu.VMEM(q_rope.shape, jnp.bfloat16),
            pltpu.VMEM(absorb_key.shape, jnp.bfloat16),
            pltpu.VMEM(value_up.shape, jnp.bfloat16),
            pltpu.VMEM(out_proj.shape, jnp.bfloat16),
            pltpu.VMEM((16, 4, WIDE // 4, rows), jnp.bfloat16),
            pltpu.VMEM((16, 2, heads * VDIM // 2, rows), jnp.bfloat16),
            pltpu.VMEM((WIDE, heads * rows), jnp.bfloat16),
            pltpu.VMEM((8, heads * rows), jnp.float32),
            pltpu.VMEM((8, heads * rows), jnp.float32),
            pltpu.VMEM((LAT, heads * rows), jnp.float32),
            pltpu.VMEM((columns, rows), jnp.float32),
            dma((9,)),
            dma((16, 4)),
            dma((2, 4, 2)),
            dma((2, 5, 2)),
            dma((2, 5, 2)),
            dma((2, 5, 2)),
            dma((16, 2)),
            dma((8, 2, 2)),
            dma((2, 2)),
            dma((8, 2)),
        ],
        compiler_params=pltpu.CompilerParams(
            collective_id=0, has_side_effects=True, vmem_limit_bytes=56 * 1024 * 1024
        ),
        cost_estimate=pl.CostEstimate(
            flops=12 * 10**9, bytes_accessed=10 * 10**6, transcendentals=4 * 10**6
        ),
    )(q_nope, q_rope, absorb_key, kv_parts, value_up, out_proj)
    return mixed.T


def solution(mesh):
    placed = (
        P("inner", "outer"),
        P("inner", "outer"),
        P("outer", None, None),
        P("inner", None),
        P("outer", None, None),
        P(None, "outer"),
    )
    return jax.shard_map(
        on_device, mesh=mesh, in_specs=placed, out_specs=P("inner", "outer"), check_vma=False
    )
```

```python
import math

import jax
import jax.numpy as jnp
from jax import lax
from jax.experimental import pallas as pl
from jax.experimental.pallas import tpu as pltpu
from jax.sharding import PartitionSpec as P

NOPE = 128
ROPE = 64
VDIM = 128
LAT = 512
WIDE = LAT + ROPE
MESH = pl.DeviceIdType.MESH
SCALE = math.log2(math.e) / math.sqrt(NOPE + ROPE)
NX, NZ = 4, 8


def div(a, b):
    return a // b if isinstance(a, int) else lax.div(a, b)


def rem(a, b):
    return a % b if isinstance(a, int) else lax.rem(a, b)


def kernel(
    qn_hbm, qr_hbm, ak_hbm, kv_hbm, vu_hbm, wo_hbm, out_ref,
    qn, qr, ak, vu, wo, kvbuf, vbuf, query, peak, total, acc, mix,
    local_sem, kv_recv, send_z, send_y, sib_a, sib_b, far_z, far_y, far_x, far_sib,
    v_recv, send_x, send_c, sib_v,
):
    heads, rows = ak.shape[0], qn.shape[0]
    o, i = lax.axis_index("outer"), lax.axis_index("inner")
    core, yh, x = rem(o, 2), rem(div(o, 2), 2), div(o, 4)
    yl, z = div(i, NZ), rem(i, NZ)

    def outer_of(x_, yh_, core_):
        return (x_ * 2 + yh_) * 2 + core_

    def wrap(n, size):
        return jnp.where(n >= size, n - size, n)

    sibling = (outer_of(x, yh, 1 - core), i)
    z_up = (o, yl * NZ + wrap(z + 1, NZ))
    z_down = (o, yl * NZ + wrap(z + NZ - 1, NZ))
    y_up = (outer_of(x, wrap(yh + yl, 2), core), (1 - yl) * NZ + z)
    y_down = (outer_of(x, wrap(yh + 1 - yl, 2), core), (1 - yl) * NZ + z)
    y_far = (outer_of(x, 1 - yh, core), i)
    x_up = (outer_of(wrap(x + 1, NX), yh, core), i)
    x_down = (outer_of(wrap(x + NX - 1, NX), yh, core), i)

    x_far = (outer_of(wrap(x + 2, NX), yh, core), i)
    z_far = (o, yl * NZ + wrap(z + 4, NZ))

    locals_ = [
        pltpu.make_async_copy(kv_hbm.at[part], kvbuf.at[i, part], local_sem.at[part])
        for part in range(4)
    ]
    for n, (src, dst) in enumerate(
        [(qn_hbm, qn), (ak_hbm, ak), (qr_hbm, qr), (vu_hbm, vu), (wo_hbm, wo)]
    ):
        locals_.append(pltpu.make_async_copy(src, dst, local_sem.at[4 + n]))
    barrier = pltpu.get_barrier_semaphore()
    partners = (sibling, z_up, z_down, z_far, y_up, y_down, y_far, x_up, x_down, x_far)
    for partner in partners:
        pl.semaphore_signal(barrier, inc=1, device_id=partner, device_id_type=MESH)
    for copy in locals_:
        copy.start()
    pl.semaphore_wait(barrier, len(partners))

    mine, others = 2 * core, 2 * (1 - core)

    def part_copy(j, part, send_sem, target):
        piece = kvbuf.at[j, part]
        return pltpu.make_async_remote_copy(
            src_ref=piece, dst_ref=piece, send_sem=send_sem,
            recv_sem=kv_recv.at[j, part], device_id=target, device_id_type=MESH,
        )

    def kv_copy(j, k, send_sem, target):
        return part_copy(j, mine + k, send_sem, target)

    def kv_arrived(j, part):
        piece = kvbuf.at[j, part]
        pltpu.make_async_remote_copy(
            src_ref=piece, dst_ref=piece, send_sem=send_z.at[0, 0, 0],
            recv_sem=kv_recv.at[j, part], device_id=sibling, device_id_type=MESH,
        ).wait_recv()

    def ring(d, side):
        return wrap(z + (d if side else NZ - d), NZ)

    def z_forwards(d, side, src):
        late = (src <= 2) if side else (z < NZ - 1)
        return (d <= 2) & ((yl == 0) | late)

    def held_a(d, side, src):
        late = (src <= 2) if side else (z >= d)
        return (d <= 3) & ((yl == 0) | late)

    first_a = yl * NZ

    def z_send(j, d, side, k):
        return kv_copy(j, k, send_z.at[side, d, k], (z_up, z_down)[side])

    o_far = outer_of(x, 1 - yh, core)

    def y_send(j, d, side, k):
        return kv_copy(j, k, send_y.at[side, d, k], (jnp.where(k == 0, o, o_far), NZ + z))

    def sib_a_send(j, d, side, k):
        return kv_copy(j, k, sib_a.at[side, d, k], sibling)

    def sib_b_send(j, d, side, k):
        return kv_copy(j, k, sib_b.at[side, d, k], sibling)

    def relay_a(d, k):
        for side in range(2):
            src = ring(d, side)

            @pl.when(held_a(d, side, src))
            def _():
                j = first_a + src
                kv_arrived(j, mine + k)

                @pl.when(z_forwards(d, side, src))
                def _():
                    z_send(j, d, side, k).start()

                @pl.when(yl == 0)
                def _():
                    y_send(j, d, side, k).start()

                @pl.when(j < i)
                def _():
                    sib_a_send(j, d, side, k).start()

    def relay_b(d, k):
        @pl.when(d == 0)
        def _():
            kv_arrived(z, mine + k)
            sib_b_send(z, 0, 0, k).start()

        @pl.when(d >= 1)
        def _():
            for side in range(2):
                j = ring(d, side)
                kv_arrived(j, mine + k)
                sib_b_send(j, d, side, k).start()

    opposite = wrap(z + 4, NZ)
    far_core = core == lax.rem(z, 2)
    far_shards = (first_a + opposite, opposite)

    def far_needed(ab):
        return far_core & ((yl == 1) if ab else (far_shards[0] < i))

    far_sent = far_core & ((yl == 0) | (z < 4))
    far_held = far_core & ((yl == 0) | (z >= 4))

    def far_z_send():
        return part_copy(i, x, far_z.at[0], z_far)

    def far_y_send():
        return part_copy(opposite, x, far_y.at[0], (jnp.where(lax.rem(x, 2) == 0, o, o_far), NZ + z))

    def far_x_sends(ab):
        return [
            part_copy(far_shards[ab], x, far_x.at[ab, n], target)
            for n, target in enumerate((x_up, x_down, x_far))
        ]

    def far_sib_send(ab, n):
        return part_copy(far_shards[ab], wrap(x + n, NX), far_sib.at[ab, n], sibling)

    def far_first(ab):
        @pl.when(((yl == 1) & far_core) if ab else far_held)
        def _():
            kv_arrived(far_shards[ab], x)

        if ab == 0:
            @pl.when((yl == 0) & far_core)
            def _():
                far_y_send().start()

        @pl.when(far_needed(ab))
        def _():
            for copy in far_x_sends(ab):
                copy.start()
            far_sib_send(ab, 0).start()

    def far_rest(ab):
        @pl.when(far_needed(ab))
        def _():
            for n in range(1, NX):
                kv_arrived(far_shards[ab], wrap(x + n, NX))
                far_sib_send(ab, n).start()

    for part in range(4):
        locals_[part].wait()

    def own(k):
        for side in range(2):
            @pl.when(z_forwards(0, side, z))
            def _():
                z_send(i, 0, side, k).start()

        @pl.when(yl == 0)
        def _():
            y_send(i, 0, 0, k).start()

    own(0)

    locals_[4].wait()
    locals_[5].wait()
    locals_[6].wait()
    qr_across = qr[...].T
    for h in range(heads):
        at = slice(h * rows, (h + 1) * rows)
        query[:LAT, at] = jnp.dot(
            qn[:, h * NOPE : (h + 1) * NOPE], ak[h], preferred_element_type=jnp.float32
        ).astype(jnp.bfloat16).T
        query[LAT:, at] = qr_across[h * ROPE : (h + 1) * ROPE]

    def attend(j, first, pairs):
        latent = kvbuf[j].reshape(WIDE, rows)
        keys = latent.T
        width = 2 * rows

        def scores(pair):
            at = slice(pair * width, (pair + 1) * width)
            s = jnp.dot(keys, query[:, at], preferred_element_type=jnp.float32) * SCALE
            if first:
                key = lax.broadcasted_iota(jnp.int32, s.shape, 0)
                row = lax.broadcasted_iota(jnp.int32, s.shape, 1)
                s = jnp.where(key <= jnp.where(row >= rows, row - rows, row), s, jnp.float32(-1e30))
            return s.reshape(rows // 8, 8, width)

        def fold(pair, s):
            at = slice(pair * width, (pair + 1) * width)
            top = jnp.max(jnp.max(s, axis=0), axis=0, keepdims=True)
            if first:
                new = jnp.broadcast_to(top, (8, width))
            else:
                old = peak[:, at]
                new = jnp.maximum(old, top)
            w = jnp.exp2(s - new[None])
            part = jnp.sum(w, axis=0)
            update = jnp.dot(
                latent[:LAT], w.reshape(rows, width).astype(jnp.bfloat16),
                preferred_element_type=jnp.float32,
            )
            peak[:, at] = new
            if first:
                total[:, at] = part
                acc[:, at] = update
            else:
                shrink = jnp.exp2(old - new)
                total[:, at] = total[:, at] * shrink + part
                grown = acc[:, at].reshape(LAT // 8, 8, width) * shrink[None]
                acc[:, at] = grown.reshape(LAT, width) + update

        s = [scores(pair) for pair in pairs]
        for pair, pair_scores in zip(pairs, s):
            fold(pair, pair_scores)

    own(1)

    @pl.when(far_sent)
    def _():
        far_z_send().start()

    attend(i, True, (0, 1))

    def swapped(j):
        for k in range(2):
            kv_arrived(j, others + k)

    def hop(d, carry):
        def half_step(k, carry):
            @pl.when(d <= 3)
            def _():
                relay_a(d, k)

            @pl.when((d == 2) & (k == 1))
            def _():
                far_first(0)

            @pl.when((d == 3) & (k == 0))
            def _():
                far_rest(0)

            def group(ab, carry):
                @pl.when((ab == 2) & (yl == 1) & (d <= 4))
                def _():
                    relay_b(d - 1, k)

                @pl.when((ab == 2) & (yl == 1) & (d == 3) & (k == 1))
                def _():
                    far_first(1)

                @pl.when((ab == 2) & (yl == 1) & (d == 4) & (k == 0))
                def _():
                    far_rest(1)

                far = (ab == 1) | (ab == 3)
                dd = jnp.where(ab >= 2, d - 2, d - 1)
                zz = wrap(jnp.where(k == 0, z + NZ - dd, z + dd), NZ)
                j = jnp.where(ab < 2, first_a, 0) + jnp.where(far, opposite, zz)
                middle = (dd >= 1) & (dd <= 3)
                in_a = (ab == 0) & middle & ((yl == 1) | (dd < 3) | (k == 0))
                in_b = (ab == 2) & (yl == 1) & ((middle & ((dd < 3) | (k == 0))) | ((dd == 0) & (k == 0)))
                in_far = ((ab == 1) & (d == 4) & (k == 0)) | ((ab == 3) & (yl == 1) & (d == 4) & (k == 1))

                @pl.when((in_a | in_b | in_far) & (j < i))
                def _():
                    @pl.when(jnp.logical_not(far))
                    def _():
                        swapped(j)

                    @pl.when(far & jnp.logical_not(far_core))
                    def _():
                        for part in range(4):
                            kv_arrived(j, part)

                    attend(j, False, (0, 1))

                return carry

            return lax.fori_loop(0, 4, group, carry)

        return lax.fori_loop(0, 2, half_step, carry)

    lax.fori_loop(1, 6, hop, 0)
    last = wrap(z + 3, NZ)

    own_slots, sib_slots = [], []
    for there in (yh, 1 - yh):
        for dx in (0, 1, 3, 2):
            place = outer_of(wrap(x + dx, NX), there, 0)
            own_slots.append(place + core)
            sib_slots.append(place + 1 - core)

    def v_arrived(slot, k):
        piece = vbuf.at[slot, k]
        pltpu.make_async_remote_copy(
            src_ref=piece, dst_ref=piece, send_sem=send_c.at[0, 0],
            recv_sem=v_recv.at[slot, k], device_id=sibling, device_id_type=MESH,
        ).wait_recv()

    locals_[7].wait()

    def send(e, k, way):
        sem = {
            "far": lambda: send_c.at[e, k], "up": lambda: send_x.at[e, k, 0],
            "down": lambda: send_x.at[e, k, 1], "sib": lambda: sib_v.at[e, k],
        }[way]()
        target = {"far": y_far, "up": x_up, "down": x_down, "sib": sibling}[way]
        piece = vbuf.at[own_slots[e], k]
        return pltpu.make_async_remote_copy(
            src_ref=piece, dst_ref=piece, send_sem=sem,
            recv_sem=v_recv.at[own_slots[e], k], device_id=target, device_id_type=MESH,
        )

    for k in range(2):
        pair = (2 * k, 2 * k + 1)

        @pl.when(last < i)
        def _():
            if k == 0:
                swapped(last)
            attend(last, False, (k,))

        for h in pair:
            at = slice(h * rows, (h + 1) * rows)
            whole = jnp.sum(total[:, at], axis=0, keepdims=True)
            latent_out = (acc[:, at] * (1.0 / whole)).astype(jnp.bfloat16)
            vbuf[o, k, (h % 2) * VDIM : (h % 2 + 1) * VDIM, :] = jnp.dot(
                vu[h].T, latent_out, preferred_element_type=jnp.float32
            ).astype(jnp.bfloat16)
        for way in ("up", "down", "far", "sib"):
            send(0, k, way).start()

    for k in range(2):
        for side in range(2):
            @pl.when(z_forwards(0, side, z))
            def _():
                z_send(i, 0, side, k).wait_send()

        @pl.when(yl == 0)
        def _():
            y_send(i, 0, 0, k).wait_send()

        @pl.when(yl == 1)
        def _():
            sib_b_send(z, 0, 0, k).wait_send()

    def drain(d, carry):
        for k in range(2):
            for side in range(2):
                src = ring(d, side)
                j = first_a + src

                @pl.when(held_a(d, side, src))
                def _():
                    @pl.when(z_forwards(d, side, src))
                    def _():
                        z_send(j, d, side, k).wait_send()

                    @pl.when(yl == 0)
                    def _():
                        y_send(j, d, side, k).wait_send()

                    @pl.when(j < i)
                    def _():
                        sib_a_send(j, d, side, k).wait_send()

                @pl.when(yl == 1)
                def _():
                    sib_b_send(src, d, side, k).wait_send()

        return carry

    lax.fori_loop(1, 4, drain, 0)

    @pl.when(far_sent)
    def _():
        far_z_send().wait_send()

    @pl.when((yl == 0) & far_core)
    def _():
        far_y_send().wait_send()

    for ab in range(2):
        @pl.when(far_needed(ab))
        def _():
            for copy in far_x_sends(ab):
                copy.wait_send()
            for n in range(NX):
                far_sib_send(ab, n).wait_send()

    mix[...] = jnp.zeros_like(mix)

    def project(slots):
        depth = heads * VDIM
        term = mix[...]
        for slot in slots:
            start = pl.multiple_of(slot * depth, depth)
            term = term + jnp.dot(
                wo[:, pl.ds(start, depth)], vbuf[slot].reshape(depth, rows),
                preferred_element_type=jnp.float32,
            )
        mix[...] = term

    came = (
        ((1, 0, "far"), (2, 0, "up"), (4, 0, "up")),
        ((1, 1, "down", "far"), (2, 1), (4, 1, "up")),
        ((3, 0), (5, 0, "down"), (3, 1)),
        ((6, 0), (5, 1, "down")),
        ((6, 1),),
        ((7, 0),),
        ((7, 1),),
    )

    def event(t, carry):
        for n, items in enumerate(came):
            @pl.when(t == n)
            def _():
                for e, k, *ways in items:
                    v_arrived(own_slots[e], k)
                    for way in (*ways, "sib"):
                        send(e, k, way).start()

        @pl.when(t == 0)
        def _():
            locals_[8].wait()

        @pl.when(t == 7)
        def _():
            for k in range(2):
                for way in ("up", "down", "far", "sib"):
                    send(0, k, way).wait_send()
            for items in came:
                for e, k, *ways in items:
                    for way in (*ways, *(("sib",) if e < 7 else ())):
                        send(e, k, way).wait_send()

        n = jnp.where(t >= 4, t - 4, t)
        dx = jnp.where(n == 2, 3, jnp.where(n == 3, 2, n))
        place = outer_of(wrap(x + dx, NX), jnp.where(t >= 4, 1 - yh, yh), 0)
        for k in range(2):
            v_arrived(place + 1 - core, k)
        project((place + core, place + 1 - core))
        return carry

    lax.fori_loop(0, 8, event, 0)
    out_ref[...] = mix[...].astype(jnp.bfloat16)

    for k in range(2):
        send(7, k, "sib").wait_send()


def on_device(q_nope, q_rope, absorb_key, kv_latent, value_up, out_proj):
    rows = q_nope.shape[0]
    heads = absorb_key.shape[0]
    columns = out_proj.shape[1]
    kv_parts = kv_latent.T.reshape(4, WIDE // 4, rows)
    out_proj = out_proj.T
    dma = pltpu.SemaphoreType.DMA
    mixed = pl.pallas_call(
        kernel,
        out_shape=pltpu.VMEM((columns, rows), jnp.bfloat16),
        in_specs=[pl.BlockSpec(memory_space=pl.ANY)] * 6,
        out_specs=pl.BlockSpec(memory_space=pltpu.VMEM),
        scratch_shapes=[
            pltpu.VMEM(q_nope.shape, jnp.bfloat16),
            pltpu.VMEM(q_rope.shape, jnp.bfloat16),
            pltpu.VMEM(absorb_key.shape, jnp.bfloat16),
            pltpu.VMEM(value_up.shape, jnp.bfloat16),
            pltpu.VMEM(out_proj.shape, jnp.bfloat16),
            pltpu.VMEM((16, 4, WIDE // 4, rows), jnp.bfloat16),
            pltpu.VMEM((16, 2, heads * VDIM // 2, rows), jnp.bfloat16),
            pltpu.VMEM((WIDE, heads * rows), jnp.bfloat16),
            pltpu.VMEM((8, heads * rows), jnp.float32),
            pltpu.VMEM((8, heads * rows), jnp.float32),
            pltpu.VMEM((LAT, heads * rows), jnp.float32),
            pltpu.VMEM((columns, rows), jnp.float32),
            dma((9,)),
            dma((16, 4)),
            dma((2, 3, 2)),
            dma((2, 4, 2)),
            dma((2, 4, 2)),
            dma((2, 4, 2)),
            dma((1,)),
            dma((1,)),
            dma((2, 3)),
            dma((2, 4)),
            dma((16, 2)),
            dma((8, 2, 2)),
            dma((2, 2)),
            dma((8, 2)),
        ],
        compiler_params=pltpu.CompilerParams(
            collective_id=0, has_side_effects=True, vmem_limit_bytes=56 * 1024 * 1024
        ),
        cost_estimate=pl.CostEstimate(
            flops=12 * 10**9, bytes_accessed=10 * 10**6, transcendentals=4 * 10**6
        ),
    )(q_nope, q_rope, absorb_key, kv_parts, value_up, out_proj)
    return mixed.T


def solution(mesh):
    placed = (
        P("inner", "outer"),
        P("inner", "outer"),
        P("outer", None, None),
        P("inner", None),
        P("outer", None, None),
        P(None, "outer"),
    )
    return jax.shard_map(
        on_device, mesh=mesh, in_specs=placed, out_specs=P("inner", "outer"), check_vma=False
    )
```

```python
import math

import jax
import jax.numpy as jnp
from jax import lax
from jax.experimental import pallas as pl
from jax.experimental.pallas import tpu as pltpu
from jax.sharding import PartitionSpec as P

NOPE = 128
ROPE = 64
VDIM = 128
LAT = 512
WIDE = LAT + ROPE
MESH = pl.DeviceIdType.MESH
SCALE = math.log2(math.e) / math.sqrt(NOPE + ROPE)
NX, NZ = 4, 8


def div(a, b):
    return a // b if isinstance(a, int) else lax.div(a, b)


def rem(a, b):
    return a % b if isinstance(a, int) else lax.rem(a, b)


def kernel(
    qn_hbm, qr_hbm, ak_hbm, kv_hbm, vu_hbm, wo_hbm, out_ref,
    qn, qr, ak, vu, wo, kvbuf, vbuf, query, peak, total, acc, mix,
    local_sem, kv_recv, send_z, send_y, sib_a, sib_b, v_recv, send_x, send_c, sib_v,
):
    heads, rows = ak.shape[0], qn.shape[0]
    o, i = lax.axis_index("outer"), lax.axis_index("inner")
    core, yh, x = rem(o, 2), rem(div(o, 2), 2), div(o, 4)
    yl, z = div(i, NZ), rem(i, NZ)

    def outer_of(x_, yh_, core_):
        return (x_ * 2 + yh_) * 2 + core_

    def wrap(n, size):
        return jnp.where(n >= size, n - size, n)

    sibling = (outer_of(x, yh, 1 - core), i)
    z_up = (o, yl * NZ + wrap(z + 1, NZ))
    z_down = (o, yl * NZ + wrap(z + NZ - 1, NZ))
    y_up = (outer_of(x, wrap(yh + yl, 2), core), (1 - yl) * NZ + z)
    y_down = (outer_of(x, wrap(yh + 1 - yl, 2), core), (1 - yl) * NZ + z)
    y_far = (outer_of(x, 1 - yh, core), i)
    x_up = (outer_of(wrap(x + 1, NX), yh, core), i)
    x_down = (outer_of(wrap(x + NX - 1, NX), yh, core), i)

    locals_ = [
        pltpu.make_async_copy(kv_hbm.at[part], kvbuf.at[i, part], local_sem.at[part])
        for part in range(4)
    ]
    for n, (src, dst) in enumerate(
        [(qn_hbm, qn), (ak_hbm, ak), (qr_hbm, qr), (vu_hbm, vu), (wo_hbm, wo)]
    ):
        locals_.append(pltpu.make_async_copy(src, dst, local_sem.at[4 + n]))
    barrier = pltpu.get_barrier_semaphore()
    partners = (sibling, z_up, z_down, y_up, y_down, y_far, x_up, x_down)
    for partner in partners:
        pl.semaphore_signal(barrier, inc=1, device_id=partner, device_id_type=MESH)
    for copy in locals_:
        copy.start()
    pl.semaphore_wait(barrier, len(partners))

    mine, others = 2 * core, 2 * (1 - core)

    def kv_copy(j, k, send_sem, target):
        piece = kvbuf.at[j, mine + k]
        return pltpu.make_async_remote_copy(
            src_ref=piece, dst_ref=piece, send_sem=send_sem,
            recv_sem=kv_recv.at[j, mine + k], device_id=target, device_id_type=MESH,
        )

    def kv_arrived(j, part):
        piece = kvbuf.at[j, part]
        pltpu.make_async_remote_copy(
            src_ref=piece, dst_ref=piece, send_sem=send_z.at[0, 0, 0],
            recv_sem=kv_recv.at[j, part], device_id=sibling, device_id_type=MESH,
        ).wait_recv()

    def ring(d, side):
        return wrap(z + (d if side else NZ - d), NZ)

    def z_forwards(d, side, k, src):
        late = (
            (src <= 2) & ((d <= 2) | ((d == 3) & (src == 0) & (k == 1)))
            if side
            else (z < NZ - 1) & ((d <= 2) | ((d == 3) & ((src > 0) | (k == 0))))
        )
        return ((yl == 0) & ((d <= 2) | ((d == 3) & (k == side)))) | ((yl == 1) & late)

    def held_a(d, side, k, src):
        late = (
            (src <= 2) & ((d <= 3) | ((d == 4) & (src == 0) & (k == 1)))
            if side
            else (z >= d) & ((d <= 3) | ((d == 4) & ((src > 0) | (k == 0))))
        )
        return ((yl == 0) & held_b(d, side, k)) | ((yl == 1) & late)

    def held_b(d, side, k):
        return (d <= 3) | ((d == 4) & (k == side))

    first_a = yl * NZ

    def z_send(j, d, side, k):
        return kv_copy(j, k, send_z.at[side, d, k], (z_up, z_down)[side])

    o_far = outer_of(x, 1 - yh, core)

    def y_send(j, d, side, k):
        return kv_copy(j, k, send_y.at[side, d, k], (jnp.where(k == 0, o, o_far), NZ + z))

    def sib_a_send(j, d, side, k):
        return kv_copy(j, k, sib_a.at[side, d, k], sibling)

    def sib_b_send(j, d, side, k):
        return kv_copy(j, k, sib_b.at[side, d, k], sibling)

    def relay_a(d, k):
        for side in range(2):
            src = ring(d, side)

            @pl.when(held_a(d, side, k, src))
            def _():
                j = first_a + src
                kv_arrived(j, mine + k)

                @pl.when(z_forwards(d, side, k, src))
                def _():
                    z_send(j, d, side, k).start()

                @pl.when(yl == 0)
                def _():
                    y_send(j, d, side, k).start()

                @pl.when(j < i)
                def _():
                    sib_a_send(j, d, side, k).start()

    def relay_b(d, k):
        @pl.when(d == 0)
        def _():
            kv_arrived(z, mine + k)
            sib_b_send(z, 0, 0, k).start()

        for side in range(2):
            @pl.when((d >= 1) & held_b(d, side, k))
            def _():
                j = ring(d, side)
                kv_arrived(j, mine + k)
                sib_b_send(j, d, side, k).start()

    for part in range(4):
        locals_[part].wait()

    def own(k):
        for side in range(2):
            @pl.when(z_forwards(0, side, k, z))
            def _():
                z_send(i, 0, side, k).start()

        @pl.when(yl == 0)
        def _():
            y_send(i, 0, 0, k).start()

    own(0)

    locals_[4].wait()
    locals_[5].wait()
    locals_[6].wait()
    qr_across = qr[...].T
    for h in range(heads):
        at = slice(h * rows, (h + 1) * rows)
        query[:LAT, at] = jnp.dot(
            qn[:, h * NOPE : (h + 1) * NOPE], ak[h], preferred_element_type=jnp.float32
        ).astype(jnp.bfloat16).T
        query[LAT:, at] = qr_across[h * ROPE : (h + 1) * ROPE]

    def attend(j, first, pairs):
        latent = kvbuf[j].reshape(WIDE, rows)
        keys = latent.T
        width = 2 * rows

        def scores(pair):
            at = slice(pair * width, (pair + 1) * width)
            s = jnp.dot(keys, query[:, at], preferred_element_type=jnp.float32) * SCALE
            if first:
                key = lax.broadcasted_iota(jnp.int32, s.shape, 0)
                row = lax.broadcasted_iota(jnp.int32, s.shape, 1)
                s = jnp.where(key <= jnp.where(row >= rows, row - rows, row), s, jnp.float32(-1e30))
            return s.reshape(rows // 8, 8, width)

        def fold(pair, s):
            at = slice(pair * width, (pair + 1) * width)
            top = jnp.max(jnp.max(s, axis=0), axis=0, keepdims=True)
            if first:
                new = jnp.broadcast_to(top, (8, width))
            else:
                old = peak[:, at]
                new = jnp.maximum(old, top)
            w = jnp.exp2(s - new[None])
            part = jnp.sum(w, axis=0)
            update = jnp.dot(
                latent[:LAT], w.reshape(rows, width).astype(jnp.bfloat16),
                preferred_element_type=jnp.float32,
            )
            peak[:, at] = new
            if first:
                total[:, at] = part
                acc[:, at] = update
            else:
                shrink = jnp.exp2(old - new)
                total[:, at] = total[:, at] * shrink + part
                grown = acc[:, at].reshape(LAT // 8, 8, width) * shrink[None]
                acc[:, at] = grown.reshape(LAT, width) + update

        s = [scores(pair) for pair in pairs]
        for pair, pair_scores in zip(pairs, s):
            fold(pair, pair_scores)

    own(1)
    attend(i, True, (0, 1))

    def swapped(j):
        for k in range(2):
            kv_arrived(j, others + k)

    def hop(d, carry):
        def half_step(k, carry):
            @pl.when(d <= 4)
            def _():
                relay_a(d, k)

            def group(ab, carry):
                @pl.when((ab == 1) & (yl == 1))
                def _():
                    relay_b(d - 1, k)

                dd = d - 2 - ab
                j = jnp.where(ab == 0, first_a, 0) + wrap(jnp.where(k == 0, z + NZ - dd, z + dd), NZ)
                in_a = (ab == 0) & (((dd >= 1) & (dd <= 3)) | ((dd == 4) & (k == 0) & (yl == 1)))
                in_b = (ab == 1) & (yl == 1) & (((dd >= 1) & (dd <= 3)) | ((dd == 0) & (k == 0)))

                @pl.when((in_a | in_b) & (j < i))
                def _():
                    swapped(j)
                    attend(j, False, (0, 1))

                return carry

            return lax.fori_loop(0, 2, group, carry)

        return lax.fori_loop(0, 2, half_step, carry)

    lax.fori_loop(1, 7, hop, 0)
    last = wrap(z + 4, NZ)

    own_slots, sib_slots = [], []
    for there in (yh, 1 - yh):
        for dx in (0, 1, 3, 2):
            place = outer_of(wrap(x + dx, NX), there, 0)
            own_slots.append(place + core)
            sib_slots.append(place + 1 - core)

    def v_arrived(slot, k):
        piece = vbuf.at[slot, k]
        pltpu.make_async_remote_copy(
            src_ref=piece, dst_ref=piece, send_sem=send_c.at[0, 0],
            recv_sem=v_recv.at[slot, k], device_id=sibling, device_id_type=MESH,
        ).wait_recv()

    locals_[7].wait()

    def send(e, k, way):
        sem = {
            "far": lambda: send_c.at[e, k], "up": lambda: send_x.at[e, k, 0],
            "down": lambda: send_x.at[e, k, 1], "sib": lambda: sib_v.at[e, k],
        }[way]()
        target = {"far": y_far, "up": x_up, "down": x_down, "sib": sibling}[way]
        piece = vbuf.at[own_slots[e], k]
        return pltpu.make_async_remote_copy(
            src_ref=piece, dst_ref=piece, send_sem=sem,
            recv_sem=v_recv.at[own_slots[e], k], device_id=target, device_id_type=MESH,
        )

    for k in range(2):
        pair = (2 * k, 2 * k + 1)

        @pl.when(last < i)
        def _():
            if k == 0:
                swapped(last)
            attend(last, False, (k,))

        for h in pair:
            at = slice(h * rows, (h + 1) * rows)
            whole = jnp.sum(total[:, at], axis=0, keepdims=True)
            latent_out = (acc[:, at] * (1.0 / whole)).astype(jnp.bfloat16)
            vbuf[o, k, (h % 2) * VDIM : (h % 2 + 1) * VDIM, :] = jnp.dot(
                vu[h].T, latent_out, preferred_element_type=jnp.float32
            ).astype(jnp.bfloat16)
        for way in ("up", "down", "far", "sib"):
            send(0, k, way).start()

    for k in range(2):
        for side in range(2):
            @pl.when(z_forwards(0, side, k, z))
            def _():
                z_send(i, 0, side, k).wait_send()

        @pl.when(yl == 0)
        def _():
            y_send(i, 0, 0, k).wait_send()

        @pl.when(yl == 1)
        def _():
            sib_b_send(z, 0, 0, k).wait_send()

    def drain(d, carry):
        for k in range(2):
            for side in range(2):
                src = ring(d, side)
                j = first_a + src

                @pl.when(held_a(d, side, k, src))
                def _():
                    @pl.when(z_forwards(d, side, k, src))
                    def _():
                        z_send(j, d, side, k).wait_send()

                    @pl.when(yl == 0)
                    def _():
                        y_send(j, d, side, k).wait_send()

                    @pl.when(j < i)
                    def _():
                        sib_a_send(j, d, side, k).wait_send()

                @pl.when((yl == 1) & held_b(d, side, k))
                def _():
                    sib_b_send(src, d, side, k).wait_send()

        return carry

    lax.fori_loop(1, 5, drain, 0)

    mix[...] = jnp.zeros_like(mix)

    def project(slots):
        depth = heads * VDIM
        term = mix[...]
        for slot in slots:
            start = pl.multiple_of(slot * depth, depth)
            term = term + jnp.dot(
                wo[:, pl.ds(start, depth)], vbuf[slot].reshape(depth, rows),
                preferred_element_type=jnp.float32,
            )
        mix[...] = term

    came = (
        ((1, 0, "far"), (2, 0, "up"), (4, 0, "up")),
        ((1, 1, "down", "far"), (2, 1), (4, 1, "up")),
        ((3, 0), (5, 0, "down"), (3, 1)),
        ((6, 0), (5, 1, "down")),
        ((6, 1),),
        ((7, 0),),
        ((7, 1),),
    )

    def event(t, carry):
        for n, items in enumerate(came):
            @pl.when(t == n)
            def _():
                for e, k, *ways in items:
                    v_arrived(own_slots[e], k)
                    for way in (*ways, "sib"):
                        send(e, k, way).start()

        @pl.when(t == 0)
        def _():
            locals_[8].wait()

        @pl.when(t == 7)
        def _():
            for k in range(2):
                for way in ("up", "down", "far", "sib"):
                    send(0, k, way).wait_send()
            for items in came:
                for e, k, *ways in items:
                    for way in (*ways, *(("sib",) if e < 7 else ())):
                        send(e, k, way).wait_send()

        n = jnp.where(t >= 4, t - 4, t)
        dx = jnp.where(n == 2, 3, jnp.where(n == 3, 2, n))
        place = outer_of(wrap(x + dx, NX), jnp.where(t >= 4, 1 - yh, yh), 0)
        for k in range(2):
            v_arrived(place + 1 - core, k)
        project((place + core, place + 1 - core))
        return carry

    lax.fori_loop(0, 8, event, 0)
    out_ref[...] = mix[...].astype(jnp.bfloat16)

    for k in range(2):
        send(7, k, "sib").wait_send()


def on_device(q_nope, q_rope, absorb_key, kv_latent, value_up, out_proj):
    rows = q_nope.shape[0]
    heads = absorb_key.shape[0]
    columns = out_proj.shape[1]
    kv_parts = kv_latent.T.reshape(4, WIDE // 4, rows)
    out_proj = out_proj.T
    dma = pltpu.SemaphoreType.DMA
    mixed = pl.pallas_call(
        kernel,
        out_shape=pltpu.VMEM((columns, rows), jnp.bfloat16),
        in_specs=[pl.BlockSpec(memory_space=pl.ANY)] * 6,
        out_specs=pl.BlockSpec(memory_space=pltpu.VMEM),
        scratch_shapes=[
            pltpu.VMEM(q_nope.shape, jnp.bfloat16),
            pltpu.VMEM(q_rope.shape, jnp.bfloat16),
            pltpu.VMEM(absorb_key.shape, jnp.bfloat16),
            pltpu.VMEM(value_up.shape, jnp.bfloat16),
            pltpu.VMEM(out_proj.shape, jnp.bfloat16),
            pltpu.VMEM((16, 4, WIDE // 4, rows), jnp.bfloat16),
            pltpu.VMEM((16, 2, heads * VDIM // 2, rows), jnp.bfloat16),
            pltpu.VMEM((WIDE, heads * rows), jnp.bfloat16),
            pltpu.VMEM((8, heads * rows), jnp.float32),
            pltpu.VMEM((8, heads * rows), jnp.float32),
            pltpu.VMEM((LAT, heads * rows), jnp.float32),
            pltpu.VMEM((columns, rows), jnp.float32),
            dma((9,)),
            dma((16, 4)),
            dma((2, 4, 2)),
            dma((2, 5, 2)),
            dma((2, 5, 2)),
            dma((2, 5, 2)),
            dma((16, 2)),
            dma((8, 2, 2)),
            dma((2, 2)),
            dma((8, 2)),
        ],
        compiler_params=pltpu.CompilerParams(
            collective_id=0, has_side_effects=True, vmem_limit_bytes=56 * 1024 * 1024
        ),
        cost_estimate=pl.CostEstimate(
            flops=12 * 10**9, bytes_accessed=10 * 10**6, transcendentals=4 * 10**6
        ),
    )(q_nope, q_rope, absorb_key, kv_parts, value_up, out_proj)
    return mixed.T


def solution(mesh):
    placed = (
        P("inner", "outer"),
        P("inner", "outer"),
        P("outer", None, None),
        P("inner", None),
        P("outer", None, None),
        P(None, "outer"),
    )
    return jax.shard_map(
        on_device, mesh=mesh, in_specs=placed, out_specs=P("inner", "outer"), check_vma=False
    )
```

```python
import math

import jax
import jax.numpy as jnp
from jax import lax
from jax.experimental import pallas as pl
from jax.experimental.pallas import tpu as pltpu
from jax.sharding import PartitionSpec as P

NOPE = 128
ROPE = 64
VDIM = 128
LAT = 512
WIDE = LAT + ROPE
MESH = pl.DeviceIdType.MESH
SCALE = math.log2(math.e) / math.sqrt(NOPE + ROPE)
NX, NZ = 4, 8


def div(a, b):
    return a // b if isinstance(a, int) else lax.div(a, b)


def rem(a, b):
    return a % b if isinstance(a, int) else lax.rem(a, b)


def kernel(
    qn_hbm, qr_hbm, ak_hbm, kv_hbm, vu_hbm, wo_hbm, out_ref,
    qn, qr, ak, vu, vu_across, wo, kvbuf, vbuf, query, peak, total, acc, mix,
    local_sem, kv_recv, send_z, send_y, sib_a, sib_b, v_recv, send_x, send_c, sib_v,
):
    heads, rows = ak.shape[0], qn.shape[0]
    o, i = lax.axis_index("outer"), lax.axis_index("inner")
    core, yh, x = rem(o, 2), rem(div(o, 2), 2), div(o, 4)
    yl, z = div(i, NZ), rem(i, NZ)

    def outer_of(x_, yh_, core_):
        return (x_ * 2 + yh_) * 2 + core_

    def wrap(n, size):
        return jnp.where(n >= size, n - size, n)

    sibling = (outer_of(x, yh, 1 - core), i)
    z_up = (o, yl * NZ + wrap(z + 1, NZ))
    z_down = (o, yl * NZ + wrap(z + NZ - 1, NZ))
    y_up = (outer_of(x, wrap(yh + yl, 2), core), (1 - yl) * NZ + z)
    y_down = (outer_of(x, wrap(yh + 1 - yl, 2), core), (1 - yl) * NZ + z)
    y_far = (outer_of(x, 1 - yh, core), i)
    x_up = (outer_of(wrap(x + 1, NX), yh, core), i)
    x_down = (outer_of(wrap(x + NX - 1, NX), yh, core), i)

    locals_ = [
        pltpu.make_async_copy(kv_hbm.at[part], kvbuf.at[i, part], local_sem.at[part])
        for part in range(4)
    ]
    for n, (src, dst) in enumerate(
        [(qn_hbm, qn), (ak_hbm, ak), (qr_hbm, qr), (vu_hbm, vu), (wo_hbm, wo)]
    ):
        locals_.append(pltpu.make_async_copy(src, dst, local_sem.at[4 + n]))
    barrier = pltpu.get_barrier_semaphore()
    partners = (sibling, z_up, z_down, y_up, y_down, y_far, x_up, x_down)
    for partner in partners:
        pl.semaphore_signal(barrier, inc=1, device_id=partner, device_id_type=MESH)
    for copy in locals_:
        copy.start()
    pl.semaphore_wait(barrier, len(partners))

    mine, others = 2 * core, 2 * (1 - core)

    def kv_copy(j, k, send_sem, target):
        piece = kvbuf.at[j, mine + k]
        return pltpu.make_async_remote_copy(
            src_ref=piece, dst_ref=piece, send_sem=send_sem,
            recv_sem=kv_recv.at[j, mine + k], device_id=target, device_id_type=MESH,
        )

    def kv_arrived(j, part):
        piece = kvbuf.at[j, part]
        pltpu.make_async_remote_copy(
            src_ref=piece, dst_ref=piece, send_sem=send_z.at[0, 0, 0],
            recv_sem=kv_recv.at[j, part], device_id=sibling, device_id_type=MESH,
        ).wait_recv()

    def ring(d, side):
        return wrap(z + (d if side else NZ - d), NZ)

    def z_forwards(d, side, k, src):
        late = (
            (src <= 2) & ((d <= 2) | ((d == 3) & (src == 0) & (k == 1)))
            if side
            else (z < NZ - 1) & ((d <= 2) | ((d == 3) & ((src > 0) | (k == 0))))
        )
        return ((yl == 0) & ((d <= 2) | ((d == 3) & (k == side)))) | ((yl == 1) & late)

    def held_a(d, side, k, src):
        late = (
            (src <= 2) & ((d <= 3) | ((d == 4) & (src == 0) & (k == 1)))
            if side
            else (z >= d) & ((d <= 3) | ((d == 4) & ((src > 0) | (k == 0))))
        )
        return ((yl == 0) & held_b(d, side, k)) | ((yl == 1) & late)

    def held_b(d, side, k):
        return (d <= 3) | ((d == 4) & (k == side))

    first_a = yl * NZ

    def z_send(j, d, side, k):
        return kv_copy(j, k, send_z.at[side, d, k], (z_up, z_down)[side])

    o_far = outer_of(x, 1 - yh, core)

    def y_send(j, d, side, k):
        return kv_copy(j, k, send_y.at[side, d, k], (jnp.where(k == 0, o, o_far), NZ + z))

    def sib_a_send(j, d, side, k):
        return kv_copy(j, k, sib_a.at[side, d, k], sibling)

    def sib_b_send(j, d, side, k):
        return kv_copy(j, k, sib_b.at[side, d, k], sibling)

    def relay_a(d, k):
        for side in range(2):
            src = ring(d, side)

            @pl.when(held_a(d, side, k, src))
            def _():
                j = first_a + src
                kv_arrived(j, mine + k)

                @pl.when(z_forwards(d, side, k, src))
                def _():
                    z_send(j, d, side, k).start()

                @pl.when(yl == 0)
                def _():
                    y_send(j, d, side, k).start()

                @pl.when(j < i)
                def _():
                    sib_a_send(j, d, side, k).start()

    def relay_b(d, k):
        @pl.when(d == 0)
        def _():
            kv_arrived(z, mine + k)
            sib_b_send(z, 0, 0, k).start()

        for side in range(2):
            @pl.when((d >= 1) & held_b(d, side, k))
            def _():
                j = ring(d, side)
                kv_arrived(j, mine + k)
                sib_b_send(j, d, side, k).start()

    for part in range(4):
        locals_[part].wait()

    def own(k):
        for side in range(2):
            @pl.when(z_forwards(0, side, k, z))
            def _():
                z_send(i, 0, side, k).start()

        @pl.when(yl == 0)
        def _():
            y_send(i, 0, 0, k).start()

    own(0)

    locals_[4].wait()
    locals_[5].wait()
    locals_[6].wait()
    qr_across = qr[...].T
    for h in range(heads):
        at = slice(h * rows, (h + 1) * rows)
        query[:LAT, at] = jnp.dot(
            qn[:, h * NOPE : (h + 1) * NOPE], ak[h], preferred_element_type=jnp.float32
        ).astype(jnp.bfloat16).T
        query[LAT:, at] = qr_across[h * ROPE : (h + 1) * ROPE]

    def attend(j, first, pairs):
        latent = kvbuf[j].reshape(WIDE, rows)
        keys = latent.T
        width = 2 * rows

        def scores(pair):
            at = slice(pair * width, (pair + 1) * width)
            s = jnp.dot(keys, query[:, at], preferred_element_type=jnp.float32) * SCALE
            if first:
                key = lax.broadcasted_iota(jnp.int32, s.shape, 0)
                row = lax.broadcasted_iota(jnp.int32, s.shape, 1)
                s = jnp.where(key <= jnp.where(row >= rows, row - rows, row), s, jnp.float32(-1e30))
            return s.reshape(rows // 8, 8, width)

        def fold(pair, s):
            at = slice(pair * width, (pair + 1) * width)
            top = jnp.max(jnp.max(s, axis=0), axis=0, keepdims=True)
            if first:
                new = jnp.broadcast_to(top, (8, width))
            else:
                old = peak[:, at]
                new = jnp.maximum(old, top)
            w = jnp.exp2(s - new[None])
            part = jnp.sum(w, axis=0)
            update = jnp.dot(
                latent[:LAT], w.reshape(rows, width).astype(jnp.bfloat16),
                preferred_element_type=jnp.float32,
            )
            peak[:, at] = new
            if first:
                total[:, at] = part
                acc[:, at] = update
            else:
                shrink = jnp.exp2(old - new)
                total[:, at] = total[:, at] * shrink + part
                grown = acc[:, at].reshape(LAT // 8, 8, width) * shrink[None]
                acc[:, at] = grown.reshape(LAT, width) + update

        s = [scores(pair) for pair in pairs]
        for pair, pair_scores in zip(pairs, s):
            fold(pair, pair_scores)

    own(1)
    attend(i, True, (0, 1))
    locals_[7].wait()
    for h in range(heads):
        vu_across[h] = vu[h].T

    def swapped(j):
        for k in range(2):
            kv_arrived(j, others + k)

    def hop(d, carry):
        def half_step(k, carry):
            @pl.when(d <= 4)
            def _():
                relay_a(d, k)

            def group(ab, carry):
                @pl.when((ab == 1) & (yl == 1))
                def _():
                    relay_b(d - 1, k)

                dd = d - 1 - ab
                j = jnp.where(ab == 0, first_a, 0) + wrap(jnp.where(k == 0, z + NZ - dd, z + dd), NZ)
                in_a = (ab == 0) & (((dd >= 1) & (dd <= 3)) | ((dd == 4) & (k == 0) & (yl == 1)))
                in_b = (ab == 1) & (yl == 1) & (((dd >= 1) & (dd <= 3)) | ((dd == 0) & (k == 0)))

                @pl.when((in_a | in_b) & (j < i))
                def _():
                    swapped(j)
                    attend(j, False, (0, 1))

                return carry

            return lax.fori_loop(0, 2, group, carry)

        return lax.fori_loop(0, 2, half_step, carry)

    lax.fori_loop(1, 6, hop, 0)
    last = wrap(z + 4, NZ)

    own_slots, sib_slots = [], []
    for there in (yh, 1 - yh):
        for dx in (0, 1, 3, 2):
            place = outer_of(wrap(x + dx, NX), there, 0)
            own_slots.append(place + core)
            sib_slots.append(place + 1 - core)

    def v_arrived(slot, k):
        piece = vbuf.at[slot, k]
        pltpu.make_async_remote_copy(
            src_ref=piece, dst_ref=piece, send_sem=send_c.at[0, 0],
            recv_sem=v_recv.at[slot, k], device_id=sibling, device_id_type=MESH,
        ).wait_recv()


    def send(e, k, way):
        sem = {
            "far": lambda: send_c.at[e, k], "up": lambda: send_x.at[e, k, 0],
            "down": lambda: send_x.at[e, k, 1], "sib": lambda: sib_v.at[e, k],
        }[way]()
        target = {"far": y_far, "up": x_up, "down": x_down, "sib": sibling}[way]
        piece = vbuf.at[own_slots[e], k]
        return pltpu.make_async_remote_copy(
            src_ref=piece, dst_ref=piece, send_sem=sem,
            recv_sem=v_recv.at[own_slots[e], k], device_id=target, device_id_type=MESH,
        )

    for k in range(2):
        pair = (2 * k, 2 * k + 1)

        @pl.when(last < i)
        def _():
            if k == 0:
                swapped(last)
            attend(last, False, (k,))

        for h in pair:
            at = slice(h * rows, (h + 1) * rows)
            whole = jnp.sum(total[:, at], axis=0, keepdims=True)
            latent_out = (acc[:, at] * (1.0 / whole)).astype(jnp.bfloat16)
            vbuf[o, k, (h % 2) * VDIM : (h % 2 + 1) * VDIM, :] = jnp.dot(
                vu_across[h], latent_out, preferred_element_type=jnp.float32
            ).astype(jnp.bfloat16)
        for way in ("up", "down", "far", "sib"):
            send(0, k, way).start()

    for k in range(2):
        for side in range(2):
            @pl.when(z_forwards(0, side, k, z))
            def _():
                z_send(i, 0, side, k).wait_send()

        @pl.when(yl == 0)
        def _():
            y_send(i, 0, 0, k).wait_send()

        @pl.when(yl == 1)
        def _():
            sib_b_send(z, 0, 0, k).wait_send()

    def drain(d, carry):
        for k in range(2):
            for side in range(2):
                src = ring(d, side)
                j = first_a + src

                @pl.when(held_a(d, side, k, src))
                def _():
                    @pl.when(z_forwards(d, side, k, src))
                    def _():
                        z_send(j, d, side, k).wait_send()

                    @pl.when(yl == 0)
                    def _():
                        y_send(j, d, side, k).wait_send()

                    @pl.when(j < i)
                    def _():
                        sib_a_send(j, d, side, k).wait_send()

                @pl.when((yl == 1) & held_b(d, side, k))
                def _():
                    sib_b_send(src, d, side, k).wait_send()

        return carry

    lax.fori_loop(1, 5, drain, 0)

    mix[...] = jnp.zeros_like(mix)

    def project(slot):
        depth = heads * VDIM
        start = pl.multiple_of(slot * depth, depth)
        mix[...] += jnp.dot(
            wo[:, pl.ds(start, depth)], vbuf[slot].reshape(depth, rows),
            preferred_element_type=jnp.float32,
        )

    came = (
        ((1, 0, "far"), (2, 0, "up"), (4, 0, "up")),
        ((1, 1, "down", "far"), (2, 1), (4, 1, "up")),
        ((3, 0), (5, 0, "down"), (3, 1)),
        ((6, 0), (5, 1, "down")),
        ((6, 1),),
        ((7, 0),),
        ((7, 1),),
    )

    def event(t, carry):
        for n, items in enumerate(came):
            @pl.when(t == n)
            def _():
                for e, k, *ways in items:
                    v_arrived(own_slots[e], k)
                    for way in (*ways, "sib"):
                        send(e, k, way).start()

        @pl.when(t == 0)
        def _():
            locals_[8].wait()

        @pl.when(t == 7)
        def _():
            for k in range(2):
                for way in ("up", "down", "far", "sib"):
                    send(0, k, way).wait_send()
            for items in came:
                for e, k, *ways in items:
                    for way in (*ways, *(("sib",) if e < 7 else ())):
                        send(e, k, way).wait_send()

        n = jnp.where(t >= 4, t - 4, t)
        dx = jnp.where(n == 2, 3, jnp.where(n == 3, 2, n))
        place = outer_of(wrap(x + dx, NX), jnp.where(t >= 4, 1 - yh, yh), 0)

        def half(n, carry):
            @pl.when(n == 1)
            def _():
                for k in range(2):
                    v_arrived(place + 1 - core, k)

            project(place + jnp.where(n == 0, core, 1 - core))
            return carry

        return lax.fori_loop(0, 2, half, carry)

    lax.fori_loop(0, 8, event, 0)
    out_ref[...] = mix[...].astype(jnp.bfloat16)

    for k in range(2):
        send(7, k, "sib").wait_send()


def on_device(q_nope, q_rope, absorb_key, kv_latent, value_up, out_proj):
    rows = q_nope.shape[0]
    heads = absorb_key.shape[0]
    columns = out_proj.shape[1]
    kv_parts = kv_latent.T.reshape(4, WIDE // 4, rows)
    out_proj = out_proj.T
    dma = pltpu.SemaphoreType.DMA
    mixed = pl.pallas_call(
        kernel,
        out_shape=pltpu.VMEM((columns, rows), jnp.bfloat16),
        in_specs=[pl.BlockSpec(memory_space=pl.ANY)] * 6,
        out_specs=pl.BlockSpec(memory_space=pltpu.VMEM),
        scratch_shapes=[
            pltpu.VMEM(q_nope.shape, jnp.bfloat16),
            pltpu.VMEM(q_rope.shape, jnp.bfloat16),
            pltpu.VMEM(absorb_key.shape, jnp.bfloat16),
            pltpu.VMEM(value_up.shape, jnp.bfloat16),
            pltpu.VMEM((heads, VDIM, LAT), jnp.bfloat16),
            pltpu.VMEM(out_proj.shape, jnp.bfloat16),
            pltpu.VMEM((16, 4, WIDE // 4, rows), jnp.bfloat16),
            pltpu.VMEM((16, 2, heads * VDIM // 2, rows), jnp.bfloat16),
            pltpu.VMEM((WIDE, heads * rows), jnp.bfloat16),
            pltpu.VMEM((8, heads * rows), jnp.float32),
            pltpu.VMEM((8, heads * rows), jnp.float32),
            pltpu.VMEM((LAT, heads * rows), jnp.float32),
            pltpu.VMEM((columns, rows), jnp.float32),
            dma((9,)),
            dma((16, 4)),
            dma((2, 4, 2)),
            dma((2, 5, 2)),
            dma((2, 5, 2)),
            dma((2, 5, 2)),
            dma((16, 2)),
            dma((8, 2, 2)),
            dma((2, 2)),
            dma((8, 2)),
        ],
        compiler_params=pltpu.CompilerParams(
            collective_id=0, has_side_effects=True, vmem_limit_bytes=56 * 1024 * 1024
        ),
        cost_estimate=pl.CostEstimate(
            flops=12 * 10**9, bytes_accessed=10 * 10**6, transcendentals=4 * 10**6
        ),
    )(q_nope, q_rope, absorb_key, kv_parts, value_up, out_proj)
    return mixed.T


def solution(mesh):
    placed = (
        P("inner", "outer"),
        P("inner", "outer"),
        P("outer", None, None),
        P("inner", None),
        P("outer", None, None),
        P(None, "outer"),
    )
    return jax.shard_map(
        on_device, mesh=mesh, in_specs=placed, out_specs=P("inner", "outer"), check_vma=False
    )
```

```python
import math

import jax
import jax.numpy as jnp
from jax import lax
from jax.experimental import pallas as pl
from jax.experimental.pallas import tpu as pltpu
from jax.sharding import PartitionSpec as P

NOPE = 128
ROPE = 64
VDIM = 128
LAT = 512
WIDE = LAT + ROPE
MESH = pl.DeviceIdType.MESH
SCALE = math.log2(math.e) / math.sqrt(NOPE + ROPE)
NX, NZ = 4, 8


def div(a, b):
    return a // b if isinstance(a, int) else lax.div(a, b)


def rem(a, b):
    return a % b if isinstance(a, int) else lax.rem(a, b)


def kernel(
    qn_hbm, qr_hbm, ak_hbm, kv_hbm, vu_hbm, wo_hbm, out_ref,
    qn, qr, ak, vu, vu_across, wo, kvbuf, vbuf, query, peak, total, acc, mix,
    local_sem, kv_recv, send_z, send_y, sib_a, sib_b, v_recv, send_x, send_c, sib_v,
):
    heads, rows = ak.shape[0], qn.shape[0]
    o, i = lax.axis_index("outer"), lax.axis_index("inner")
    core, yh, x = rem(o, 2), rem(div(o, 2), 2), div(o, 4)
    yl, z = div(i, NZ), rem(i, NZ)

    def outer_of(x_, yh_, core_):
        return (x_ * 2 + yh_) * 2 + core_

    def wrap(n, size):
        return jnp.where(n >= size, n - size, n)

    sibling = (outer_of(x, yh, 1 - core), i)
    z_up = (o, yl * NZ + wrap(z + 1, NZ))
    z_down = (o, yl * NZ + wrap(z + NZ - 1, NZ))
    y_up = (outer_of(x, wrap(yh + yl, 2), core), (1 - yl) * NZ + z)
    y_down = (outer_of(x, wrap(yh + 1 - yl, 2), core), (1 - yl) * NZ + z)
    y_far = (outer_of(x, 1 - yh, core), i)
    x_plus, x_minus = wrap(x + 1, NX), wrap(x + NX - 1, NX)
    x_up = (outer_of(jnp.where(core == 0, x_plus, x_minus), yh, core), i)
    x_down = (outer_of(jnp.where(core == 0, x_minus, x_plus), yh, core), i)

    locals_ = [
        pltpu.make_async_copy(kv_hbm.at[part], kvbuf.at[i, part], local_sem.at[part])
        for part in range(4)
    ]
    for n, (src, dst) in enumerate(
        [(qn_hbm, qn), (ak_hbm, ak), (qr_hbm, qr), (vu_hbm, vu), (wo_hbm, wo)]
    ):
        locals_.append(pltpu.make_async_copy(src, dst, local_sem.at[4 + n]))
    barrier = pltpu.get_barrier_semaphore()
    partners = (sibling, z_up, z_down, y_up, y_down, y_far, x_up, x_down)
    for partner in partners:
        pl.semaphore_signal(barrier, inc=1, device_id=partner, device_id_type=MESH)
    for copy in locals_:
        copy.start()
    pl.semaphore_wait(barrier, len(partners))

    mine, others = 2 * core, 2 * (1 - core)

    def kv_copy(j, k, send_sem, target):
        piece = kvbuf.at[j, mine + k]
        return pltpu.make_async_remote_copy(
            src_ref=piece, dst_ref=piece, send_sem=send_sem,
            recv_sem=kv_recv.at[j, mine + k], device_id=target, device_id_type=MESH,
        )

    def kv_arrived(j, part):
        piece = kvbuf.at[j, part]
        pltpu.make_async_remote_copy(
            src_ref=piece, dst_ref=piece, send_sem=send_z.at[0, 0, 0],
            recv_sem=kv_recv.at[j, part], device_id=sibling, device_id_type=MESH,
        ).wait_recv()

    def ring(d, side):
        return wrap(z + (d if side else NZ - d), NZ)

    def z_forwards(d, side, k, src):
        late = (
            (src <= 2) & ((d <= 2) | ((d == 3) & (src == 0) & (k == 1)))
            if side
            else (z < NZ - 1) & ((d <= 2) | ((d == 3) & ((src > 0) | (k == 0))))
        )
        return ((yl == 0) & ((d <= 2) | ((d == 3) & (k == side)))) | ((yl == 1) & late)

    def held_a(d, side, k, src):
        late = (
            (src <= 2) & ((d <= 3) | ((d == 4) & (src == 0) & (k == 1)))
            if side
            else (z >= d) & ((d <= 3) | ((d == 4) & ((src > 0) | (k == 0))))
        )
        return ((yl == 0) & held_b(d, side, k)) | ((yl == 1) & late)

    def held_b(d, side, k):
        return (d <= 3) | ((d == 4) & (k == side))

    first_a = yl * NZ

    def z_send(j, d, side, k):
        return kv_copy(j, k, send_z.at[side, d, k], (z_up, z_down)[side])

    o_far = outer_of(x, 1 - yh, core)

    def y_send(j, d, side, k):
        return kv_copy(j, k, send_y.at[side, d, k], (jnp.where(k == 0, o, o_far), NZ + z))

    def sib_a_send(j, d, side, k):
        return kv_copy(j, k, sib_a.at[side, d, k], sibling)

    def sib_b_send(j, d, side, k):
        return kv_copy(j, k, sib_b.at[side, d, k], sibling)

    def relay_a(d, k):
        for side in range(2):
            src = ring(d, side)

            @pl.when(held_a(d, side, k, src))
            def _():
                j = first_a + src
                kv_arrived(j, mine + k)

                @pl.when(z_forwards(d, side, k, src))
                def _():
                    z_send(j, d, side, k).start()

                @pl.when(yl == 0)
                def _():
                    y_send(j, d, side, k).start()

                @pl.when(j < i)
                def _():
                    sib_a_send(j, d, side, k).start()

    def relay_b(d, k):
        @pl.when(d == 0)
        def _():
            kv_arrived(z, mine + k)
            sib_b_send(z, 0, 0, k).start()

        for side in range(2):
            @pl.when((d >= 1) & held_b(d, side, k))
            def _():
                j = ring(d, side)
                kv_arrived(j, mine + k)
                sib_b_send(j, d, side, k).start()

    for part in range(4):
        locals_[part].wait()

    def own(k):
        for side in range(2):
            @pl.when(z_forwards(0, side, k, z))
            def _():
                z_send(i, 0, side, k).start()

        @pl.when(yl == 0)
        def _():
            y_send(i, 0, 0, k).start()

    own(0)

    locals_[4].wait()
    locals_[5].wait()
    locals_[6].wait()
    qr_across = qr[...].T
    for h in range(heads):
        at = slice(h * rows, (h + 1) * rows)
        query[:LAT, at] = jnp.dot(
            qn[:, h * NOPE : (h + 1) * NOPE], ak[h], preferred_element_type=jnp.float32
        ).astype(jnp.bfloat16).T
        query[LAT:, at] = qr_across[h * ROPE : (h + 1) * ROPE]

    def attend(j, first, pairs):
        latent = kvbuf[j].reshape(WIDE, rows)
        keys = latent.T
        width = 2 * rows

        def scores(pair):
            at = slice(pair * width, (pair + 1) * width)
            s = jnp.dot(keys, query[:, at], preferred_element_type=jnp.float32) * SCALE
            if first:
                key = lax.broadcasted_iota(jnp.int32, s.shape, 0)
                row = lax.broadcasted_iota(jnp.int32, s.shape, 1)
                s = jnp.where(key <= jnp.where(row >= rows, row - rows, row), s, jnp.float32(-1e30))
            return s.reshape(rows // 8, 8, width)

        def fold(pair, s):
            at = slice(pair * width, (pair + 1) * width)
            top = jnp.max(jnp.max(s, axis=0), axis=0, keepdims=True)
            if first:
                new = jnp.broadcast_to(top, (8, width))
            else:
                old = peak[:, at]
                new = jnp.maximum(old, top)
            w = jnp.exp2(s - new[None])
            part = jnp.sum(w, axis=0)
            update = jnp.dot(
                latent[:LAT], w.reshape(rows, width).astype(jnp.bfloat16),
                preferred_element_type=jnp.float32,
            )
            peak[:, at] = new
            if first:
                total[:, at] = part
                acc[:, at] = update
            else:
                shrink = jnp.exp2(old - new)
                total[:, at] = total[:, at] * shrink + part
                grown = acc[:, at].reshape(LAT // 8, 8, width) * shrink[None]
                acc[:, at] = grown.reshape(LAT, width) + update

        s = [scores(pair) for pair in pairs]
        for pair, pair_scores in zip(pairs, s):
            fold(pair, pair_scores)

    own(1)
    attend(i, True, (0, 1))
    locals_[7].wait()
    for h in range(heads):
        vu_across[h] = vu[h].T

    def swapped(j):
        for k in range(2):
            kv_arrived(j, others + k)

    def hop(d, carry):
        def half_step(k, carry):
            @pl.when(d <= 4)
            def _():
                relay_a(d, k)

            def group(ab, carry):
                @pl.when((ab == 1) & (yl == 1))
                def _():
                    relay_b(d - 1, k)

                dd = d - 1 - ab
                j = jnp.where(ab == 0, first_a, 0) + wrap(jnp.where(k == 0, z + NZ - dd, z + dd), NZ)
                in_a = (ab == 0) & (((dd >= 1) & (dd <= 3)) | ((dd == 4) & (k == 0) & (yl == 1)))
                in_b = (ab == 1) & (yl == 1) & (((dd >= 1) & (dd <= 3)) | ((dd == 0) & (k == 0)))

                @pl.when((in_a | in_b) & (j < i))
                def _():
                    swapped(j)
                    attend(j, False, (0, 1))

                return carry

            return lax.fori_loop(0, 2, group, carry)

        return lax.fori_loop(0, 2, half_step, carry)

    lax.fori_loop(1, 6, hop, 0)
    last = wrap(z + 4, NZ)

    def slot_of(dx, there, core_):
        return outer_of(wrap(jnp.where(core_ == 0, x + dx, x + NX - dx), NX), there, core_)

    own_slots = [slot_of(dx, there, core) for there in (yh, 1 - yh) for dx in (0, 1, 3, 2)]

    def v_arrived(slot, k):
        piece = vbuf.at[slot, k]
        pltpu.make_async_remote_copy(
            src_ref=piece, dst_ref=piece, send_sem=send_c.at[0, 0],
            recv_sem=v_recv.at[slot, k], device_id=sibling, device_id_type=MESH,
        ).wait_recv()


    def send(e, k, way):
        sem = {
            "far": lambda: send_c.at[e, k], "up": lambda: send_x.at[e, k, 0],
            "down": lambda: send_x.at[e, k, 1], "sib": lambda: sib_v.at[e, k],
        }[way]()
        target = {"far": y_far, "up": x_up, "down": x_down, "sib": sibling}[way]
        piece = vbuf.at[own_slots[e], k]
        return pltpu.make_async_remote_copy(
            src_ref=piece, dst_ref=piece, send_sem=sem,
            recv_sem=v_recv.at[own_slots[e], k], device_id=target, device_id_type=MESH,
        )

    for k in range(2):
        pair = (2 * k, 2 * k + 1)

        @pl.when(last < i)
        def _():
            if k == 0:
                swapped(last)
            attend(last, False, (k,))

        for h in pair:
            at = slice(h * rows, (h + 1) * rows)
            whole = jnp.sum(total[:, at], axis=0, keepdims=True)
            latent_out = (acc[:, at] * (1.0 / whole)).astype(jnp.bfloat16)
            vbuf[o, k, (h % 2) * VDIM : (h % 2 + 1) * VDIM, :] = jnp.dot(
                vu_across[h], latent_out, preferred_element_type=jnp.float32
            ).astype(jnp.bfloat16)
        for way in ("up", "down", "far", "sib"):
            send(0, k, way).start()

    for k in range(2):
        for side in range(2):
            @pl.when(z_forwards(0, side, k, z))
            def _():
                z_send(i, 0, side, k).wait_send()

        @pl.when(yl == 0)
        def _():
            y_send(i, 0, 0, k).wait_send()

        @pl.when(yl == 1)
        def _():
            sib_b_send(z, 0, 0, k).wait_send()

    def drain(d, carry):
        for k in range(2):
            for side in range(2):
                src = ring(d, side)
                j = first_a + src

                @pl.when(held_a(d, side, k, src))
                def _():
                    @pl.when(z_forwards(d, side, k, src))
                    def _():
                        z_send(j, d, side, k).wait_send()

                    @pl.when(yl == 0)
                    def _():
                        y_send(j, d, side, k).wait_send()

                    @pl.when(j < i)
                    def _():
                        sib_a_send(j, d, side, k).wait_send()

                @pl.when((yl == 1) & held_b(d, side, k))
                def _():
                    sib_b_send(src, d, side, k).wait_send()

        return carry

    lax.fori_loop(1, 5, drain, 0)

    mix[...] = jnp.zeros_like(mix)

    def project(slot):
        depth = heads * VDIM
        start = pl.multiple_of(slot * depth, depth)
        mix[...] += jnp.dot(
            wo[:, pl.ds(start, depth)], vbuf[slot].reshape(depth, rows),
            preferred_element_type=jnp.float32,
        )

    came = (
        ((1, 0, "far"), (2, 0, "up"), (4, 0, "up")),
        ((1, 1, "down", "far"), (2, 1), (4, 1, "up")),
        ((3, 0), (5, 0, "down"), (3, 1)),
        ((6, 0), (5, 1, "down")),
        ((6, 1),),
        ((7, 0),),
        ((7, 1),),
    )

    def event(t, carry):
        for n, items in enumerate(came):
            @pl.when(t == n)
            def _():
                for e, k, *ways in items:
                    v_arrived(own_slots[e], k)
                    for way in (*ways, "sib"):
                        send(e, k, way).start()

        @pl.when(t == 0)
        def _():
            locals_[8].wait()

        @pl.when(t == 7)
        def _():
            for k in range(2):
                for way in ("up", "down", "far", "sib"):
                    send(0, k, way).wait_send()
            for items in came:
                for e, k, *ways in items:
                    for way in (*ways, *(("sib",) if e < 7 else ())):
                        send(e, k, way).wait_send()

        n = jnp.where(t >= 4, t - 4, t)
        dx = jnp.where(n == 2, 3, jnp.where(n == 3, 2, n))
        there = jnp.where(t >= 4, 1 - yh, yh)
        own_slot, sib_slot = slot_of(dx, there, core), slot_of(dx, there, 1 - core)

        def half(n, carry):
            @pl.when(n == 1)
            def _():
                for k in range(2):
                    v_arrived(sib_slot, k)

            project(jnp.where(n == 0, own_slot, sib_slot))
            return carry

        return lax.fori_loop(0, 2, half, carry)

    lax.fori_loop(0, 8, event, 0)
    out_ref[...] = mix[...].astype(jnp.bfloat16)

    for k in range(2):
        send(7, k, "sib").wait_send()


def on_device(q_nope, q_rope, absorb_key, kv_latent, value_up, out_proj):
    rows = q_nope.shape[0]
    heads = absorb_key.shape[0]
    columns = out_proj.shape[1]
    kv_parts = kv_latent.T.reshape(4, WIDE // 4, rows)
    out_proj = out_proj.T
    dma = pltpu.SemaphoreType.DMA
    mixed = pl.pallas_call(
        kernel,
        out_shape=pltpu.VMEM((columns, rows), jnp.bfloat16),
        in_specs=[pl.BlockSpec(memory_space=pl.ANY)] * 6,
        out_specs=pl.BlockSpec(memory_space=pltpu.VMEM),
        scratch_shapes=[
            pltpu.VMEM(q_nope.shape, jnp.bfloat16),
            pltpu.VMEM(q_rope.shape, jnp.bfloat16),
            pltpu.VMEM(absorb_key.shape, jnp.bfloat16),
            pltpu.VMEM(value_up.shape, jnp.bfloat16),
            pltpu.VMEM((heads, VDIM, LAT), jnp.bfloat16),
            pltpu.VMEM(out_proj.shape, jnp.bfloat16),
            pltpu.VMEM((16, 4, WIDE // 4, rows), jnp.bfloat16),
            pltpu.VMEM((16, 2, heads * VDIM // 2, rows), jnp.bfloat16),
            pltpu.VMEM((WIDE, heads * rows), jnp.bfloat16),
            pltpu.VMEM((8, heads * rows), jnp.float32),
            pltpu.VMEM((8, heads * rows), jnp.float32),
            pltpu.VMEM((LAT, heads * rows), jnp.float32),
            pltpu.VMEM((columns, rows), jnp.float32),
            dma((9,)),
            dma((16, 4)),
            dma((2, 4, 2)),
            dma((2, 5, 2)),
            dma((2, 5, 2)),
            dma((2, 5, 2)),
            dma((16, 2)),
            dma((8, 2, 2)),
            dma((2, 2)),
            dma((8, 2)),
        ],
        compiler_params=pltpu.CompilerParams(
            collective_id=0, has_side_effects=True, vmem_limit_bytes=56 * 1024 * 1024
        ),
        cost_estimate=pl.CostEstimate(
            flops=12 * 10**9, bytes_accessed=10 * 10**6, transcendentals=4 * 10**6
        ),
    )(q_nope, q_rope, absorb_key, kv_parts, value_up, out_proj)
    return mixed.T


def solution(mesh):
    placed = (
        P("inner", "outer"),
        P("inner", "outer"),
        P("outer", None, None),
        P("inner", None),
        P("outer", None, None),
        P(None, "outer"),
    )
    return jax.shard_map(
        on_device, mesh=mesh, in_specs=placed, out_specs=P("inner", "outer"), check_vma=False
    )
```

```python
import math

import jax
import jax.numpy as jnp
from jax import lax
from jax.experimental import pallas as pl
from jax.experimental.pallas import tpu as pltpu
from jax.sharding import PartitionSpec as P

NOPE = 128
ROPE = 64
VDIM = 128
LAT = 512
WIDE = LAT + ROPE
MESH = pl.DeviceIdType.MESH
SCALE = math.log2(math.e) / math.sqrt(NOPE + ROPE)
NX, NZ = 4, 8


def div(a, b):
    return a // b if isinstance(a, int) else lax.div(a, b)


def rem(a, b):
    return a % b if isinstance(a, int) else lax.rem(a, b)


def kernel(
    qn_hbm, qr_hbm, ak_hbm, kv_hbm, vu_hbm, wo_hbm, out_ref,
    qn, qr, ak, vu, vu_across, wo, kvbuf, vbuf, query, peak, total, acc, mix,
    local_sem, kv_recv, send_z, send_y, sib_a, sib_b, v_recv, send_x, send_c, sib_v,
):
    heads, rows = ak.shape[0], qn.shape[0]
    o, i = lax.axis_index("outer"), lax.axis_index("inner")
    core, yh, x = rem(o, 2), rem(div(o, 2), 2), div(o, 4)
    yl, z = div(i, NZ), rem(i, NZ)

    def outer_of(x_, yh_, core_):
        return (x_ * 2 + yh_) * 2 + core_

    def wrap(n, size):
        return jnp.where(n >= size, n - size, n)

    sibling = (outer_of(x, yh, 1 - core), i)
    z_up = (o, yl * NZ + wrap(z + 1, NZ))
    z_down = (o, yl * NZ + wrap(z + NZ - 1, NZ))
    y_up = (outer_of(x, wrap(yh + yl, 2), core), (1 - yl) * NZ + z)
    y_down = (outer_of(x, wrap(yh + 1 - yl, 2), core), (1 - yl) * NZ + z)
    y_far = (outer_of(x, 1 - yh, core), i)
    x_plus, x_minus = wrap(x + 1, NX), wrap(x + NX - 1, NX)
    x_up = (outer_of(jnp.where(core == 0, x_plus, x_minus), yh, core), i)
    x_down = (outer_of(jnp.where(core == 0, x_minus, x_plus), yh, core), i)

    locals_ = [
        pltpu.make_async_copy(kv_hbm.at[part], kvbuf.at[i, part], local_sem.at[part])
        for part in range(4)
    ]
    for n, (src, dst) in enumerate(
        [(qn_hbm, qn), (ak_hbm, ak), (qr_hbm, qr), (vu_hbm, vu), (wo_hbm, wo)]
    ):
        locals_.append(pltpu.make_async_copy(src, dst, local_sem.at[4 + n]))
    barrier = pltpu.get_barrier_semaphore()
    partners = (sibling, z_up, z_down, y_up, y_down, y_far, x_up, x_down)
    for partner in partners:
        pl.semaphore_signal(barrier, inc=1, device_id=partner, device_id_type=MESH)
    for copy in locals_:
        copy.start()
    pl.semaphore_wait(barrier, len(partners))

    mine, others = 2 * core, 2 * (1 - core)

    def kv_copy(j, k, send_sem, target):
        piece = kvbuf.at[j, mine + k]
        return pltpu.make_async_remote_copy(
            src_ref=piece, dst_ref=piece, send_sem=send_sem,
            recv_sem=kv_recv.at[j, mine + k], device_id=target, device_id_type=MESH,
        )

    def kv_arrived(j, part):
        piece = kvbuf.at[j, part]
        pltpu.make_async_remote_copy(
            src_ref=piece, dst_ref=piece, send_sem=send_z.at[0, 0, 0],
            recv_sem=kv_recv.at[j, part], device_id=sibling, device_id_type=MESH,
        ).wait_recv()

    def ring(d, side):
        return wrap(z + (d if side else NZ - d), NZ)

    def z_forwards(d, side, k, src):
        late = (
            (src <= 2) & ((d <= 2) | ((d == 3) & (src == 0) & (k == 1)))
            if side
            else (z < NZ - 1) & ((d <= 2) | ((d == 3) & ((src > 0) | (k == 0))))
        )
        return ((yl == 0) & ((d <= 2) | ((d == 3) & (k == side)))) | ((yl == 1) & late)

    def held_a(d, side, k, src):
        late = (
            (src <= 2) & ((d <= 3) | ((d == 4) & (src == 0) & (k == 1)))
            if side
            else (z >= d) & ((d <= 3) | ((d == 4) & ((src > 0) | (k == 0))))
        )
        return ((yl == 0) & held_b(d, side, k)) | ((yl == 1) & late)

    def held_b(d, side, k):
        return (d <= 3) | ((d == 4) & (k == side))

    first_a = yl * NZ

    def z_send(j, d, side, k):
        return kv_copy(j, k, send_z.at[side, d, k], (z_up, z_down)[side])

    o_far = outer_of(x, 1 - yh, core)

    def y_send(j, d, side, k):
        return kv_copy(j, k, send_y.at[side, d, k], (jnp.where(k == core, o, o_far), NZ + z))

    def sib_a_send(j, d, side, k):
        return kv_copy(j, k, sib_a.at[side, d, k], sibling)

    def sib_b_send(j, d, side, k):
        return kv_copy(j, k, sib_b.at[side, d, k], sibling)

    def relay_a(d, k):
        for side in range(2):
            src = ring(d, side)

            @pl.when(held_a(d, side, k, src))
            def _():
                j = first_a + src
                kv_arrived(j, mine + k)

                @pl.when(z_forwards(d, side, k, src))
                def _():
                    z_send(j, d, side, k).start()

                @pl.when(yl == 0)
                def _():
                    y_send(j, d, side, k).start()

                @pl.when(j < i)
                def _():
                    sib_a_send(j, d, side, k).start()

    def relay_b(d, k):
        @pl.when(d == 0)
        def _():
            kv_arrived(z, mine + k)
            sib_b_send(z, 0, 0, k).start()

        for side in range(2):
            @pl.when((d >= 1) & held_b(d, side, k))
            def _():
                j = ring(d, side)
                kv_arrived(j, mine + k)
                sib_b_send(j, d, side, k).start()

    for part in range(4):
        locals_[part].wait()

    def own(k):
        for side in range(2):
            @pl.when(z_forwards(0, side, k, z))
            def _():
                z_send(i, 0, side, k).start()

        @pl.when(yl == 0)
        def _():
            y_send(i, 0, 0, k).start()

    own(0)

    locals_[4].wait()
    locals_[5].wait()
    locals_[6].wait()
    qr_across = qr[...].T
    for h in range(heads):
        at = slice(h * rows, (h + 1) * rows)
        query[:LAT, at] = jnp.dot(
            qn[:, h * NOPE : (h + 1) * NOPE], ak[h], preferred_element_type=jnp.float32
        ).astype(jnp.bfloat16).T
        query[LAT:, at] = qr_across[h * ROPE : (h + 1) * ROPE]

    def attend(j, first, pairs):
        latent = kvbuf[j].reshape(WIDE, rows)
        keys = latent.T
        width = 2 * rows

        def scores(pair):
            at = slice(pair * width, (pair + 1) * width)
            s = jnp.dot(keys, query[:, at], preferred_element_type=jnp.float32) * SCALE
            if first:
                key = lax.broadcasted_iota(jnp.int32, s.shape, 0)
                row = lax.broadcasted_iota(jnp.int32, s.shape, 1)
                s = jnp.where(key <= jnp.where(row >= rows, row - rows, row), s, jnp.float32(-1e30))
            return s.reshape(rows // 8, 8, width)

        def fold(pair, s):
            at = slice(pair * width, (pair + 1) * width)
            top = jnp.max(jnp.max(s, axis=0), axis=0, keepdims=True)
            if first:
                new = jnp.broadcast_to(top, (8, width))
            else:
                old = peak[:, at]
                new = jnp.maximum(old, top)
            w = jnp.exp2(s - new[None])
            part = jnp.sum(w, axis=0)
            update = jnp.dot(
                latent[:LAT], w.reshape(rows, width).astype(jnp.bfloat16),
                preferred_element_type=jnp.float32,
            )
            peak[:, at] = new
            if first:
                total[:, at] = part
                acc[:, at] = update
            else:
                shrink = jnp.exp2(old - new)
                total[:, at] = total[:, at] * shrink + part
                grown = acc[:, at].reshape(LAT // 8, 8, width) * shrink[None]
                acc[:, at] = grown.reshape(LAT, width) + update

        s = [scores(pair) for pair in pairs]
        for pair, pair_scores in zip(pairs, s):
            fold(pair, pair_scores)

    own(1)
    attend(i, True, (0, 1))
    locals_[7].wait()
    for h in range(heads):
        vu_across[h] = vu[h].T

    def swapped(j):
        for k in range(2):
            kv_arrived(j, others + k)

    def hop(d, carry):
        def half_step(k, carry):
            @pl.when(d <= 4)
            def _():
                relay_a(d, k)

            def group(ab, carry):
                @pl.when((ab == 1) & (yl == 1))
                def _():
                    relay_b(d - 1, k)

                dd = d - 1 - ab
                j = jnp.where(ab == 0, first_a, 0) + wrap(jnp.where(k == 0, z + NZ - dd, z + dd), NZ)
                in_a = (ab == 0) & (((dd >= 1) & (dd <= 3)) | ((dd == 4) & (k == 0) & (yl == 1)))
                in_b = (ab == 1) & (yl == 1) & (((dd >= 1) & (dd <= 3)) | ((dd == 0) & (k == 0)))

                @pl.when((in_a | in_b) & (j < i))
                def _():
                    swapped(j)
                    attend(j, False, (0, 1))

                return carry

            return lax.fori_loop(0, 2, group, carry)

        return lax.fori_loop(0, 2, half_step, carry)

    lax.fori_loop(1, 6, hop, 0)
    last = wrap(z + 4, NZ)

    def slot_of(dx, there, core_):
        return outer_of(wrap(jnp.where(core_ == 0, x + dx, x + NX - dx), NX), there, core_)

    own_slots = [slot_of(dx, there, core) for there in (yh, 1 - yh) for dx in (0, 1, 3, 2)]

    def v_arrived(slot, k):
        piece = vbuf.at[slot, k]
        pltpu.make_async_remote_copy(
            src_ref=piece, dst_ref=piece, send_sem=send_c.at[0, 0],
            recv_sem=v_recv.at[slot, k], device_id=sibling, device_id_type=MESH,
        ).wait_recv()


    def send(e, k, way):
        sem = {
            "far": lambda: send_c.at[e, k], "up": lambda: send_x.at[e, k, 0],
            "down": lambda: send_x.at[e, k, 1], "sib": lambda: sib_v.at[e, k],
        }[way]()
        target = {"far": y_far, "up": x_up, "down": x_down, "sib": sibling}[way]
        piece = vbuf.at[own_slots[e], k]
        return pltpu.make_async_remote_copy(
            src_ref=piece, dst_ref=piece, send_sem=sem,
            recv_sem=v_recv.at[own_slots[e], k], device_id=target, device_id_type=MESH,
        )

    for k in range(2):
        pair = (2 * k, 2 * k + 1)

        @pl.when(last < i)
        def _():
            if k == 0:
                swapped(last)
            attend(last, False, (k,))

        for h in pair:
            at = slice(h * rows, (h + 1) * rows)
            whole = jnp.sum(total[:, at], axis=0, keepdims=True)
            latent_out = (acc[:, at] * (1.0 / whole)).astype(jnp.bfloat16)
            vbuf[o, k, (h % 2) * VDIM : (h % 2 + 1) * VDIM, :] = jnp.dot(
                vu_across[h], latent_out, preferred_element_type=jnp.float32
            ).astype(jnp.bfloat16)
        for way in ("up", "down", "far", "sib"):
            send(0, k, way).start()

    for k in range(2):
        for side in range(2):
            @pl.when(z_forwards(0, side, k, z))
            def _():
                z_send(i, 0, side, k).wait_send()

        @pl.when(yl == 0)
        def _():
            y_send(i, 0, 0, k).wait_send()

        @pl.when(yl == 1)
        def _():
            sib_b_send(z, 0, 0, k).wait_send()

    def drain(d, carry):
        for k in range(2):
            for side in range(2):
                src = ring(d, side)
                j = first_a + src

                @pl.when(held_a(d, side, k, src))
                def _():
                    @pl.when(z_forwards(d, side, k, src))
                    def _():
                        z_send(j, d, side, k).wait_send()

                    @pl.when(yl == 0)
                    def _():
                        y_send(j, d, side, k).wait_send()

                    @pl.when(j < i)
                    def _():
                        sib_a_send(j, d, side, k).wait_send()

                @pl.when((yl == 1) & held_b(d, side, k))
                def _():
                    sib_b_send(src, d, side, k).wait_send()

        return carry

    lax.fori_loop(1, 5, drain, 0)

    mix[...] = jnp.zeros_like(mix)

    def project(slot):
        depth = heads * VDIM
        start = pl.multiple_of(slot * depth, depth)
        mix[...] += jnp.dot(
            wo[:, pl.ds(start, depth)], vbuf[slot].reshape(depth, rows),
            preferred_element_type=jnp.float32,
        )

    came = (
        ((1, 0, "far"), (2, 0, "up"), (4, 0, "up")),
        ((1, 1, "down", "far"), (2, 1), (4, 1, "up")),
        ((3, 0), (5, 0, "down"), (3, 1)),
        ((6, 0), (5, 1, "down")),
        ((6, 1),),
        ((7, 0),),
        ((7, 1),),
    )

    def event(t, carry):
        for n, items in enumerate(came):
            @pl.when(t == n)
            def _():
                for e, k, *ways in items:
                    v_arrived(own_slots[e], k)
                    for way in (*ways, "sib"):
                        send(e, k, way).start()

        @pl.when(t == 0)
        def _():
            locals_[8].wait()

        @pl.when(t == 7)
        def _():
            for k in range(2):
                for way in ("up", "down", "far", "sib"):
                    send(0, k, way).wait_send()
            for items in came:
                for e, k, *ways in items:
                    for way in (*ways, *(("sib",) if e < 7 else ())):
                        send(e, k, way).wait_send()

        n = jnp.where(t >= 4, t - 4, t)
        dx = jnp.where(n == 2, 3, jnp.where(n == 3, 2, n))
        there = jnp.where(t >= 4, 1 - yh, yh)
        own_slot, sib_slot = slot_of(dx, there, core), slot_of(dx, there, 1 - core)

        def half(n, carry):
            @pl.when(n == 1)
            def _():
                for k in range(2):
                    v_arrived(sib_slot, k)

            project(jnp.where(n == 0, own_slot, sib_slot))
            return carry

        return lax.fori_loop(0, 2, half, carry)

    lax.fori_loop(0, 8, event, 0)
    out_ref[...] = mix[...].astype(jnp.bfloat16)

    for k in range(2):
        send(7, k, "sib").wait_send()


def on_device(q_nope, q_rope, absorb_key, kv_latent, value_up, out_proj):
    rows = q_nope.shape[0]
    heads = absorb_key.shape[0]
    columns = out_proj.shape[1]
    kv_parts = kv_latent.T.reshape(4, WIDE // 4, rows)
    out_proj = out_proj.T
    dma = pltpu.SemaphoreType.DMA
    mixed = pl.pallas_call(
        kernel,
        out_shape=pltpu.VMEM((columns, rows), jnp.bfloat16),
        in_specs=[pl.BlockSpec(memory_space=pl.ANY)] * 6,
        out_specs=pl.BlockSpec(memory_space=pltpu.VMEM),
        scratch_shapes=[
            pltpu.VMEM(q_nope.shape, jnp.bfloat16),
            pltpu.VMEM(q_rope.shape, jnp.bfloat16),
            pltpu.VMEM(absorb_key.shape, jnp.bfloat16),
            pltpu.VMEM(value_up.shape, jnp.bfloat16),
            pltpu.VMEM((heads, VDIM, LAT), jnp.bfloat16),
            pltpu.VMEM(out_proj.shape, jnp.bfloat16),
            pltpu.VMEM((16, 4, WIDE // 4, rows), jnp.bfloat16),
            pltpu.VMEM((16, 2, heads * VDIM // 2, rows), jnp.bfloat16),
            pltpu.VMEM((WIDE, heads * rows), jnp.bfloat16),
            pltpu.VMEM((8, heads * rows), jnp.float32),
            pltpu.VMEM((8, heads * rows), jnp.float32),
            pltpu.VMEM((LAT, heads * rows), jnp.float32),
            pltpu.VMEM((columns, rows), jnp.float32),
            dma((9,)),
            dma((16, 4)),
            dma((2, 4, 2)),
            dma((2, 5, 2)),
            dma((2, 5, 2)),
            dma((2, 5, 2)),
            dma((16, 2)),
            dma((8, 2, 2)),
            dma((2, 2)),
            dma((8, 2)),
        ],
        compiler_params=pltpu.CompilerParams(
            collective_id=0, has_side_effects=True, vmem_limit_bytes=56 * 1024 * 1024
        ),
        cost_estimate=pl.CostEstimate(
            flops=12 * 10**9, bytes_accessed=10 * 10**6, transcendentals=4 * 10**6
        ),
    )(q_nope, q_rope, absorb_key, kv_parts, value_up, out_proj)
    return mixed.T


def solution(mesh):
    placed = (
        P("inner", "outer"),
        P("inner", "outer"),
        P("outer", None, None),
        P("inner", None),
        P("outer", None, None),
        P(None, "outer"),
    )
    return jax.shard_map(
        on_device, mesh=mesh, in_specs=placed, out_specs=P("inner", "outer"), check_vma=False
    )
```
